32 devices in a mesh: ctx: 8 (over y, x, core), fsdp: 4 (over z).
Axes of the slice: x: 2, y: 2, z: 4, core: 2. Of those that a mesh axis runs over, the one named last changes fastest.
Arguments:
- inputs: bfloat16 [4, 1024, 2304], P('fsdp', 'ctx'), may hold values from -6 to 6
- cotangent: bfloat16 [4, 1024, 2304], P('fsdp', 'ctx'), may hold values from -6 to 6
- weights_in: float32 [2304, 16, 256], P('ctx', 'fsdp'), may hold values from -0.20833333 to 0.20833333
- weights_out: float32 [2304, 8, 256], P('ctx', 'fsdp'), may hold values from -0.125 to 0.125
- ffn_weights: float32 [2304, 3, 9216], P('ctx', None, 'fsdp'), may hold values from -0.125 to 0.125
- norm_gains: float32 [4, 2304], replicated, may hold values from -0.5 to 0.5
- momentum_in: float32 [2304, 16, 256], P('ctx', 'fsdp'), may hold values from -256 to 256
- momentum_out: float32 [2304, 8, 256], P('ctx', 'fsdp'), may hold values from -256 to 256
- ffn_momentum: float32 [2304, 3, 9216], P('ctx', None, 'fsdp'), may hold values from -192 to 192
- gain_first: float32 [4, 2304], replicated, may hold values from -32 to 32
- gain_second: float32 [4, 2304], replicated, may hold values from 204.8 to 819.2
- stretch_order: int32 [16], replicated, may hold values from 0 to 15, each once
Outputs:
- outputs: bfloat16 [4, 1024, 2304], P('fsdp', 'ctx')
- input_grad: float32 [4, 1024, 2304], P('fsdp', 'ctx')
- new_weights_in: float32 [2304, 16, 256], P('ctx', 'fsdp')
- new_weights_out: float32 [2304, 8, 256], P('ctx', 'fsdp')
- new_ffn_weights: float32 [2304, 3, 9216], P('ctx', None, 'fsdp')
- new_momentum_in: float32 [2304, 16, 256], P('ctx', 'fsdp')
- new_momentum_out: float32 [2304, 8, 256], P('ctx', 'fsdp')
- new_ffn_momentum: float32 [2304, 3, 9216], P('ctx', None, 'fsdp')
- new_norm_gains: float32 [4, 2304], replicated
- new_gain_first: float32 [4, 2304], replicated
- new_gain_second: float32 [4, 2304], replicated
The draws below stay inside these ranges and needn't reach their ends.
Inputs may be any that keep to these rules, and one draw needn't show every extreme that they name: stretch_order is a permutation: every stretch of a sequence stands in exactly one storage slot.
All inputs are finite; a program needn't handle non-finite values.
Results may differ from the reference program's by a relative error of at most 0.025.
Values may be sent and summed in bfloat16 or wider, within the bound.
A program may use at most 320 MiB of HBM per device.

```python
import math
import jax
import jax.numpy as jnp
from jax import lax

D = 2304
QUERY_HEADS = 8
KEY_VALUE_HEADS = 4
HEAD_SIZE = 256
FF = 9216
FBLK = 128
STRETCH = 64
ITERS = 5
STEP = 10
INPUT_MATRICES = 16
SEQUENCE_TOKENS = 1024
BATCH = 4
TOKENS = 4096
N_CTX = 8


def draw_weights_in(key, part):
    key = jax.random.fold_in(key, 17)
    base = jax.random.truncated_normal(key, -6.0, 6.0, (D, INPUT_MATRICES, HEAD_SIZE), jnp.float32)
    raise_factor = jnp.where(jnp.arange(INPUT_MATRICES) < QUERY_HEADS + KEY_VALUE_HEADS, 1.65, 1.0).astype(jnp.float32)
    return base * raise_factor[None, :, None] / math.sqrt(D)


def level_of(key, extent, cuts, smallest, largest):
    def one(axis_at, blocks):
        heights = jax.random.uniform(jax.random.fold_in(jax.random.fold_in(key, 6), axis_at), (blocks,), jnp.float32, smallest / len(cuts), largest / len(cuts))
        return jnp.repeat(jnp.exp(heights), extent[axis_at] // blocks).reshape((-1,) + (1,) * (len(extent) - axis_at - 1))

    factor_of = one(*cuts[0])
    for cut in cuts[1:]:
        factor_of = factor_of * one(*cut)
    return factor_of


def bell_draw(own_key, dims, scale, most, pieces=(), kind=jnp.bfloat16):
    array = jax.random.normal(own_key, dims, jnp.float32) * scale
    if len(pieces) > 0:
        array = level_of(own_key, dims, pieces, -0.22, 0.18) * array
    return jnp.clip(array, min=-most, max=most).astype(kind)


def setup_inputs(seed: int = 0) -> dict:
    key_of = jax.random.split(jax.random.key(seed), 13)
    return {
        "inputs": bell_draw(key_of[0], (BATCH, SEQUENCE_TOKENS, D), 1.0, 6.0, ((0, 4), (1, 8))),
        "cotangent": bell_draw(key_of[1], (BATCH, SEQUENCE_TOKENS, D), 1.0, 6.0, ((0, 4), (1, 8))),
        "weights_in": draw_weights_in(jax.random.fold_in(key_of[12], 71), 0),
        "weights_out": bell_draw(key_of[3], (D, QUERY_HEADS, HEAD_SIZE), D ** -0.5, 0.125, ((0, 8), (1, 4)), jnp.float32),
        "ffn_weights": bell_draw(key_of[4], (D, 3, FF), D ** -0.5, 0.125, ((0, 8), (2, 4)), jnp.float32),
        "norm_gains": jnp.clip(jax.random.uniform(key_of[5], (4, D), jnp.float32, -0.5, 0.5), -0.5, 0.5),
        "momentum_in": bell_draw(key_of[6], (D, INPUT_MATRICES, HEAD_SIZE), (TOKENS ** 0.5), 256.0, ((0, 8), (1, 4)), jnp.float32),
        "momentum_out": bell_draw(key_of[7], (D, QUERY_HEADS, HEAD_SIZE), (TOKENS ** 0.5), 256.0, ((0, 8), (1, 4)), jnp.float32),
        "ffn_momentum": bell_draw(key_of[8], (D, 3, FF), (0.5 * TOKENS ** 0.5), 192.0, ((0, 8), (2, 4)), jnp.float32),
        "gain_first": bell_draw(key_of[9], (4, D), (0.12 * TOKENS ** 0.5), 32.0, (), jnp.float32),
        "gain_second": jnp.clip(jnp.exp(jax.random.uniform(key_of[10], (4, D), jnp.float32, math.log(204.8), math.log(819.2))), 204.8, 819.2),
        "stretch_order": jax.random.permutation(key_of[11], 2 * N_CTX).astype(jnp.int32),
    }


SOFT_CAP = 50.0
EXP_SHIFT = 20.0
NORM_EPS = 1e-06
ROPE_THETA = 10000.0
MOMENTUM_DECAY = 0.95
LEARN_RATE = 0.3
WEIGHT_DECAY = 0.01
BETA_ONE = 0.9
BETA_TWO = 0.95
GAIN_RATE = 0.3
ADAM_EPS = 1e-08
NEWTON_A = 3.4445
NEWTON_B = -4.775
NEWTON_C = 2.0315
GELU_SCALE = 0.7978845608028654
GELU_CUBE = 0.044715
PRECISE = lax.Precision.HIGHEST

@jax.custom_vjp
def low(v):
    return lax.optimization_barrier(v.astype(jnp.bfloat16)).astype(jnp.float32)

@jax.custom_vjp
def low_back(v):
    return v

def low_keep(v):
    return (low(v), None)

def low_pass(kept, grad):
    return (grad,)

def back_keep(v):
    return (v, None)

def back_low(kept, grad):
    return (low(grad),)
low.defvjp(low_keep, low_pass)
low_back.defvjp(back_keep, back_low)

def positions(stretch_order):
    row_index = jnp.arange(SEQUENCE_TOKENS, dtype=jnp.int32)
    return stretch_order[row_index // STRETCH] * STRETCH + row_index % STRETCH

def rope_tables(places, width):
    half_width = width // 2
    frequency = ROPE_THETA ** (-(2.0 * jnp.arange(half_width, dtype=jnp.float32)) / width)
    angles = places.astype(jnp.float32)[:, None] * frequency[None, :]
    return (jnp.cos(angles), jnp.sin(angles))

def apply_rotation(values, cosine_lookup, sine_lookup):
    half_width = values.shape[-1] // 2
    first_half = values[..., :half_width]
    second_half = values[..., half_width:]
    cosine_part = cosine_lookup[:, None, :]
    sine_part = sine_lookup[:, None, :]
    return jnp.concatenate([first_half * cosine_part - second_half * sine_part, second_half * cosine_part + first_half * sine_part], -1)

def rms_scale(values):
    return lax.rsqrt(lax.optimization_barrier(jnp.mean(values * values, -1, keepdims=True)) + NORM_EPS)

def gelu_tanh(values):
    inner = GELU_SCALE * (values + GELU_CUBE * values * values * values)
    return 0.5 * values * (1.0 + jnp.tanh(inner))

def newton_step(matrices, gram_matrix):
    polynomial = NEWTON_B * gram_matrix + NEWTON_C * jnp.einsum('jef,jfg->jeg', gram_matrix, gram_matrix, precision=PRECISE)
    return NEWTON_A * matrices + jnp.einsum('jef,jfd->jed', polynomial, matrices, precision=PRECISE)

def orthogonalize(matrices):
    frob_norm = jnp.sqrt(lax.optimization_barrier(jnp.sum(matrices * matrices, axis=(1, 2), keepdims=True)))
    matrices = matrices / (frob_norm + 1e-07)
    for iteration in range(ITERS):
        gram_matrix = jnp.einsum('jed,jfd->jef', matrices, matrices, precision=PRECISE)
        matrices = newton_step(matrices, gram_matrix)
    return matrices

def block_forward(tokens, w_in, w_out, w_ffn, gains, places, cosine_lookup, sine_lookup):
    normed = low(tokens * rms_scale(tokens) * (1.0 + gains[0]))
    projection_result = low_back(jnp.einsum('td,dje->tje', normed, low(w_in), precision=PRECISE))
    query_group_width = QUERY_HEADS // KEY_VALUE_HEADS
    query_rows = low(apply_rotation(projection_result[:, :QUERY_HEADS], cosine_lookup, sine_lookup) * HEAD_SIZE ** (-0.5))
    key_rows_reduced = low(apply_rotation(projection_result[:, QUERY_HEADS:QUERY_HEADS + KEY_VALUE_HEADS], cosine_lookup, sine_lookup))
    value_rows_reduced = low(projection_result[:, QUERY_HEADS + KEY_VALUE_HEADS:])
    query_rows = query_rows.reshape(SEQUENCE_TOKENS, KEY_VALUE_HEADS, query_group_width, HEAD_SIZE)
    scores = low_back(jnp.einsum('tkge,uke->kgtu', query_rows, key_rows_reduced, precision=PRECISE))
    capped = SOFT_CAP * jnp.tanh(scores / SOFT_CAP)
    causal = places[None, :] <= places[:, None]
    exponent = jnp.where(causal, jnp.exp(capped - EXP_SHIFT), 0.0)
    row_total = lax.optimization_barrier(jnp.sum(exponent, -1))
    numerator = low_back(jnp.einsum('kgtu,uke->tkge', low(exponent), value_rows_reduced, precision=PRECISE))
    attended = low(numerator / jnp.transpose(row_total, (2, 0, 1))[..., None])
    branch = low_back(jnp.einsum('the,dhe->td', attended.reshape(SEQUENCE_TOKENS, QUERY_HEADS, HEAD_SIZE), low(w_out), precision=PRECISE))
    mixed = tokens + branch * rms_scale(branch) * (1.0 + gains[1])
    mid_low = low(mixed * rms_scale(mixed) * (1.0 + gains[2]))
    ffn_low = low(w_ffn)
    gate_up = low_back(jnp.einsum('td,dmf->tmf', mid_low, ffn_low[:, :2], precision=PRECISE))
    hidden = low(gelu_tanh(gate_up[:, 0]) * gate_up[:, 1])
    ffn_branch = low_back(jnp.einsum('tf,df->td', hidden, ffn_low[:, 2], precision=PRECISE))
    return mixed + ffn_branch * rms_scale(ffn_branch) * (1.0 + gains[3])

def reference(inputs, cotangent, weights_in, weights_out, ffn_weights, norm_gains, momentum_in, momentum_out, ffn_momentum, gain_first, gain_second, stretch_order):
    places = positions(stretch_order)
    cosine_lookup, sine_lookup = rope_tables(places, HEAD_SIZE)

    def forward(tokens, w_in, w_out, w_ffn, gain_set):
        return block_forward(tokens, w_in, w_out, w_ffn, gain_set, places, cosine_lookup, sine_lookup)

    def one_sequence(totals, seq_item):
        tokens, upstream = seq_item
        output, pullback = jax.vjp(forward, tokens.astype(jnp.float32), weights_in, weights_out, ffn_weights, norm_gains)
        grad_x, grad_in, grad_out, grad_ffn, grad_gain = pullback(upstream.astype(jnp.float32))
        new_totals = (totals[0] + grad_in, totals[1] + grad_out, totals[2] + grad_ffn, totals[3] + grad_gain)
        return (new_totals, (output.astype(jnp.bfloat16), grad_x))
    zero_state = (jnp.zeros_like(weights_in), jnp.zeros_like(weights_out), jnp.zeros_like(ffn_weights), jnp.zeros_like(norm_gains))
    (grad_in, grad_out, grad_ffn, grad_gain), (outputs, input_grad) = lax.scan(one_sequence, zero_state, (inputs, cotangent))
    shrink = 1.0 - LEARN_RATE * WEIGHT_DECAY
    new_momentum_in = MOMENTUM_DECAY * momentum_in + grad_in
    new_momentum_out = MOMENTUM_DECAY * momentum_out + grad_out
    new_ffn_momentum = MOMENTUM_DECAY * ffn_momentum + grad_ffn
    head_update = jnp.concatenate([grad_in + MOMENTUM_DECAY * new_momentum_in, grad_out + MOMENTUM_DECAY * new_momentum_out], 1)
    head_part = jnp.transpose(orthogonalize(jnp.transpose(head_update, (1, 2, 0))), (2, 0, 1))
    ffn_update = grad_ffn + MOMENTUM_DECAY * new_ffn_momentum
    ffn_blocks = jnp.transpose(ffn_update.reshape(D, 3 * (FF // FBLK), FBLK), (1, 2, 0))
    ffn_part = jnp.transpose(orthogonalize(ffn_blocks), (2, 0, 1)).reshape(D, 3, FF)
    head_rate = LEARN_RATE * (D / HEAD_SIZE) ** 0.5
    ffn_rate = LEARN_RATE * (D / FBLK) ** 0.5
    new_weights_in = weights_in * shrink - head_rate * head_part[:, :INPUT_MATRICES]
    new_weights_out = weights_out * shrink - head_rate * head_part[:, INPUT_MATRICES:]
    new_ffn_weights = ffn_weights * shrink - ffn_rate * ffn_part
    new_gain_first = BETA_ONE * gain_first + (1.0 - BETA_ONE) * grad_gain
    new_gain_second = BETA_TWO * gain_second + (1.0 - BETA_TWO) * grad_gain * grad_gain
    corrected_one = new_gain_first / (1.0 - BETA_ONE ** STEP)
    corrected_two = new_gain_second / (1.0 - BETA_TWO ** STEP)
    new_norm_gains = norm_gains - GAIN_RATE * corrected_one / (jnp.sqrt(corrected_two) + ADAM_EPS)
    return (outputs, input_grad, new_weights_in, new_weights_out, new_ffn_weights, new_momentum_in, new_momentum_out, new_ffn_momentum, new_norm_gains, new_gain_first, new_gain_second)
```

```python
import functools

import jax
import jax.numpy as jnp
from jax import lax
from jax.experimental import pallas as pl
from jax.experimental.pallas import tpu as pltpu
from jax.sharding import PartitionSpec as P

QUERY_HEADS = 8
KEY_VALUE_HEADS = 4
FBLK = 128
ITERS = 5
STEP = 10

SOFT_CAP = 50.0
EXP_SHIFT = 20.0
NORM_EPS = 1e-06
ROPE_THETA = 10000.0
MOMENTUM_DECAY = 0.95
LEARN_RATE = 0.3
WEIGHT_DECAY = 0.01
BETA_ONE = 0.9
BETA_TWO = 0.95
GAIN_RATE = 0.3
ADAM_EPS = 1e-08
NEWTON_A = 3.4445
NEWTON_B = -4.775
NEWTON_C = 2.0315
GELU_SCALE = 0.7978845608028654
GELU_CUBE = 0.044715
LOW = jnp.bfloat16
FULL = jnp.float32
SHRINK = 1.0 - LEARN_RATE * WEIGHT_DECAY
VMEM_LIMIT = 60 * 1024 * 1024


def rms_scale(values):
    return lax.rsqrt(jnp.mean(values * values, -1, keepdims=True) + NORM_EPS)


def positions_of(row_index, stretch_order, stretch_rows):
    stretch_slot = row_index // stretch_rows
    slot_table = jnp.arange(stretch_order.shape[0], dtype=jnp.int32)
    picked = jnp.sum(
        jnp.where(stretch_slot[:, None] == slot_table[None, :], stretch_order[None, :], 0), axis=1
    )
    return picked * stretch_rows + row_index % stretch_rows


def rope_tables(places, width):
    half_width = width // 2
    frequency = ROPE_THETA ** (-(2.0 * jnp.arange(half_width, dtype=jnp.float32)) / width)
    angles = places.astype(jnp.float32)[:, None] * frequency[None, :]
    return (jnp.cos(angles), jnp.sin(angles))


def rotate(values, cosine, sine):
    half = values.shape[-1] // 2
    first, second = values[..., :half], values[..., half:]
    return jnp.concatenate([first * cosine - second * sine, second * cosine + first * sine], -1)


def batched(left, right, left_dim, right_dim):
    return lax.dot_general(
        left, right, (((left_dim,), (right_dim,)), ((0,), (0,))), preferred_element_type=FULL
    )


def dot(left, right, left_dim, right_dim):
    return lax.dot_general(
        left, right, (((left_dim,), (right_dim,)), ((), ())), preferred_element_type=FULL
    )


def gram_kernel(blocks, grad_ref, old_ref, *refs):
    new_ref, update_ref, gram_ref = refs[-3:]
    grad = grad_ref[...].astype(FULL)
    new = MOMENTUM_DECAY * old_ref[0] + grad
    new_ref[0] = new
    update = (grad + MOMENTUM_DECAY * new).astype(LOW)
    update_ref[0] = update
    for block in range(blocks):
        piece = update[:, block * FBLK : (block + 1) * FBLK]
        gram_ref[block] = dot(piece, piece, 0, 0)


def ffn_gram(grads, momentum, first, blocks, earlier):
    _, rows, width = momentum.shape
    per_step = 6 if (width // FBLK) % 6 == 0 else 3
    span = per_step * FBLK
    steps = width // span
    spec = pl.BlockSpec((1, rows, span), lambda m, b: (m + first, 0, b))
    return pl.pallas_call(
        functools.partial(gram_kernel, per_step),
        grid=(grads.shape[1] // width, steps),
        in_specs=[pl.BlockSpec((rows, span), lambda m, b: (0, m * steps + b)), spec]
        + [ANY_SPEC] * len(earlier),
        out_specs=[
            spec,
            spec,
            pl.BlockSpec((per_step, FBLK, FBLK), lambda m, b: ((m + first) * steps + b, 0, 0)),
        ],
        out_shape=[
            jax.ShapeDtypeStruct(momentum.shape, FULL),
            jax.ShapeDtypeStruct(momentum.shape, LOW),
            jax.ShapeDtypeStruct((blocks, FBLK, FBLK), FULL),
        ],
        input_output_aliases={2 + index: index for index in range(len(earlier))},
        compiler_params=pltpu.CompilerParams(vmem_limit_bytes=VMEM_LIMIT),
        name="ffn_gram",
    )(grads, momentum, *earlier)


def split(values):
    high = values.astype(LOW)
    return high, (values - high.astype(FULL)).astype(LOW)


def fine_dot(left, right):
    (high, low), (right_high, right_low) = left, right
    return jnp.dot(
        jnp.concatenate([high, high, low], 1),
        jnp.concatenate([right_high, right_low, right_high], 0),
        preferred_element_type=FULL,
    )


def polys_of(grams):
    size = grams[0].shape[0]
    rows, columns = grid_of(size)
    eye = (rows == columns).astype(FULL)
    factors, totals = [], [None] * len(grams)
    for index, gram in enumerate(grams):
        trace = jnp.sum(jnp.sum(gram * eye, 0, keepdims=True), 1, keepdims=True)
        factors.append(1.0 / (jnp.sqrt(trace) + 1e-07))
        grams[index] = gram * (factors[index] * factors[index])
    for step in range(ITERS):
        parts = [split(gram) for gram in grams]
        squares = [fine_dot(part, part) for part in parts]
        quads = [
            NEWTON_A * eye + NEWTON_B * gram + NEWTON_C * square
            for gram, square in zip(grams, squares)
        ]
        quad_parts = [split(quad) for quad in quads]
        totals = [
            quad if total is None else fine_dot(split(total), part)
            for total, quad, part in zip(totals, quads, quad_parts)
        ]
        if step < ITERS - 1:
            halves = [fine_dot(quad, part) for quad, part in zip(quad_parts, parts)]
            grams = [fine_dot(split(half), quad) for half, quad in zip(halves, quad_parts)]
    return [total * factor for total, factor in zip(totals, factors)]


def moved(update, poly):
    high, low = split(poly)
    return jnp.dot(
        jnp.concatenate([update, update], 1),
        jnp.concatenate([high, low], 0),
        preferred_element_type=FULL,
    )


def tile_of(size):
    return 768 if size % 768 == 0 else 384


def remote(source, target, send, receive, axis, to):
    return pltpu.make_async_remote_copy(
        src_ref=source,
        dst_ref=target,
        send_sem=send,
        recv_sem=receive,
        device_id={axis: to},
        device_id_type=pl.DeviceIdType.MESH,
    )


def greet(peers):
    barrier = pltpu.get_barrier_semaphore()
    for axis, to in peers:
        pl.semaphore_signal(
            barrier, inc=1, device_id={axis: to}, device_id_type=pl.DeviceIdType.MESH
        )
    pl.semaphore_wait(barrier, len(peers))


def line_greet(at, size):
    barrier = pltpu.get_barrier_semaphore()
    for ok, to in ((at > 0, at - 1), (at < size - 1, at + 1)):

        @pl.when(ok)
        def _(to=to):
            pl.semaphore_signal(
                barrier, inc=1, device_id={"fsdp": to}, device_id_type=pl.DeviceIdType.MESH
            )

    inside = (at > 0) & (at < size - 1)
    for ok, peers in ((inside, 2), (jnp.logical_not(inside), 1)):

        @pl.when(ok)
        def _(peers=peers):
            pl.semaphore_wait(barrier, peers)


class LineGather:
    def __init__(self, at, size, span, out, send, receive):
        self.at, self.size, self.span = at, size, span
        self.out, self.send_sem, self.receive_sem = out, send, receive

    def piece(self, owner, chunk):
        return self.out.at[owner, pl.ds(pl.multiple_of(chunk * self.span, self.span), self.span)]

    def copy(self, owner, chunk, side):
        piece = self.piece(owner, chunk)
        to = (self.at + (1 if side == 0 else self.size - 1)) % self.size
        return remote(
            piece,
            piece,
            self.send_sem.at[side, owner, chunk],
            self.receive_sem.at[owner, chunk],
            "fsdp",
            to,
        )

    def start(self, chunk):
        @pl.when(self.at < self.size - 1)
        def _():
            self.copy(self.at, chunk, 0).start()

        @pl.when(self.at > 0)
        def _():
            self.copy(self.at, chunk, 1).start()

    def forward(self, chunk, gap):
        at, size = self.at, self.size

        @pl.when(at >= gap)
        def _(owner=at - gap):
            copy = self.copy(owner, chunk, 0)
            copy.wait_recv()

            @pl.when(at < size - 1)
            def _():
                copy.start()

        @pl.when(at + gap < size)
        def _(owner=at + gap):
            copy = self.copy(owner, chunk, 1)
            copy.wait_recv()

            @pl.when(at > 0)
            def _():
                copy.start()

    def drain(self, chunk):
        at, size = self.at, self.size
        for gap in range(size):

            @pl.when((at >= gap) & (at < size - 1))
            def _(owner=at - gap):
                self.copy(owner, chunk, 0).wait_send()

            @pl.when((at + gap < size) & (at > 0))
            def _(owner=at + gap):
                self.copy(owner, chunk, 1).wait_send()


def cut_of(rows):
    return 16 * (-(-rows // 32)) if rows >= 32 else rows


class Square:
    def __init__(self, at, size):
        self.at, self.column = at, size // 4
        self.core, self.x, self.y = at % 2, (at // 2) % 2, at // 4
        self.sibling = at + 1 - 2 * self.core

    def device(self, j, turn, core=None):
        x = 1 - self.x if turn else self.x
        core = self.core if core is None else core
        return (((self.y + j) % self.column) * 2 + x) * 2 + core

    def others(self):
        return range(1, self.column)

    def back(self, j):
        return (self.column - j) % self.column


def ctx_peers(at, size):
    square = Square(at, size)
    peers = [square.sibling, square.device(0, True)]
    return [("ctx", to) for to in peers + [square.device(j, False) for j in square.others()]]


class CtxGather:
    def __init__(self, at, size, source, slot, axis, sems):
        self.square = Square(at, size)
        self.source, self.slot, self.axis = source, slot, axis
        self.send, self.receive, self.pass_send, self.pass_receive, self.own = sems
        rows = source.shape[axis]
        cut = cut_of(rows)
        self.halves = (0, 1) if cut < rows else (0,)
        self.bounds = ((0, cut), (cut, rows - cut))

    def half(self, view, h):
        first, count = self.bounds[h]
        return view.at[(slice(None),) * self.axis + (pl.ds(first, count),)]

    def block(self, j, turn, h, core=None):
        return self.half(self.slot(self.square.device(j, turn, core)), h)

    def copy(self, source, target, h, send, j, turn, to):
        return remote(
            source,
            target,
            self.send.at[h, send],
            self.receive.at[h, j, int(turn)],
            "ctx",
            to,
        )

    def direct(self, h, j):
        square = self.square
        return self.copy(
            self.half(self.source, h),
            self.half(self.slot(square.at), h),
            h,
            j,
            square.back(j),
            j == 0,
            square.device(j, j == 0),
        )

    def onward(self, h, j):
        square = self.square
        block = self.block(0, True, 0) if h == 0 else self.block(j, False, 1)
        to = square.device(j, False) if h == 0 else square.device(0, True)
        origin = square.back(j) if h == 0 else j
        return self.copy(block, block, h, square.column + j, origin, True, to)

    def arrival(self, h, j, turn):
        block = self.block(j, turn, h)
        return remote(
            block, block, self.send.at[h, 0], self.receive.at[h, j, int(turn)], "ctx", self.square.sibling
        )

    def across(self, h, j, turn):
        block = self.block(j, turn, h)
        sems = (self.pass_send.at[h, j, int(turn)], self.pass_receive.at[h, j, int(turn)])
        return remote(block, block, *sems, "ctx", self.square.sibling)

    def crossed(self, h, j, turn):
        block = self.block(j, turn, h, 1 - self.square.core)
        sems = (self.pass_send.at[h, j, int(turn)], self.pass_receive.at[h, j, int(turn)])
        return remote(block, block, *sems, "ctx", self.square.sibling)

    def mine(self, h):
        sems = (self.pass_send.at[h, 0, 0], self.pass_receive.at[h, 0, 0])
        target = self.half(self.slot(self.square.at), h)
        return remote(self.half(self.source, h), target, *sems, "ctx", self.square.sibling)

    def keep(self):
        return pltpu.make_async_copy(self.source, self.slot(self.square.at), self.own)

    def start(self):
        others, halves = self.square.others(), self.halves
        self.direct(0, 0).start()
        for j in others:
            self.direct(halves[-1], j).start()
        if len(halves) > 1:
            self.direct(1, 0).start()
            for j in others:
                self.direct(0, j).start()
        for h in halves:
            self.mine(h).start()
        self.keep().start()

    def land(self, h, j, turn):
        self.arrival(h, j, turn).wait_recv()
        self.across(h, j, turn).start()

    def forward(self):
        others, halves = self.square.others(), self.halves
        self.land(0, 0, True)
        for j in others:
            self.onward(0, j).start()
        if len(halves) > 1:
            for j in others:
                self.land(1, j, False)
                self.onward(1, j).start()

    def rest(self):
        others, halves = self.square.others(), self.halves
        if len(halves) > 1:
            self.land(1, 0, True)
        for j in others:
            self.land(0, j, False)
        for j in others:
            for h in halves:
                self.land(h, j, True)

    def finish(self):
        square, halves = self.square, self.halves
        for h in halves:
            for j in range(square.column):
                self.direct(h, j).wait_send()
                if j > 0:
                    self.onward(h, j).wait_send()
                for turn in (False, True):
                    self.crossed(h, j, turn).wait_recv()
                    if j > 0 or turn:
                        self.across(h, j, turn).wait_send()
            self.mine(h).wait_send()
        self.keep().wait()


def ctx_gather_sems(size):
    column = size // 4
    dma = pltpu.SemaphoreType.DMA
    return [dma((2, 2 * column)), dma((2, column, 2)), dma((2, column, 2)), dma((2, column, 2)), dma]


class CtxScatter:
    def __init__(self, at, size, part, first, hold, along_x, along_y, landed, sems):
        self.square = Square(at, size)
        self.part, self.first, self.hold = part, first, hold
        self.along_x, self.along_y, self.landed = along_x, along_y, landed
        self.near_send, self.near_receive, self.send, self.receive = sems
        self.step = 16 if first.dtype == LOW else 8
        rows = hold.shape[2]
        cut = cut_of(rows)
        self.bounds = ((0, cut), (cut, rows - cut))

    def index(self, j, turn):
        return j * 2 + int(turn)

    def near(self, j, turn):
        index = self.index(j, turn)
        return remote(
            self.part(self.square.device(j, turn, 1 - self.square.core)),
            self.first.at[index],
            self.near_send.at[index],
            self.near_receive.at[index],
            "ctx",
            self.square.sibling,
        )

    def half(self, view, h):
        return view.at[:, pl.ds(*self.bounds[h])]

    def far(self, kind, j):
        square, h = self.square, kind % 2
        if kind < 2:
            source = self.half(self.hold.at[self.index(j, True)], h)
            target = self.along_x.at[j - 1] if kind == 0 else self.along_y.at[square.back(j) - 1]
        elif kind < 4:
            source = self.half(self.hold.at[self.index(0, True)], h)
            target = self.half(self.landed.at[0], h)
        else:
            source = self.half(self.hold.at[self.index(j, False)], h)
            target = self.half(self.landed.at[square.back(j)], h)
        along_x = kind in (0, 2, 3)
        to = square.device(0, True) if along_x else square.device(j, False)
        return remote(
            source,
            target,
            self.send.at[kind, j],
            self.receive.at[kind, j if along_x else square.back(j)],
            "ctx",
            to,
        )

    def arrival(self, kind, j):
        h = kind % 2
        if kind < 2:
            block = (self.along_x if kind == 0 else self.along_y).at[j - 1]
        else:
            block = self.half(self.landed.at[0 if kind < 4 else j], h)
        return remote(
            block, block, self.send.at[kind, j], self.receive.at[kind, j], "ctx", self.square.sibling
        )

    def rows(self, first, count, body):
        def one(index, carried):
            offset = pl.multiple_of(index * self.step, self.step)
            for block in range(self.hold.shape[1]):
                body(block, offset)
            return carried

        lax.fori_loop(first // self.step, (first + count) // self.step, one, 0)

    def pair(self, j, turn):
        self.near(j, turn).wait_recv()
        index = self.index(j, turn)
        part = self.part(self.square.device(j, turn))

        def add(block, offset):
            rows = pl.ds(offset, self.step)
            total = part[block, rows, :].astype(FULL)
            total = total + self.first[index, block, rows, :].astype(FULL)
            self.hold[index, block, rows, :] = total.astype(self.hold.dtype)

        self.rows(0, self.hold.shape[2], add)

    def start(self):
        others = self.square.others()
        for j in others:
            self.near(j, True).start()
        self.near(0, True).start()
        for j in others:
            self.near(j, False).start()
        self.near(0, False).start()

    def diagonal(self):
        for j in self.square.others():
            self.pair(j, True)
            self.far(0, j).start()
            self.far(1, j).start()

    def neighbours(self):
        self.pair(0, True)
        self.far(2, 0).start()
        for j in self.square.others():
            self.pair(j, False)
            self.far(5, j).start()

    def add_passing(self, index, h, block_of):
        first, count = self.bounds[h]

        def add(block, offset):
            rows = pl.ds(offset, self.step)
            local = pl.ds(pl.multiple_of(offset - first, self.step), self.step)
            total = self.hold[index, block, rows, :].astype(FULL)
            for passing in block_of:
                total = total + passing[block, local, :].astype(FULL)
            self.hold[index, block, rows, :] = total.astype(self.hold.dtype)

        self.rows(first, count, add)

    def passing(self):
        others = self.square.others()
        for j in others:
            self.arrival(0, j).wait_recv()
            self.add_passing(self.index(j, False), 0, [self.along_x.at[j - 1]])
            self.far(4, j).start()
        for j in others:
            self.arrival(1, j).wait_recv()
        self.add_passing(self.index(0, True), 1, [self.along_y.at[j - 1] for j in others])
        self.far(3, 0).start()

    def finish(self, store):
        others = self.square.others()
        self.near(0, False).wait_recv()
        for kind in (2, 3):
            self.arrival(kind, 0).wait_recv()
        for j in others:
            for kind in (5, 4):
                self.arrival(kind, j).wait_recv()
        part = self.part(self.square.at)

        def add(block, offset):
            rows = pl.ds(offset, self.step)
            total = part[block, rows, :].astype(FULL) + self.first[0, block, rows, :].astype(FULL)
            for index in range(self.landed.shape[0]):
                total = total + self.landed[index, block, rows, :].astype(FULL)
            store(block, rows, total)

        self.rows(0, self.hold.shape[2], add)

    def drain(self):
        for j in range(self.square.column):
            for turn in (False, True):
                self.near(j, turn).wait_send()
        for kind in (2, 3):
            self.far(kind, 0).wait_send()
        for j in self.square.others():
            for kind in (0, 1, 4, 5):
                self.far(kind, j).wait_send()


SCATTER = 9


def ctx_scatter_scratch(size, blocks, rows, width, kind):
    chips, column = size // 2, size // 4
    cut = cut_of(rows)
    dma = pltpu.SemaphoreType.DMA
    return [
        pltpu.VMEM((chips, blocks, rows, width), kind),
        pltpu.VMEM((chips, blocks, rows, width), kind),
        pltpu.VMEM((column - 1, blocks, cut, width), kind),
        pltpu.VMEM((column - 1, blocks, rows - cut, width), kind),
        pltpu.VMEM((column, blocks, rows, width), kind),
        dma((chips,)),
        dma((chips,)),
        dma((6, column)),
        dma((6, column)),
    ]


def ctx_scatter(at, size, part, scratch):
    return CtxScatter(at, size, part, *scratch[:5], scratch[5:9])


def rows_of_ctx(ref):
    return lambda c: ref.at[pl.ds(c, 1)]


VMEM_SPEC = pl.BlockSpec(memory_space=pltpu.VMEM)
ANY_SPEC = pl.BlockSpec(memory_space=pl.ANY)


def head_places(fsdp):
    heads = QUERY_HEADS // fsdp
    pairs = max(1, KEY_VALUE_HEADS // fsdp)
    stored = (QUERY_HEADS + 2 * KEY_VALUE_HEADS) // fsdp
    places = []
    for user in range(fsdp):
        first = (user * heads) // (QUERY_HEADS // KEY_VALUE_HEADS)
        used = [user * heads + h for h in range(heads)]
        used += [QUERY_HEADS + first + p for p in range(pairs)]
        used += [QUERY_HEADS + KEY_VALUE_HEADS + first + p for p in range(pairs)]
        places.append([(matrix // stored, matrix % stored) for matrix in used])
    return places


def prepare_kernel(
    ctx, fsdp, in_ref, out_ref, ffn_ref, x_ref, gains, mine, out_all, ffn_low, normed, *scratch
):
    at, line_at = lax.axis_index("ctx"), lax.axis_index("fsdp")
    in_low, out_low, wide, wide_sem, move_send, move_receive = scratch[:6]
    places = head_places(fsdp)
    head = in_ref.shape[2]
    greet(ctx_peers(at, ctx) + [("fsdp", (line_at + k) % fsdp) for k in range(1, fsdp)])

    def move(user, slot):
        owner, index = places[user][slot]
        return remote(
            in_low.at[index],
            mine.at[:, pl.ds(slot * head, head)],
            move_send.at[user, slot],
            move_receive.at[slot],
            "fsdp",
            user,
        )

    def load(matrix):
        return pltpu.make_async_copy(
            ffn_ref.at[matrix], wide.at[matrix % 2], wide_sem.at[matrix % 2]
        )

    load(0).start()
    for index in range(in_ref.shape[1]):
        in_low[index] = in_ref[:, index, :].astype(LOW)
    for user in range(fsdp):
        for slot in range(len(places[0])):
            owner, index = places[user][slot]

            @pl.when(line_at == owner)
            def _(user=user, slot=slot, owner=owner, index=index):
                if user == owner:
                    mine[:, slot * head : (slot + 1) * head] = in_low[index]
                else:
                    move(user, slot).start()

    for index in range(out_ref.shape[1]):
        out_low[:, index * head : (index + 1) * head] = out_ref[:, index, :].astype(LOW)
    gather = CtxGather(at, ctx, out_low, lambda c: out_all.at[c], 0, scratch[6:11])
    gather.start()
    x = x_ref[...].astype(FULL)
    normed[...] = (x * rms_scale(x) * (1.0 + gains[0:1, :])).astype(LOW)
    for matrix in range(3):
        load(matrix).wait()
        if matrix < 2:
            load(matrix + 1).start()
        ffn_low[matrix] = wide[matrix % 2].astype(LOW)
    gather.forward()
    gather.rest()
    for user in range(fsdp):

        @pl.when(line_at == user)
        def _(user=user):
            for slot in range(len(places[0])):
                if places[user][slot][0] != user:
                    move(user, slot).wait_recv()

        for slot in range(len(places[0])):
            owner, index = places[user][slot]
            if user != owner:

                @pl.when(line_at == owner)
                def _(user=user, slot=slot):
                    move(user, slot).wait_send()

    gather.finish()


def prepare(weights_in, weights_out, ffn, x, gains, ctx, fsdp):
    local_rows, in_local, head = weights_in.shape
    out_local = weights_out.shape[1]
    mine = len(head_places(fsdp)[0])
    dma = pltpu.SemaphoreType.DMA
    return pl.pallas_call(
        functools.partial(prepare_kernel, ctx, fsdp),
        in_specs=[VMEM_SPEC] * 2 + [ANY_SPEC] + [VMEM_SPEC] * 2,
        out_specs=[VMEM_SPEC, ANY_SPEC, VMEM_SPEC, VMEM_SPEC],
        out_shape=[
            jax.ShapeDtypeStruct((local_rows, mine * head), LOW),
            jax.ShapeDtypeStruct((ctx, local_rows, out_local * head), LOW),
            jax.ShapeDtypeStruct(ffn.shape, LOW),
            jax.ShapeDtypeStruct(x.shape, LOW),
        ],
        scratch_shapes=[
            pltpu.VMEM((in_local, local_rows, head), LOW),
            pltpu.VMEM((local_rows, out_local * head), LOW),
            pltpu.VMEM((2,) + ffn.shape[1:], FULL),
            dma((2,)),
            dma((fsdp, mine)),
            dma((mine,)),
        ]
        + ctx_gather_sems(ctx),
        compiler_params=pltpu.CompilerParams(vmem_limit_bytes=VMEM_LIMIT, collective_id=0),
        name="prepare",
    )(weights_in, weights_out, ffn, x, gains)


def project_kernel(
    ctx, fsdp, span, heads, own, mine, cosine, sine, normed, in_all, query, key_all, value_all, *scratch
):
    at, line_at = lax.axis_index("ctx"), lax.axis_index("fsdp")
    key, value, low_send, low_receive = scratch[:4]
    tokens = own.shape[0]
    rows = key.shape[1]
    local_rows = mine.shape[0]
    head = 2 * cosine.shape[1]
    pairs = key.shape[2] // head
    chunks = tokens // span
    greet(ctx_peers(at, ctx) + [("fsdp", (line_at + k) % fsdp) for k in range(1, fsdp)])
    line = LineGather(line_at, fsdp, span, normed, low_send, low_receive)
    normed[line_at] = own[...]
    for chunk in range(chunks):
        line.start(chunk)
    step = 16

    def slot(c):
        return in_all.at[pl.ds(pl.multiple_of(c * local_rows, step), local_rows)]

    gather_in = CtxGather(at, ctx, mine, slot, 0, scratch[4:9])
    gather_in.start()
    for chunk in range(chunks):
        line.forward(chunk, 1)
    gather_in.forward()
    for gap in range(2, fsdp):
        for chunk in range(chunks):
            line.forward(chunk, gap)
    gather_in.rest()
    gather_in.finish()

    def projected(index, write, turn, scale):
        weights = in_all[:, index * head : (index + 1) * head]
        for sequence in range(fsdp):
            result = dot(normed[sequence], weights, 1, 0)
            if turn:
                first, second = result[:, : head // 2], result[:, head // 2 :]
                result = jnp.concatenate(
                    [
                        first * cosine[...] - second * sine[...],
                        second * cosine[...] + first * sine[...],
                    ],
                    1,
                )
            write(sequence, (result * scale).astype(LOW))

    per_device = tokens // rows
    for pair in range(pairs):
        columns = slice(pair * head, (pair + 1) * head)
        for matrix, target, turn in (
            (heads + pair, key, True),
            (heads + pairs + pair, value, False),
        ):

            def write(sequence, result, target=target, columns=columns):
                for inner in range(per_device):
                    target[sequence * per_device + inner, :, columns] = result[
                        inner * rows : (inner + 1) * rows
                    ]

            projected(matrix, write, turn, 1.0)

    keys = CtxGather(at, ctx, key, lambda c: key_all.at[:, c], 1, scratch[9:14])
    values = CtxGather(at, ctx, value, lambda c: value_all.at[:, c], 1, scratch[14:19])
    keys.start()
    values.start()
    for index in range(heads):

        def write(sequence, result, index=index):
            query[sequence * tokens : (sequence + 1) * tokens, index * head : (index + 1) * head] = result

        projected(index, write, True, head ** (-0.5))
    keys.forward()
    values.forward()
    keys.rest()
    values.rest()
    for chunk in range(chunks):
        line.drain(chunk)
    keys.finish()
    values.finish()


def project(own, mine, cosine, sine, sequences, heads, pairs, ctx, fsdp):
    tokens, width = own.shape
    local_rows = mine.shape[0]
    head = 2 * cosine.shape[1]
    rows = tokens // sequences
    chunks = 4
    dma = pltpu.SemaphoreType.DMA
    block = (fsdp * sequences, rows, pairs * head)
    spread = (fsdp * sequences, ctx, rows, pairs * head)
    return pl.pallas_call(
        functools.partial(project_kernel, ctx, fsdp, tokens // chunks, heads),
        in_specs=[VMEM_SPEC] * 4,
        out_specs=[VMEM_SPEC] * 3 + [ANY_SPEC] * 2,
        out_shape=[
            jax.ShapeDtypeStruct((fsdp, tokens, width), LOW),
            jax.ShapeDtypeStruct((ctx * local_rows, mine.shape[1]), LOW),
            jax.ShapeDtypeStruct((fsdp * tokens, heads * head), LOW),
            jax.ShapeDtypeStruct(spread, LOW),
            jax.ShapeDtypeStruct(spread, LOW),
        ],
        scratch_shapes=[
            pltpu.VMEM(block, LOW),
            pltpu.VMEM(block, LOW),
            dma((2, fsdp, chunks)),
            dma((fsdp, chunks)),
        ]
        + ctx_gather_sems(ctx) * 3,
        compiler_params=pltpu.CompilerParams(vmem_limit_bytes=VMEM_LIMIT, collective_id=1),
        name="project",
    )(own, mine, cosine, sine)


class LineExchange:
    def __init__(self, at, size, span, part, low_all, mid, scratch):
        self.at, self.size, self.span, self.part, self.mid = at, size, span, part, mid
        self.hold, self.landed, self.total, self.send, self.receive = scratch[:5]
        self.chunks = part.shape[1] // span
        self.low_all = low_all
        if low_all is not None:
            self.line = LineGather(at, size, span, low_all, *scratch[5:7])
        self.steps = self.chunks + (size - 1) * (1 if low_all is None else 2)

    def hop(self, source, target, chunk, side):
        to = (self.at + (1 if side == 0 else self.size - 1)) % self.size
        rows = pl.ds(pl.multiple_of(chunk * self.span, self.span), self.span)
        return remote(
            source.at[target, rows],
            self.landed.at[side, target, rows],
            self.send.at[target, chunk],
            self.receive.at[side, target, chunk],
            "fsdp",
            to,
        )

    def pass_on(self, target, chunk, side):
        rows = pl.ds(pl.multiple_of(chunk * self.span, self.span), self.span)
        origin = self.at == 0 if side == 0 else self.at == self.size - 1

        @pl.when(origin)
        def _():
            self.hop(self.part, target, chunk, side).start()

        @pl.when(jnp.logical_not(origin))
        def _():
            self.hop(self.part, target, chunk, side).wait_recv()
            added = self.part[target, rows, :].astype(FULL)
            added = added + self.landed[side, target, rows, :].astype(FULL)
            self.hold[target, rows, :] = added.astype(LOW)
            self.hop(self.hold, target, chunk, side).start()

    def step(self, index):
        at, size, chunks = self.at, self.size, self.chunks
        for gap in range(size - 1, 0, -1):
            chunk = index - at

            @pl.when((at + gap < size) & (chunk >= 0) & (chunk < chunks))
            def _(target=at + gap, chunk=chunk):
                self.pass_on(target, chunk, 0)

            chunk = index - (size - 1 - at)

            @pl.when((at >= gap) & (chunk >= 0) & (chunk < chunks))
            def _(target=at - gap, chunk=chunk):
                self.pass_on(target, chunk, 1)

        chunk = index - (size - 1)

        @pl.when((chunk >= 0) & (chunk < chunks))
        def _():
            rows = pl.ds(pl.multiple_of(chunk * self.span, self.span), self.span)
            self.total[...] = self.part[at, rows, :].astype(FULL)
            for side, ok in ((0, at > 0), (1, at < size - 1)):

                @pl.when(ok)
                def _(side=side):
                    self.hop(self.part, at, chunk, side).wait_recv()
                    self.total[...] += self.landed[side, at, rows, :].astype(FULL)

            low = self.mid(chunk, rows, self.total[...])
            if self.low_all is not None:
                self.low_all[at, rows, :] = low
                self.line.start(chunk)

        if self.low_all is not None:
            for gap in range(1, size):
                chunk = index - (size - 1) - gap

                @pl.when((chunk >= 0) & (chunk < chunks))
                def _(gap=gap, chunk=chunk):
                    self.line.forward(chunk, gap)

    def run(self, first, last):
        def one(index, carried):
            self.step(index)
            return carried

        lax.fori_loop(first, last, one, 0)

    def drain(self):
        at, size = self.at, self.size

        def one(chunk, carried):
            for gap in range(1, size):

                @pl.when(at + gap < size)
                def _(target=at + gap):
                    self.hop(self.part, target, chunk, 0).wait_send()

                @pl.when(at >= gap)
                def _(target=at - gap):
                    self.hop(self.part, target, chunk, 1).wait_send()

            if self.low_all is not None:
                self.line.drain(chunk)
            return carried

        lax.fori_loop(0, self.chunks, one, 0)


def line_span(tokens):
    return 16


def line_scratch(fsdp, tokens, width, gather):
    span = line_span(tokens)
    chunks = tokens // span
    dma = pltpu.SemaphoreType.DMA
    return [
        pltpu.VMEM((fsdp, tokens, width), LOW),
        pltpu.VMEM((2, fsdp, tokens, width), LOW),
        pltpu.VMEM((span, width), FULL),
        dma((fsdp, chunks)),
        dma((2, fsdp, chunks)),
    ] + ([dma((2, fsdp, chunks)), dma((fsdp, chunks))] if gather else [])


def exchange_kernel(mid, size, inputs, part, *refs):
    at = lax.axis_index("fsdp")
    ins, gains, low_all, refs = refs[:inputs], refs[inputs], refs[inputs + 1], refs[inputs + 2 :]
    outs, scratch = refs[:-7], refs[-7:]
    line_greet(at, size)
    line = LineExchange(
        at,
        size,
        line_span(part.shape[1]),
        part,
        low_all,
        lambda chunk, rows, total: mid(chunk, rows, total, ins, gains, outs),
        scratch,
    )
    line.run(0, line.steps)
    line.drain()


def exchange(part, ins, gains, mid, out_shape, fsdp, collective_id, name):
    _, tokens, width = part.shape
    return pl.pallas_call(
        functools.partial(exchange_kernel, mid, fsdp, len(ins)),
        in_specs=[VMEM_SPEC] * (len(ins) + 2),
        out_specs=[VMEM_SPEC] * (len(out_shape) + 1),
        out_shape=[jax.ShapeDtypeStruct(part.shape, LOW)] + out_shape,
        scratch_shapes=line_scratch(fsdp, tokens, width, True),
        compiler_params=pltpu.CompilerParams(
            vmem_limit_bytes=VMEM_LIMIT, collective_id=collective_id
        ),
        name=name,
    )(part, *ins, gains)


class Forward:
    def __init__(self, mid, weights, hidden, gate_factor, up_factor, part, scratch):
        self.weights, self.part = weights, part
        self.outs = (hidden, gate_factor, up_factor)
        self.mid, self.hidden, self.pair, self.down, self.pair_sem, self.down_sem = scratch
        self.sequences, self.tokens, _ = mid.shape
        self.half = self.tokens // 2
        self.span, self.reach = self.pair.shape[3], self.down.shape[1]
        self.tiles = weights.shape[2] // self.span
        self.ends = weights.shape[1] // self.reach
        self.count = self.tiles + self.ends
        for half in range(2):
            for sequence in range(self.sequences):
                rows = slice(sequence * self.half, (sequence + 1) * self.half)
                self.mid[half, rows, :] = mid[sequence, half * self.half : (half + 1) * self.half, :]

    def fetch_pair(self, half, tile):
        slot = (half * self.tiles + tile) % 2
        columns = pl.ds(pl.multiple_of(tile * self.span, self.span), self.span)
        return pltpu.make_async_copy(
            self.weights.at[pl.ds(0, 2), :, columns], self.pair.at[slot], self.pair_sem.at[slot]
        )

    def fetch_down(self, half, tile):
        slot = (half * self.ends + tile) % 2
        rows = pl.ds(pl.multiple_of(tile * self.reach, self.reach), self.reach)
        return pltpu.make_async_copy(
            self.weights.at[2, rows], self.down.at[slot], self.down_sem.at[slot]
        )

    def fetch(self, index):
        half, tile = index // self.count, index % self.count

        @pl.when(tile < self.tiles)
        def _():
            self.fetch_pair(half, tile).start()

        @pl.when(tile >= self.tiles)
        def _():
            self.fetch_down(half, tile - self.tiles).start()

    def rows(self, half):
        return pl.ds(pl.multiple_of(half * self.half, 16), self.half)

    def run(self, index):
        half, tile = index // self.count, index % self.count

        @pl.when(index + 1 < 2 * self.count)
        def _():
            self.fetch(index + 1)

        @pl.when(tile < self.tiles)
        def _():
            self.fetch_pair(half, tile).wait()
            slot = (half * self.tiles + tile) % 2
            mid = self.mid[half]
            gate = dot(mid, self.pair[slot, 0], 1, 0)
            up = dot(mid, self.pair[slot, 1], 1, 0)
            columns = pl.ds(pl.multiple_of(tile * self.span, self.span), self.span)
            results = [value.astype(LOW) for value in activate(gate, up)]
            self.hidden[half, :, columns] = results[0]
            for out, value in zip(self.outs, results):
                for sequence in range(self.sequences):
                    out[sequence, self.rows(half), columns] = value[
                        sequence * self.half : (sequence + 1) * self.half
                    ]

        @pl.when(tile >= self.tiles)
        def _():
            end = tile - self.tiles
            self.fetch_down(half, end).wait()
            slot = (half * self.ends + end) % 2
            value = dot(self.hidden[half], self.down[slot], 1, 1).astype(LOW)
            columns = pl.ds(pl.multiple_of(end * self.reach, self.reach), self.reach)
            for sequence in range(self.sequences):
                self.part[sequence, self.rows(half), columns] = value[
                    sequence * self.half : (sequence + 1) * self.half
                ]


def activate(gate, up):
    square = gate * gate
    squashed = jnp.tanh(GELU_SCALE * gate * (1.0 + GELU_CUBE * square))
    half = 0.5 + 0.5 * squashed
    act = gate * half
    slope = half + act * (1.0 - squashed) * (GELU_SCALE + 3.0 * GELU_SCALE * GELU_CUBE * square)
    return act * up, up * slope, act


def late_kernel(
    size, mid, mixed, cotangent, gains, weights, late, out, gain, hidden, gate_factor, up_factor, *scratch
):
    at = lax.axis_index("fsdp")
    line_greet(at, size)
    part = scratch[0]
    line = LineExchange(
        at,
        size,
        line_span(part.shape[1]),
        part,
        late,
        lambda chunk, rows, total: late_mid(
            chunk, rows, total, (mixed, cotangent), gains, (out, gain)
        ),
        scratch[1:8],
    )
    forward = Forward(mid, weights, hidden, gate_factor, up_factor, part, scratch[8:])
    forward.fetch(0)

    def one(index, carried):
        forward.run(index)
        return carried

    lax.fori_loop(0, forward.count, one, 0)
    ahead = line.chunks // 2 - 1
    share = -(-forward.count // ahead)

    def both(index, carried):
        line.step(index)

        def more(inner, carried):
            tile = forward.count + index * share + inner

            @pl.when(tile < 2 * forward.count)
            def _():
                forward.run(tile)

            return carried

        lax.fori_loop(0, share, more, 0)
        return carried

    lax.fori_loop(0, ahead, both, 0)
    line.run(ahead, line.steps)
    line.drain()


def late_exchange(mid, weights, mixed, cotangent, gains, collective_id):
    fsdp, tokens, width = mid.shape
    units = weights.shape[2]
    span, reach = tile_of(units), tile_of(width)
    rows = fsdp * tokens // 2
    dma = pltpu.SemaphoreType.DMA
    low = jax.ShapeDtypeStruct((fsdp, tokens, units), LOW)
    return pl.pallas_call(
        functools.partial(late_kernel, fsdp),
        in_specs=[VMEM_SPEC] * 4 + [ANY_SPEC],
        out_specs=[VMEM_SPEC] * 6,
        out_shape=[
            jax.ShapeDtypeStruct(mid.shape, LOW),
            jax.ShapeDtypeStruct((tokens, width), LOW),
            jax.ShapeDtypeStruct((1, width), FULL),
            low,
            low,
            low,
        ],
        scratch_shapes=[pltpu.VMEM(mid.shape, LOW)]
        + line_scratch(fsdp, tokens, width, True)
        + [
            pltpu.VMEM((2, rows, width), LOW),
            pltpu.VMEM((2, rows, units), LOW),
            pltpu.VMEM((2, 2, width, span), LOW),
            pltpu.VMEM((2, reach, units), LOW),
            dma((2,)),
            dma((2,)),
        ],
        compiler_params=pltpu.CompilerParams(
            vmem_limit_bytes=VMEM_LIMIT, collective_id=collective_id
        ),
        name="late_exchange",
    )(mid, mixed, cotangent, gains, weights)


class Backward:
    def __init__(self, late, mid, weights, gate_factor, up_factor, part, grads, scratch):
        self.weights, self.part, self.grads, self.mid = weights, part, grads, mid
        self.factors = (gate_factor, up_factor)
        self.late, self.turned, self.pairs, self.wide, self.tall, self.stage = scratch[:6]
        self.wide_sem, self.tall_sem, self.stage_sem, self.mid_sem = scratch[6:]
        self.sequences, self.tokens, self.width = late.shape
        self.half = self.tokens // 2
        self.span, self.reach = self.wide.shape[2], self.tall.shape[2]
        self.units = weights.shape[2]
        self.tiles = self.units // self.span
        self.ends = self.width // self.reach
        self.count = self.tiles + self.ends
        self.sums = 2 * self.units // self.stage.shape[2]
        for half in range(2):
            for sequence in range(self.sequences):
                rows = slice(sequence * self.half, (sequence + 1) * self.half)
                self.late[half, rows, :] = late[sequence, half * self.half : (half + 1) * self.half, :]

    def fetch_mid(self):
        return [
            pltpu.make_async_copy(
                self.mid.at[s, pl.ds(half * self.half, self.half)],
                self.late.at[half, pl.ds(s * self.half, self.half)],
                self.mid_sem.at[half * self.sequences + s],
            )
            for half in range(2)
            for s in range(self.sequences)
        ]

    def turn(self):
        rows = self.sequences * self.half
        for copy in self.fetch_mid():
            copy.wait()
        for half in range(2):
            for first in range(0, self.width, self.reach):
                block = self.late[half, :, first : first + self.reach]
                self.turned[first : first + self.reach, half * rows : (half + 1) * rows] = block.T

    def fetch_wide(self, half, tile):
        slot = (half * self.tiles + tile) % 2
        columns = pl.ds(pl.multiple_of(tile * self.span, self.span), self.span)
        return pltpu.make_async_copy(
            self.weights.at[2, :, columns], self.wide.at[slot], self.wide_sem.at[slot]
        )

    def fetch_tall(self, half, tile):
        slot = (half * self.ends + tile) % 2
        rows = pl.ds(pl.multiple_of(tile * self.reach, self.reach), self.reach)
        return pltpu.make_async_copy(
            self.weights.at[pl.ds(0, 2), rows], self.tall.at[slot], self.tall_sem.at[slot]
        )

    def fetch(self, index):
        half, tile = index // self.count, index % self.count

        @pl.when(tile < self.tiles)
        def _():
            self.fetch_wide(half, tile).start()

        @pl.when(tile >= self.tiles)
        def _():
            self.fetch_tall(half, tile - self.tiles).start()

    def run(self, index):
        half, tile = index // self.count, index % self.count
        rows = pl.ds(pl.multiple_of(half * self.half, 16), self.half)

        @pl.when(index + 1 < 2 * self.count)
        def _():
            self.fetch(index + 1)

        @pl.when(tile < self.tiles)
        def _():
            self.fetch_wide(half, tile).wait()
            slot = (half * self.tiles + tile) % 2
            hidden_grad = dot(self.late[half], self.wide[slot], 1, 0)
            columns = pl.ds(pl.multiple_of(tile * self.span, self.span), self.span)
            for side, factor in enumerate(self.factors):
                target = pl.ds(
                    pl.multiple_of(side * self.units + tile * self.span, self.span), self.span
                )
                for s in range(self.sequences):
                    own = slice(s * self.half, (s + 1) * self.half)
                    value = hidden_grad[own] * factor[s, rows, columns].astype(FULL)
                    self.pairs[half, own, target] = value.astype(LOW)

        @pl.when(tile >= self.tiles)
        def _():
            end = tile - self.tiles
            self.fetch_tall(half, end).wait()
            slot = (half * self.ends + end) % 2
            value = dot(self.pairs[half, :, : self.units], self.tall[slot, 0], 1, 1)
            value = value + dot(self.pairs[half, :, self.units :], self.tall[slot, 1], 1, 1)
            value = value.astype(LOW)
            columns = pl.ds(pl.multiple_of(end * self.reach, self.reach), self.reach)
            for s in range(self.sequences):
                self.part[s, rows, columns] = value[s * self.half : (s + 1) * self.half]

    def put(self, index):
        span = self.stage.shape[2]
        columns = pl.ds(pl.multiple_of(index * span, span), span)
        return pltpu.make_async_copy(
            self.stage.at[index % 2], self.grads.at[:, columns], self.stage_sem.at[index % 2]
        )

    def sum(self, index):
        @pl.when(index >= 2)
        def _():
            self.put(index - 2).wait()

        span = self.stage.shape[2]
        columns = pl.ds(pl.multiple_of(index * span, span), span)
        rows = self.sequences * self.half
        for first in range(0, self.width, 768):
            own = slice(first, first + 768)
            value = dot(self.turned[own, :rows], self.pairs[0, :, columns], 1, 0)
            value = value + dot(self.turned[own, rows:], self.pairs[1, :, columns], 1, 0)
            self.stage[index % 2, own, :] = value.astype(LOW)
        self.put(index).start()


def mid_kernel(
    size, late, mixed, branch, cotangent, gains, gate_factor, up_factor, mid, weights,
    low, mixed_grad, gain, grads, *scratch
):
    at = lax.axis_index("fsdp")
    line_greet(at, size)
    part = scratch[0]
    line = LineExchange(
        at,
        size,
        line_span(part.shape[1]),
        part,
        low,
        lambda chunk, rows, total: mid_mid(
            chunk, rows, total, (mixed, branch, cotangent), gains, (mixed_grad, gain)
        ),
        scratch[1:8],
    )
    backward = Backward(late, mid, weights, gate_factor, up_factor, part, grads, scratch[8:])
    backward.fetch(0)

    def one(index, carried):
        backward.run(index)
        return carried

    lax.fori_loop(0, backward.count, one, 0)
    ahead = line.chunks // 2 - 1
    share = -(-backward.count // ahead)

    def both(index, carried):
        line.step(index)

        def more(inner, carried):
            tile = backward.count + index * share + inner

            @pl.when(tile < 2 * backward.count)
            def _():
                backward.run(tile)

            return carried

        lax.fori_loop(0, share, more, 0)
        return carried

    lax.fori_loop(0, ahead, both, 0)
    for copy in backward.fetch_mid():
        copy.start()
    line.run(ahead, ahead + 1)
    backward.turn()
    portion = -(-backward.sums // (line.steps - ahead - 1))

    def rest(index, carried):
        line.step(index)

        def more(inner, carried):
            tile = (index - ahead - 1) * portion + inner

            @pl.when(tile < backward.sums)
            def _():
                backward.sum(tile)

            return carried

        lax.fori_loop(0, portion, more, 0)
        return carried

    lax.fori_loop(ahead + 1, line.steps, rest, 0)
    line.drain()
    backward.put(backward.sums - 2).wait()
    backward.put(backward.sums - 1).wait()


def mid_exchange(
    late, mid, mixed, branch, cotangent, gains, gate_factor, up_factor, weights, collective_id
):
    fsdp, tokens, width = mid.shape
    units = weights.shape[2]
    span, reach, stage = tile_of(units), 384, 384 if fsdp <= 4 else 256
    rows = fsdp * tokens // 2
    dma = pltpu.SemaphoreType.DMA
    return pl.pallas_call(
        functools.partial(mid_kernel, fsdp),
        in_specs=[VMEM_SPEC] * 7 + [ANY_SPEC] * 2,
        out_specs=[VMEM_SPEC] * 3 + [ANY_SPEC],
        out_shape=[
            jax.ShapeDtypeStruct(mid.shape, LOW),
            jax.ShapeDtypeStruct((tokens, width), FULL),
            jax.ShapeDtypeStruct((2, width), FULL),
            jax.ShapeDtypeStruct((width, 2 * units), LOW),
        ],
        scratch_shapes=[pltpu.VMEM(mid.shape, LOW)]
        + line_scratch(fsdp, tokens, width, True)
        + [
            pltpu.VMEM((2, rows, width), LOW),
            pltpu.VMEM((width, 2 * rows), LOW),
            pltpu.VMEM((2, rows, 2 * units), LOW),
            pltpu.VMEM((2, width, span), LOW),
            pltpu.VMEM((2, 2, reach, units), LOW),
            pltpu.VMEM((2, width, stage), LOW),
            dma((2,)),
            dma((2,)),
            dma((2,)),
            dma((2 * fsdp,)),
        ],
        compiler_params=pltpu.CompilerParams(
            vmem_limit_bytes=VMEM_LIMIT, collective_id=collective_id
        ),
        name="mid_exchange",
    )(late, mixed, branch, cotangent, gains, gate_factor, up_factor, mid, weights)


def row_sum(values):
    return jnp.sum(values, 0, keepdims=True)


def add_gain(ref, chunk, index, values):
    @pl.when(chunk == 0)
    def _():
        ref[index : index + 1, :] = row_sum(values)

    @pl.when(chunk > 0)
    def _():
        ref[index : index + 1, :] += row_sum(values)


def branch_mid(chunk, rows, branch, ins, gains, outs):
    (x,), (branch_out, mixed_out) = ins, outs
    branch_out[rows, :] = branch
    post_hat = branch * rms_scale(branch)
    mixed = x[rows, :].astype(FULL) + post_hat * (1.0 + gains[1:2, :])
    mixed_out[rows, :] = mixed
    return (mixed * rms_scale(mixed) * (1.0 + gains[2:3, :])).astype(LOW)


def late_mid(chunk, rows, ffn_branch, ins, gains, outs):
    (mixed, cotangent), (out, gain) = ins, outs
    inv_late = rms_scale(ffn_branch)
    late_hat = ffn_branch * inv_late
    scale = 1.0 + gains[3:4, :]
    out[rows, :] = (mixed[rows, :] + late_hat * scale).astype(LOW)
    upstream = cotangent[rows, :].astype(FULL)
    add_gain(gain, chunk, 0, upstream * late_hat)
    scaled = upstream * scale
    grad = inv_late * (scaled - late_hat * jnp.mean(scaled * late_hat, -1, keepdims=True))
    return grad.astype(LOW)


def mid_mid(chunk, rows, mid_grad, ins, gains, outs):
    (mixed, branch, cotangent), (mixed_grad_out, gain) = ins, outs
    mixed = mixed[rows, :]
    inv_mid = rms_scale(mixed)
    mid_hat = mixed * inv_mid
    add_gain(gain, chunk, 1, mid_grad * mid_hat)
    scaled = mid_grad * (1.0 + gains[2:3, :])
    mixed_grad = cotangent[rows, :].astype(FULL) + inv_mid * (
        scaled - mid_hat * jnp.mean(scaled * mid_hat, -1, keepdims=True)
    )
    mixed_grad_out[rows, :] = mixed_grad
    branch = branch[rows, :]
    inv_post = rms_scale(branch)
    post_hat = branch * inv_post
    add_gain(gain, chunk, 0, mixed_grad * post_hat)
    hat = mixed_grad * (1.0 + gains[1:2, :])
    grad = inv_post * (hat - post_hat * jnp.mean(hat * post_hat, -1, keepdims=True))
    return grad.astype(LOW)


def pre_mid(chunk, rows, normed_grad, ins, gains, outs):
    (x, mixed_grad), (out, gain) = ins, outs
    x = x[rows, :].astype(FULL)
    inv_pre = rms_scale(x)
    normed = x * inv_pre
    add_gain(gain, chunk, 0, normed_grad * normed)
    scaled = normed_grad * (1.0 + gains[0:1, :])
    out[rows, :] = mixed_grad[rows, :] + inv_pre * (
        scaled - normed * jnp.mean(scaled * normed, -1, keepdims=True)
    )


def pair_sums_kernel(ctx, key, value, key_sum, value_sum, *scratch):
    at = lax.axis_index("ctx")
    greet(ctx_peers(at, ctx))
    keys = ctx_scatter(at, ctx, lambda c: key.at[:, c], scratch)
    values = ctx_scatter(at, ctx, lambda c: value.at[:, c], scratch[SCATTER:])
    keys.start()
    values.start()
    keys.diagonal()
    values.diagonal()
    keys.neighbours()
    values.neighbours()
    keys.passing()
    values.passing()
    for scatter, out in ((keys, key_sum), (values, value_sum)):

        def store(block, rows, total, out=out):
            out[block, rows, :] = total

        scatter.finish(store)
    keys.drain()
    values.drain()


def scatter_pairs(key, value):
    sequences, ctx, rows, width = key.shape
    return pl.pallas_call(
        functools.partial(pair_sums_kernel, ctx),
        in_specs=[VMEM_SPEC] * 2,
        out_specs=[VMEM_SPEC] * 2,
        out_shape=[jax.ShapeDtypeStruct((sequences, rows, width), FULL)] * 2,
        scratch_shapes=ctx_scatter_scratch(ctx, sequences, rows, width, LOW) * 2,
        compiler_params=pltpu.CompilerParams(vmem_limit_bytes=VMEM_LIMIT, collective_id=2),
        name="scatter_pairs",
    )(key, value)


def tail_kernel(
    ctx, fsdp, in_part, out_part, pre_part, x, mixed_grad, gains, in_old, out_old, after, *refs
):
    at, line_at = lax.axis_index("ctx"), lax.axis_index("fsdp")
    in_new, out_new, update, gram, input_grad, gain = refs[:6]
    scratch = refs[6:]
    places = head_places(fsdp)
    mine = len(places[0])
    scratch, others = scratch[: 2 * SCATTER], scratch[2 * SCATTER :]
    mine_sum, arrived, move_send, move_receive, out_sum = others[:5]
    head = arrived.shape[-1]
    greet(ctx_peers(at, ctx) + [("fsdp", (line_at + k) % fsdp) for k in range(1, fsdp)])
    ins = ctx_scatter(at, ctx, rows_of_ctx(in_part), scratch)
    outs = ctx_scatter(at, ctx, rows_of_ctx(out_part), scratch[SCATTER:])
    line = LineExchange(
        line_at,
        fsdp,
        line_span(pre_part.shape[1]),
        pre_part,
        None,
        lambda chunk, rows, total: pre_mid(
            chunk, rows, total, (x, mixed_grad), gains, (input_grad, gain)
        ),
        others[5:10],
    )
    ins.start()
    outs.start()
    ins.diagonal()
    ins.neighbours()
    line.run(0, 3)
    ins.passing()
    outs.diagonal()
    outs.neighbours()
    line.run(3, 6)
    outs.passing()
    line.run(6, 8)

    def store_in(block, rows, total):
        mine_sum[rows, :] = total.astype(LOW)

    def store_out(block, rows, total):
        out_sum[rows, :] = total

    ins.finish(store_in)

    def copies_of(owner, index):
        return [
            (user, slot)
            for user in range(fsdp)
            for slot in range(mine)
            if places[user][slot] == (owner, index)
        ]

    def move(user, slot):
        owner, index = places[user][slot]
        copy = copies_of(owner, index).index((user, slot))
        return remote(
            mine_sum.at[:, pl.ds(slot * head, head)],
            arrived.at[index, copy],
            move_send.at[slot],
            move_receive.at[index, copy],
            "fsdp",
            owner,
        )

    for user in range(fsdp):
        for slot in range(mine):

            @pl.when(line_at == user)
            def _(user=user, slot=slot):
                owner, index = places[user][slot]
                if owner == user:
                    copy = copies_of(owner, index).index((user, slot))
                    arrived[index, copy] = mine_sum[:, slot * head : (slot + 1) * head]
                else:
                    move(user, slot).start()

    line.run(8, line.steps)
    outs.finish(store_out)

    def step_of(index, grad, old_ref, new_ref, at):
        new = MOMENTUM_DECAY * old_ref[:, at, :] + grad
        new_ref[:, at, :] = new
        low = (grad + MOMENTUM_DECAY * new).astype(LOW)
        update[index] = low
        gram[index] = dot(low, low, 0, 0)

    stored = in_old.shape[1]
    for index in range(out_old.shape[1]):
        grad = out_sum[:, index * head : (index + 1) * head]
        step_of(stored + index, grad, out_old, out_new, index)
    for index in range(stored + out_old.shape[1], gram.shape[0]):
        gram[index] = jnp.zeros((head, head), FULL)
    for owner in range(fsdp):

        @pl.when(line_at == owner)
        def _(owner=owner):
            for index in range(stored):
                for user, slot in copies_of(owner, index):
                    if user != owner:
                        move(user, slot).wait_recv()

    for index in range(stored):
        grad = arrived[index, 0].astype(FULL)
        for copy in range(1, arrived.shape[1]):
            more = arrived[index, copy].astype(FULL)
            paired = line_at * stored + index >= QUERY_HEADS
            grad = grad + jnp.where(paired, more, 0.0)
        step_of(index, grad, in_old, in_new, index)
    for user in range(fsdp):
        for slot in range(mine):
            if places[user][slot][0] != user:

                @pl.when(line_at == user)
                def _(user=user, slot=slot):
                    move(user, slot).wait_send()

    ins.drain()
    outs.drain()
    line.drain()


def tail(in_part, out_part, pre_part, x, mixed_grad, gains, in_old, out_old, after):
    _, stored, head = in_old.shape
    matrices = stored + out_old.shape[1]
    ctx, rows, in_width = in_part.shape
    out_width = out_part.shape[2]
    fsdp, tokens, width = pre_part.shape
    mine = len(head_places(fsdp)[0])
    copies = max(1, fsdp // KEY_VALUE_HEADS)
    dma = pltpu.SemaphoreType.DMA
    return pl.pallas_call(
        functools.partial(tail_kernel, ctx, fsdp),
        in_specs=[VMEM_SPEC] * 8 + [ANY_SPEC],
        out_specs=[VMEM_SPEC] * 6,
        out_shape=[
            jax.ShapeDtypeStruct(in_old.shape, FULL),
            jax.ShapeDtypeStruct(out_old.shape, FULL),
            jax.ShapeDtypeStruct((matrices, rows, head), LOW),
            jax.ShapeDtypeStruct((ctx * (-(-matrices // ctx)), head, head), FULL),
            jax.ShapeDtypeStruct((tokens, width), FULL),
            jax.ShapeDtypeStruct((1, width), FULL),
        ],
        scratch_shapes=ctx_scatter_scratch(ctx, 1, rows, in_width, LOW)
        + ctx_scatter_scratch(ctx, 1, rows, out_width, LOW)
        + [
            pltpu.VMEM((rows, in_width), LOW),
            pltpu.VMEM((stored, copies, rows, head), LOW),
            dma((mine,)),
            dma((stored, copies)),
            pltpu.VMEM((rows, out_width), FULL),
        ]
        + line_scratch(fsdp, tokens, width, False),
        compiler_params=pltpu.CompilerParams(vmem_limit_bytes=VMEM_LIMIT, collective_id=3),
        name="tail",
    )(in_part, out_part, pre_part, x, mixed_grad, gains, in_old, out_old, after)


def packed_rows(small, large):
    squares = -(-small // 2)
    return squares * FBLK + large * 2 * FBLK + 16 * (-(-(squares + large) // 16))


def grid_of(size):
    rows = lax.broadcasted_iota(jnp.int32, (size, size), 0)
    return rows, lax.broadcasted_iota(jnp.int32, (size, size), 1)


def pack_two(first, second):
    rows, columns = grid_of(FBLK)
    if second is None:
        return first, jnp.zeros((1, FBLK), FULL)
    diagonal = jnp.sum(jnp.where(rows == columns, second, 0.0), 0, keepdims=True)
    return jnp.where(rows <= columns, first, second), diagonal


def unpack_two(square, diagonal, both):
    rows, columns = grid_of(FBLK)
    if not both:
        return square, None
    turned = square.T
    first = jnp.where(rows <= columns, square, turned)
    second = jnp.where(rows > columns, square, jnp.where(rows < columns, turned, diagonal))
    return first, second


def pack_all(blocks, heads, write):
    small, large = blocks[0], heads[0]
    squares = -(-small // 2)
    edge = squares * FBLK + large * 2 * FBLK
    for index in range(squares):
        second = blocks[1](2 * index + 1) if 2 * index + 1 < small else None
        square, diagonal = pack_two(blocks[1](2 * index), second)
        write(index * FBLK, square)
        write(edge + index, diagonal)
    for index in range(large):
        head = heads[1](index)
        square, diagonal = pack_two(head[:FBLK, :FBLK], head[FBLK:, FBLK:])
        base = squares * FBLK + index * 2 * FBLK
        write(base, square)
        write(base + FBLK, head[:FBLK, FBLK:])
        write(edge + squares + index, diagonal)


def unpack_all(small, large, read):
    squares = -(-small // 2)
    edge = squares * FBLK + large * 2 * FBLK
    blocks, heads = [], []
    for index in range(squares):
        both = 2 * index + 1 < small
        first, second = unpack_two(read(index * FBLK, FBLK), read(edge + index, 1), both)
        blocks += [first, second] if both else [first]
    for index in range(large):
        base = squares * FBLK + index * 2 * FBLK
        first, second = unpack_two(read(base, FBLK), read(edge + squares + index, 1), True)
        corner = read(base + FBLK, FBLK)
        heads.append(
            jnp.concatenate(
                [
                    jnp.concatenate([first, corner], 1),
                    jnp.concatenate([corner.T, second], 1),
                ],
                0,
            )
        )
    return blocks, heads


def newton_kernel(
    ctx, fsdp, head_rate, ffn_rate, heads, blocks, gains, head_update, in_old, out_old, ffn_update,
    ffn_old, in_new, out_new, ffn_new, gains_all, *scratch
):
    at, line_at = lax.axis_index("ctx"), lax.axis_index("fsdp")
    small, large = blocks.shape[1], heads.shape[1]
    packed, gram, poly, poly_all, gains_line, gains_sum, gain_send, gain_receive = scratch[:8]
    update, weights, update_sem, weight_sem, out_sem = scratch[8:13]
    scratch = scratch[13:]
    matrices, _, width = weights.shape
    per_matrix = width // FBLK
    count = matrices * per_matrix
    greet(ctx_peers(at, ctx) + [("fsdp", (line_at + k) % fsdp) for k in range(1, fsdp)])

    def gain_copy(k):
        return remote(
            gains,
            gains_line.at[k],
            gain_send.at[k],
            gain_receive.at[k],
            "fsdp",
            (line_at + k) % fsdp,
        )

    def fetches(matrix):
        return [
            pltpu.make_async_copy(
                ffn_update.at[matrix], update.at[matrix], update_sem.at[matrix]
            ),
            pltpu.make_async_copy(ffn_old.at[matrix], weights.at[matrix], weight_sem.at[matrix]),
        ]

    for k in range(1, fsdp):
        gain_copy(k).start()
    edge = packed_rows(small, large) - 16 * (-(-(-(-small // 2) + large) // 16))

    def pack_for(index, carried):
        packed[index, edge:, :] = jnp.zeros((packed.shape[1] - edge, FBLK), FULL)

        def write(first, rows):
            packed[index, first : first + rows.shape[0], :] = rows

        pack_all((small, lambda i: blocks[index, i]), (large, lambda i: heads[index, i]), write)
        return carried

    lax.fori_loop(0, ctx, pack_for, 0)
    scatter = ctx_scatter(at, ctx, rows_of_ctx(packed), scratch)
    scatter.start()
    for matrix in range(matrices):
        for copy in fetches(matrix):
            copy.start()
    scatter.diagonal()
    scatter.neighbours()
    scatter.passing()
    total = gains[...]
    for k in range(1, fsdp):
        gain_copy(k).wait_recv()
        total = total + gains_line[k]
    gains_sum[...] = total
    scratch = scratch[SCATTER:]
    gather_gains = CtxGather(at, ctx, gains_sum, lambda c: gains_all.at[c], 0, scratch[:5])
    gather = CtxGather(at, ctx, poly, lambda c: poly_all.at[c], 0, scratch[5:10])

    def store(block, rows, total):
        gram[rows, :] = total

    scatter.finish(store)
    gather_gains.start()
    block_grams, head_grams = unpack_all(
        small, large, lambda first, count: gram[first : first + count, :]
    )
    head_polys, block_polys = polys_of(head_grams), polys_of(block_grams)
    poly[edge:, :] = jnp.zeros((poly.shape[0] - edge, FBLK), FULL)

    def write(first, rows):
        poly[first : first + rows.shape[0], :] = rows

    pack_all((small, lambda i: block_polys[i]), (large, lambda i: head_polys[i]), write)
    gather.start()
    for matrix in range(matrices):
        for copy in fetches(matrix):
            copy.wait()

    def place(block):
        matrix = block // per_matrix
        columns = pl.ds(pl.multiple_of((block % per_matrix) * FBLK, FBLK), FBLK)
        return matrix, columns

    def put(block):
        matrix, columns = place(block)
        return pltpu.make_async_copy(
            weights.at[matrix, :, columns], ffn_new.at[matrix, :, columns], out_sem.at[block]
        )

    def apply(source, first):
        found, _ = unpack_all(small, 0, lambda row, count: source(row, count))
        for index, found_poly in enumerate(found):
            block = first * small + index

            @pl.when(block < count)
            def _(block=block, found_poly=found_poly):
                matrix, columns = place(block)
                step = moved(update[matrix, :, columns], found_poly)
                weights[matrix, :, columns] = weights[matrix, :, columns] * SHRINK - ffn_rate * step
                put(block).start()

    shift = large * 2 * FBLK

    def reader(view):
        edge_small = -(-small // 2) * FBLK

        def read(row, count):
            row = row + shift if row >= edge_small else row
            return view[row : row + count, :]

        return read

    apply(reader(poly), at)
    gather_gains.forward()
    gather.forward()
    gather_gains.rest()
    gather.rest()
    square = gather.square
    for j in range(square.column):
        for turn in (False, True):
            if j > 0 or turn:
                device = square.device(j, turn)
                apply(reader(poly_all.at[device]), device)
    for k in range(1, fsdp):
        gain_copy(k).wait_send()
    gather_gains.finish()
    gather.finish()
    for j in range(square.column):
        for turn in (False, True):
            device = square.device(j, turn, 1 - square.core)
            apply(reader(poly_all.at[device]), device)
    stored = in_old.shape[1]
    for device in range(ctx):
        first = device * large
        if first < head_update.shape[0]:
            _, found = unpack_all(
                small, large, lambda row, count: poly_all[device, row : row + count, :]
            )
            for index in range(first, min(first + large, head_update.shape[0])):
                step = head_rate * moved(head_update[index], found[index - first])
                if index < stored:
                    in_new[:, index, :] = in_old[:, index, :] * SHRINK - step
                else:
                    out_new[:, index - stored, :] = out_old[:, index - stored, :] * SHRINK - step
    scatter.drain()

    def finish(block, carried):
        put(block).wait()
        return carried

    lax.fori_loop(0, count, finish, 0)


def newton(
    heads, blocks, gains, head_update, in_old, out_old, ffn_update, ffn_old, head_rate, ffn_rate, fsdp
):
    ctx, large = heads.shape[:2]
    small = blocks.shape[1]
    rows = packed_rows(small, large)
    dma = pltpu.SemaphoreType.DMA
    matrices = ffn_old.shape[0]
    return pl.pallas_call(
        functools.partial(newton_kernel, ctx, fsdp, head_rate, ffn_rate),
        in_specs=[VMEM_SPEC] * 6 + [ANY_SPEC] * 2,
        out_specs=[VMEM_SPEC] * 2 + [ANY_SPEC, VMEM_SPEC],
        out_shape=[
            jax.ShapeDtypeStruct(in_old.shape, FULL),
            jax.ShapeDtypeStruct(out_old.shape, FULL),
            jax.ShapeDtypeStruct(ffn_old.shape, FULL),
            jax.ShapeDtypeStruct((ctx,) + gains.shape, FULL),
        ],
        scratch_shapes=[
            pltpu.VMEM((ctx, rows, FBLK), FULL),
            pltpu.VMEM((rows, FBLK), FULL),
            pltpu.VMEM((rows, FBLK), FULL),
            pltpu.VMEM((ctx, rows, FBLK), FULL),
            pltpu.VMEM((fsdp,) + gains.shape, FULL),
            pltpu.VMEM(gains.shape, FULL),
            dma((fsdp,)),
            dma((fsdp,)),
            pltpu.VMEM(ffn_update.shape, LOW),
            pltpu.VMEM(ffn_old.shape, FULL),
            dma((matrices,)),
            dma((matrices,)),
            dma((ctx * small,)),
        ]
        + ctx_scatter_scratch(ctx, 1, rows, FBLK, FULL)
        + ctx_gather_sems(ctx) * 2,
        compiler_params=pltpu.CompilerParams(vmem_limit_bytes=VMEM_LIMIT, collective_id=4),
        name="newton",
    )(heads, blocks, gains, head_update, in_old, out_old, ffn_update, ffn_old)


def local(
    inputs,
    cotangent,
    weights_in,
    weights_out,
    ffn_weights,
    norm_gains,
    momentum_in,
    momentum_out,
    ffn_momentum,
    gain_first,
    gain_second,
    stretch_order,
):
    sequences, rows, width = inputs.shape
    stretch_rows = rows // 2
    local_rows, in_local, head = weights_in.shape
    out_local = weights_out.shape[1]
    ffn_local = ffn_weights.shape[2]
    ctx, fsdp = lax.axis_size("ctx"), lax.axis_size("fsdp")
    ctx_at = lax.axis_index("ctx")
    tokens = sequences * rows
    all_sequences = sequences * fsdp
    heads = QUERY_HEADS // fsdp
    pairs = max(1, KEY_VALUE_HEADS // fsdp)
    shared = heads // pairs
    mine = heads + 2 * pairs

    ffn_mine = jnp.transpose(ffn_weights, (1, 0, 2))

    flat = inputs.reshape(tokens, width)
    mine_in, w_out, ffn_cut, own_normed = prepare(
        weights_in, weights_out, ffn_mine, flat, norm_gains, ctx, fsdp
    )
    ffn_low = lax.all_gather(ffn_cut, "ctx", axis=1, tiled=True)
    own_places = positions_of(
        ctx_at * rows + jnp.arange(rows, dtype=jnp.int32), stretch_order, stretch_rows
    )
    all_places = positions_of(
        jnp.arange(ctx * rows, dtype=jnp.int32), stretch_order, stretch_rows
    )
    cosine, sine = rope_tables(own_places, head)
    normed_low, w_in, query, key_all, value_all = project(
        own_normed,
        mine_in,
        jnp.tile(cosine, (sequences, 1)),
        jnp.tile(sine, (sequences, 1)),
        sequences,
        heads,
        pairs,
        ctx,
        fsdp,
    )
    normed_low = normed_low.reshape(fsdp * tokens, width)
    w_out = w_out.reshape(width, out_local * head)
    cosine, sine = jnp.tile(cosine, (all_sequences, 1)), jnp.tile(sine, (all_sequences, 1))
    scale = head ** (-0.5)

    def column(values, index):
        return values[:, index * head : (index + 1) * head]

    def by_sequence(columns):
        return jnp.concatenate([c.reshape(all_sequences, rows, head) for c in columns], 1)

    def flat_heads(values, count):
        return [
            values[:, g * rows : (g + 1) * rows].reshape(all_sequences * rows, head)
            for g in range(count)
        ]

    def heads_of(pair):
        return range(pair * shared, (pair + 1) * shared)

    query = [by_sequence([column(query, h) for h in heads_of(pair)]) for pair in range(pairs)]
    key_all = key_all.reshape(all_sequences, ctx * rows, pairs * head)
    value_all = value_all.reshape(all_sequences, ctx * rows, pairs * head)
    key_of = [key_all[:, :, p * head : (p + 1) * head] for p in range(pairs)]
    value_of = [value_all[:, :, p * head : (p + 1) * head] for p in range(pairs)]
    visible = jnp.tile(all_places[None, :] <= own_places[:, None], (shared, 1))[None]
    exponent, slope, exponent_low, row_total, attended = [], [], [], [], []
    for p in range(pairs):
        scores = batched(query[p], key_of[p], 2, 2)
        squashed = jnp.tanh(scores / SOFT_CAP)
        exponent.append(jnp.where(visible, jnp.exp(SOFT_CAP * squashed - EXP_SHIFT), 0.0))
        slope.append(exponent[p] * (1.0 - squashed * squashed))
        row_total.append(jnp.sum(exponent[p], -1, keepdims=True))
        exponent_low.append(exponent[p].astype(LOW))
        attended.append(batched(exponent_low[p], value_of[p], 2, 1) / row_total[p])
    attended_low = jnp.concatenate(
        sum([flat_heads(attended[p].astype(LOW), shared) for p in range(pairs)], []), 1
    )

    def parts(values):
        return values.astype(LOW).reshape(fsdp, tokens, width)

    full_rows = jax.ShapeDtypeStruct((tokens, width), FULL)
    low_rows = jax.ShapeDtypeStruct((tokens, width), LOW)

    def gain_rows(count):
        return jax.ShapeDtypeStruct((count, width), FULL)

    upstream = cotangent.reshape(tokens, width)
    mid_low, branch, mixed = exchange(
        parts(dot(attended_low, w_out, 1, 1)),
        [flat],
        norm_gains,
        branch_mid,
        [full_rows, full_rows],
        fsdp,
        5,
        "branch_exchange",
    )

    late_low, outputs, gain_late, hidden_low, gate_factor, up_factor = late_exchange(
        mid_low, ffn_low, mixed, upstream, norm_gains, 6
    )
    down_grads = lax.psum_scatter(
        dot(
            late_low.reshape(fsdp * tokens, width),
            hidden_low.reshape(fsdp * tokens, ffn_local),
            0,
            0,
        ).astype(LOW),
        "ctx",
        scatter_dimension=0,
        tiled=True,
    )
    branch_low, mixed_grad, gain_middle, pair_part = mid_exchange(
        late_low, mid_low, mixed, branch, upstream, norm_gains, gate_factor, up_factor, ffn_low, 7
    )
    pair_grads = lax.psum_scatter(pair_part, "ctx", scatter_dimension=0, tiled=True)

    branch_low = branch_low.reshape(fsdp * tokens, width)
    attended_grad = dot(branch_low, w_out, 1, 0)
    query_grad, key_part, value_part = [], [], []
    for p in range(pairs):
        grad = by_sequence([column(attended_grad, h) for h in heads_of(p)])
        numerator_low = (grad / row_total[p]).astype(LOW)
        row_term = jnp.sum(grad * attended[p], -1, keepdims=True) / row_total[p]
        pulled = batched(numerator_low, value_of[p], 2, 2)
        score_low = (slope[p] * (pulled - row_term)).astype(LOW)
        query_grad += flat_heads(batched(score_low, key_of[p], 2, 1), shared)
        key_part.append(batched(score_low, query[p], 1, 1).astype(LOW))
        value_part.append(batched(exponent_low[p], numerator_low, 1, 1).astype(LOW))
    spread = (all_sequences, ctx, rows, pairs * head)
    key_grad, value_grad = scatter_pairs(
        jnp.concatenate(key_part, 2).reshape(spread), jnp.concatenate(value_part, 2).reshape(spread)
    )
    key_grad = key_grad.reshape(all_sequences * rows, pairs * head)
    value_grad = value_grad.reshape(all_sequences * rows, pairs * head)
    projected_grad = jnp.concatenate(
        [rotate(grad * scale, cosine, -sine) for grad in query_grad]
        + [rotate(column(key_grad, p), cosine, -sine) for p in range(pairs)]
        + [value_grad],
        1,
    ).astype(LOW)
    momentum = jnp.transpose(ffn_momentum, (1, 0, 2))
    small = -(-3 * (ffn_local // FBLK) // ctx)
    earlier = ffn_gram(down_grads, momentum, 2, ctx * small, [])
    momentum_new_in, momentum_new_out, head_update, head_gram, input_grad, gain_pre = tail(
        dot(normed_low, projected_grad, 0, 0).astype(LOW).reshape(ctx, local_rows, mine * head),
        dot(branch_low, attended_low, 0, 0).astype(LOW).reshape(ctx, local_rows, out_local * head),
        parts(dot(projected_grad, w_in, 1, 1)),
        flat,
        mixed_grad,
        norm_gains,
        momentum_in,
        momentum_out,
        earlier[2][-1, :8],
    )
    input_grad = input_grad.reshape(inputs.shape)
    outputs = outputs.reshape(inputs.shape)
    gain_parts = jnp.concatenate([gain_pre, gain_middle, gain_late], 0)

    new_ffn, ffn_update, block_gram = ffn_gram(pair_grads, momentum, 0, ctx * small, earlier)
    new_weights_in, new_weights_out, new_ffn_weights, gain_every = newton(
        head_gram.reshape(ctx, -1, head, head),
        block_gram.reshape(ctx, small, FBLK, FBLK),
        gain_parts,
        head_update,
        weights_in,
        weights_out,
        ffn_update,
        ffn_mine,
        LEARN_RATE * (width / head) ** 0.5,
        LEARN_RATE * (width / FBLK) ** 0.5,
        fsdp,
    )
    gain_grad = jnp.sum(gain_every, 0)
    new_gain_first = BETA_ONE * gain_first + (1.0 - BETA_ONE) * gain_grad
    new_gain_second = BETA_TWO * gain_second + (1.0 - BETA_TWO) * gain_grad * gain_grad
    corrected_one = new_gain_first / (1.0 - BETA_ONE**STEP)
    corrected_two = new_gain_second / (1.0 - BETA_TWO**STEP)
    new_norm_gains = norm_gains - GAIN_RATE * corrected_one / (jnp.sqrt(corrected_two) + ADAM_EPS)
    return (
        outputs,
        input_grad,
        new_weights_in,
        new_weights_out,
        jnp.transpose(new_ffn_weights, (1, 0, 2)),
        momentum_new_in,
        momentum_new_out,
        jnp.transpose(new_ffn, (1, 0, 2)),
        new_norm_gains,
        new_gain_first,
        new_gain_second,
    )


def solution(mesh):
    return jax.shard_map(
        local,
        mesh=mesh,
        in_specs=(
            P("fsdp", "ctx", None),
            P("fsdp", "ctx", None),
            P("ctx", "fsdp", None),
            P("ctx", "fsdp", None),
            P("ctx", None, "fsdp"),
            P(),
            P("ctx", "fsdp", None),
            P("ctx", "fsdp", None),
            P("ctx", None, "fsdp"),
            P(),
            P(),
            P(),
        ),
        out_specs=(
            P("fsdp", "ctx", None),
            P("fsdp", "ctx", None),
            P("ctx", "fsdp", None),
            P("ctx", "fsdp", None),
            P("ctx", None, "fsdp"),
            P("ctx", "fsdp", None),
            P("ctx", "fsdp", None),
            P("ctx", None, "fsdp"),
            P(),
            P(),
            P(),
        ),
        check_vma=False,
    )
```

```python
import functools

import jax
import jax.numpy as jnp
from jax import lax
from jax.experimental import pallas as pl
from jax.experimental.pallas import tpu as pltpu
from jax.sharding import PartitionSpec as P

QUERY_HEADS = 8
KEY_VALUE_HEADS = 4
FBLK = 128
ITERS = 5
STEP = 10

SOFT_CAP = 50.0
EXP_SHIFT = 20.0
NORM_EPS = 1e-06
ROPE_THETA = 10000.0
MOMENTUM_DECAY = 0.95
LEARN_RATE = 0.3
WEIGHT_DECAY = 0.01
BETA_ONE = 0.9
BETA_TWO = 0.95
GAIN_RATE = 0.3
ADAM_EPS = 1e-08
NEWTON_A = 3.4445
NEWTON_B = -4.775
NEWTON_C = 2.0315
GELU_SCALE = 0.7978845608028654
GELU_CUBE = 0.044715
LOW = jnp.bfloat16
FULL = jnp.float32
SHRINK = 1.0 - LEARN_RATE * WEIGHT_DECAY
VMEM_LIMIT = 60 * 1024 * 1024


def rms_scale(values):
    return lax.rsqrt(jnp.mean(values * values, -1, keepdims=True) + NORM_EPS)


def positions_of(row_index, stretch_order, stretch_rows):
    stretch_slot = row_index // stretch_rows
    slot_table = jnp.arange(stretch_order.shape[0], dtype=jnp.int32)
    picked = jnp.sum(
        jnp.where(stretch_slot[:, None] == slot_table[None, :], stretch_order[None, :], 0), axis=1
    )
    return picked * stretch_rows + row_index % stretch_rows


def rope_tables(places, width):
    half_width = width // 2
    frequency = ROPE_THETA ** (-(2.0 * jnp.arange(half_width, dtype=jnp.float32)) / width)
    angles = places.astype(jnp.float32)[:, None] * frequency[None, :]
    return (jnp.cos(angles), jnp.sin(angles))


def rotate(values, cosine, sine):
    half = values.shape[-1] // 2
    first, second = values[..., :half], values[..., half:]
    return jnp.concatenate([first * cosine - second * sine, second * cosine + first * sine], -1)


def batched(left, right, left_dim, right_dim):
    return lax.dot_general(
        left, right, (((left_dim,), (right_dim,)), ((0,), (0,))), preferred_element_type=FULL
    )


def dot(left, right, left_dim, right_dim):
    return lax.dot_general(
        left, right, (((left_dim,), (right_dim,)), ((), ())), preferred_element_type=FULL
    )


def gram_kernel(blocks, grad_ref, old_ref, *refs):
    new_ref, update_ref, gram_ref = refs[-3:]
    grad = grad_ref[...].astype(FULL)
    new = MOMENTUM_DECAY * old_ref[0] + grad
    new_ref[0] = new
    update = (grad + MOMENTUM_DECAY * new).astype(LOW)
    update_ref[0] = update
    for block in range(blocks):
        piece = update[:, block * FBLK : (block + 1) * FBLK]
        gram_ref[block] = dot(piece, piece, 0, 0)


def ffn_gram(grads, momentum, first, blocks, earlier):
    _, rows, width = momentum.shape
    per_step = 6 if (width // FBLK) % 6 == 0 else 3
    span = per_step * FBLK
    steps = width // span
    spec = pl.BlockSpec((1, rows, span), lambda m, b: (m + first, 0, b))
    return pl.pallas_call(
        functools.partial(gram_kernel, per_step),
        grid=(grads.shape[1] // width, steps),
        in_specs=[pl.BlockSpec((rows, span), lambda m, b: (0, m * steps + b)), spec]
        + [ANY_SPEC] * len(earlier),
        out_specs=[
            spec,
            spec,
            pl.BlockSpec((per_step, FBLK, FBLK), lambda m, b: ((m + first) * steps + b, 0, 0)),
        ],
        out_shape=[
            jax.ShapeDtypeStruct(momentum.shape, FULL),
            jax.ShapeDtypeStruct(momentum.shape, LOW),
            jax.ShapeDtypeStruct((blocks, FBLK, FBLK), FULL),
        ],
        input_output_aliases={2 + index: index for index in range(len(earlier))},
        compiler_params=pltpu.CompilerParams(vmem_limit_bytes=VMEM_LIMIT),
        name="ffn_gram",
    )(grads, momentum, *earlier)


def split(values):
    high = values.astype(LOW)
    return high, (values - high.astype(FULL)).astype(LOW)


def fine_dot(left, right):
    (high, low), (right_high, right_low) = left, right
    return jnp.dot(
        jnp.concatenate([high, high, low], 1),
        jnp.concatenate([right_high, right_low, right_high], 0),
        preferred_element_type=FULL,
    )


def polys_of(grams):
    eyes = {}
    for gram in grams:
        rows, columns = grid_of(gram.shape[0])
        eyes[gram.shape[0]] = (rows == columns).astype(FULL)
    factors, totals = [], [None] * len(grams)
    for index, gram in enumerate(grams):
        eye = eyes[gram.shape[0]]
        trace = jnp.sum(jnp.sum(gram * eye, 0, keepdims=True), 1, keepdims=True)
        factors.append(1.0 / (jnp.sqrt(trace) + 1e-07))
        grams[index] = gram * (factors[index] * factors[index])
    for step in range(ITERS):
        parts = [split(gram) for gram in grams]
        squares = [fine_dot(part, part) for part in parts]
        quads = [
            NEWTON_A * eyes[gram.shape[0]] + NEWTON_B * gram + NEWTON_C * square
            for gram, square in zip(grams, squares)
        ]
        quad_parts = [split(quad) for quad in quads]
        totals = [
            quad if total is None else fine_dot(split(total), part)
            for total, quad, part in zip(totals, quads, quad_parts)
        ]
        if step < ITERS - 1:
            halves = [fine_dot(quad, part) for quad, part in zip(quad_parts, parts)]
            grams = [fine_dot(split(half), quad) for half, quad in zip(halves, quad_parts)]
    return [total * factor for total, factor in zip(totals, factors)]


def moved(update, poly):
    high, low = split(poly)
    return jnp.dot(
        jnp.concatenate([update, update], 1),
        jnp.concatenate([high, low], 0),
        preferred_element_type=FULL,
    )


def tile_of(size):
    return 768 if size % 768 == 0 else 384


def remote(source, target, send, receive, axis, to):
    return pltpu.make_async_remote_copy(
        src_ref=source,
        dst_ref=target,
        send_sem=send,
        recv_sem=receive,
        device_id={axis: to},
        device_id_type=pl.DeviceIdType.MESH,
    )


def greet(peers):
    barrier = pltpu.get_barrier_semaphore()
    for axis, to in peers:
        pl.semaphore_signal(
            barrier, inc=1, device_id={axis: to}, device_id_type=pl.DeviceIdType.MESH
        )
    pl.semaphore_wait(barrier, len(peers))


def line_greet(at, size):
    barrier = pltpu.get_barrier_semaphore()
    for ok, to in ((at > 0, at - 1), (at < size - 1, at + 1)):

        @pl.when(ok)
        def _(to=to):
            pl.semaphore_signal(
                barrier, inc=1, device_id={"fsdp": to}, device_id_type=pl.DeviceIdType.MESH
            )

    inside = (at > 0) & (at < size - 1)
    for ok, peers in ((inside, 2), (jnp.logical_not(inside), 1)):

        @pl.when(ok)
        def _(peers=peers):
            pl.semaphore_wait(barrier, peers)


class LineGather:
    def __init__(self, at, size, span, out, send, receive):
        self.at, self.size, self.span = at, size, span
        self.out, self.send_sem, self.receive_sem = out, send, receive

    def piece(self, owner, chunk):
        return self.out.at[owner, pl.ds(pl.multiple_of(chunk * self.span, self.span), self.span)]

    def copy(self, owner, chunk, side):
        piece = self.piece(owner, chunk)
        to = (self.at + (1 if side == 0 else self.size - 1)) % self.size
        return remote(
            piece,
            piece,
            self.send_sem.at[side, owner, chunk],
            self.receive_sem.at[owner, chunk],
            "fsdp",
            to,
        )

    def start(self, chunk):
        @pl.when(self.at < self.size - 1)
        def _():
            self.copy(self.at, chunk, 0).start()

        @pl.when(self.at > 0)
        def _():
            self.copy(self.at, chunk, 1).start()

    def forward(self, chunk, gap):
        at, size = self.at, self.size

        @pl.when(at >= gap)
        def _(owner=at - gap):
            copy = self.copy(owner, chunk, 0)
            copy.wait_recv()

            @pl.when(at < size - 1)
            def _():
                copy.start()

        @pl.when(at + gap < size)
        def _(owner=at + gap):
            copy = self.copy(owner, chunk, 1)
            copy.wait_recv()

            @pl.when(at > 0)
            def _():
                copy.start()

    def drain(self, chunk):
        at, size = self.at, self.size
        for gap in range(size):

            @pl.when((at >= gap) & (at < size - 1))
            def _(owner=at - gap):
                self.copy(owner, chunk, 0).wait_send()

            @pl.when((at + gap < size) & (at > 0))
            def _(owner=at + gap):
                self.copy(owner, chunk, 1).wait_send()


def cut_of(rows):
    return 16 * (-(-rows // 32)) if rows >= 32 else rows


class Square:
    def __init__(self, at, size):
        self.at, self.column = at, size // 4
        self.core, self.x, self.y = at % 2, (at // 2) % 2, at // 4
        self.sibling = at + 1 - 2 * self.core

    def device(self, j, turn, core=None):
        x = 1 - self.x if turn else self.x
        core = self.core if core is None else core
        return (((self.y + j) % self.column) * 2 + x) * 2 + core

    def others(self):
        return range(1, self.column)

    def back(self, j):
        return (self.column - j) % self.column


def ctx_peers(at, size):
    square = Square(at, size)
    peers = [square.sibling, square.device(0, True)]
    return [("ctx", to) for to in peers + [square.device(j, False) for j in square.others()]]


class CtxGather:
    def __init__(self, at, size, source, slot, axis, sems):
        self.square = Square(at, size)
        self.source, self.slot, self.axis = source, slot, axis
        self.send, self.receive, self.pass_send, self.pass_receive, self.own = sems
        rows = source.shape[axis]
        cut = cut_of(rows)
        self.halves = (0, 1) if cut < rows else (0,)
        self.bounds = ((0, cut), (cut, rows - cut))

    def half(self, view, h):
        first, count = self.bounds[h]
        return view.at[(slice(None),) * self.axis + (pl.ds(first, count),)]

    def block(self, j, turn, h, core=None):
        return self.half(self.slot(self.square.device(j, turn, core)), h)

    def copy(self, source, target, h, send, j, turn, to):
        return remote(
            source,
            target,
            self.send.at[h, send],
            self.receive.at[h, j, int(turn)],
            "ctx",
            to,
        )

    def direct(self, h, j):
        square = self.square
        return self.copy(
            self.half(self.source, h),
            self.half(self.slot(square.at), h),
            h,
            j,
            square.back(j),
            j == 0,
            square.device(j, j == 0),
        )

    def onward(self, h, j):
        square = self.square
        block = self.block(0, True, 0) if h == 0 else self.block(j, False, 1)
        to = square.device(j, False) if h == 0 else square.device(0, True)
        origin = square.back(j) if h == 0 else j
        return self.copy(block, block, h, square.column + j, origin, True, to)

    def arrival(self, h, j, turn):
        block = self.block(j, turn, h)
        return remote(
            block, block, self.send.at[h, 0], self.receive.at[h, j, int(turn)], "ctx", self.square.sibling
        )

    def across(self, h, j, turn):
        block = self.block(j, turn, h)
        sems = (self.pass_send.at[h, j, int(turn)], self.pass_receive.at[h, j, int(turn)])
        return remote(block, block, *sems, "ctx", self.square.sibling)

    def crossed(self, h, j, turn):
        block = self.block(j, turn, h, 1 - self.square.core)
        sems = (self.pass_send.at[h, j, int(turn)], self.pass_receive.at[h, j, int(turn)])
        return remote(block, block, *sems, "ctx", self.square.sibling)

    def mine(self, h):
        sems = (self.pass_send.at[h, 0, 0], self.pass_receive.at[h, 0, 0])
        target = self.half(self.slot(self.square.at), h)
        return remote(self.half(self.source, h), target, *sems, "ctx", self.square.sibling)

    def keep(self):
        return pltpu.make_async_copy(self.source, self.slot(self.square.at), self.own)

    def start(self):
        others, halves = self.square.others(), self.halves
        self.direct(0, 0).start()
        for j in others:
            self.direct(halves[-1], j).start()
        if len(halves) > 1:
            self.direct(1, 0).start()
            for j in others:
                self.direct(0, j).start()
        for h in halves:
            self.mine(h).start()
        self.keep().start()

    def land(self, h, j, turn):
        self.arrival(h, j, turn).wait_recv()
        self.across(h, j, turn).start()

    def forward(self):
        others, halves = self.square.others(), self.halves
        self.land(0, 0, True)
        for j in others:
            self.onward(0, j).start()
        if len(halves) > 1:
            for j in others:
                self.land(1, j, False)
                self.onward(1, j).start()

    def rest(self):
        others, halves = self.square.others(), self.halves
        if len(halves) > 1:
            self.land(1, 0, True)
        for j in others:
            self.land(0, j, False)
        for j in others:
            for h in halves:
                self.land(h, j, True)

    def finish(self):
        square, halves = self.square, self.halves
        for h in halves:
            for j in range(square.column):
                self.direct(h, j).wait_send()
                if j > 0:
                    self.onward(h, j).wait_send()
                for turn in (False, True):
                    self.crossed(h, j, turn).wait_recv()
                    if j > 0 or turn:
                        self.across(h, j, turn).wait_send()
            self.mine(h).wait_send()
        self.keep().wait()


def ctx_gather_sems(size):
    column = size // 4
    dma = pltpu.SemaphoreType.DMA
    return [dma((2, 2 * column)), dma((2, column, 2)), dma((2, column, 2)), dma((2, column, 2)), dma]


class CtxScatter:
    def __init__(self, at, size, part, first, hold, along_x, along_y, landed, sems):
        self.square = Square(at, size)
        self.part, self.first, self.hold = part, first, hold
        self.along_x, self.along_y, self.landed = along_x, along_y, landed
        self.near_send, self.near_receive, self.send, self.receive = sems
        self.step = 16 if first.dtype == LOW else 8
        rows = hold.shape[2]
        cut = cut_of(rows)
        self.bounds = ((0, cut), (cut, rows - cut))

    def index(self, j, turn):
        return j * 2 + int(turn)

    def near(self, j, turn):
        index = self.index(j, turn)
        return remote(
            self.part(self.square.device(j, turn, 1 - self.square.core)),
            self.first.at[index],
            self.near_send.at[index],
            self.near_receive.at[index],
            "ctx",
            self.square.sibling,
        )

    def half(self, view, h):
        return view.at[:, pl.ds(*self.bounds[h])]

    def far(self, kind, j):
        square, h = self.square, kind % 2
        if kind < 2:
            source = self.half(self.hold.at[self.index(j, True)], h)
            target = self.along_x.at[j - 1] if kind == 0 else self.along_y.at[square.back(j) - 1]
        elif kind < 4:
            source = self.half(self.hold.at[self.index(0, True)], h)
            target = self.half(self.landed.at[0], h)
        else:
            source = self.half(self.hold.at[self.index(j, False)], h)
            target = self.half(self.landed.at[square.back(j)], h)
        along_x = kind in (0, 2, 3)
        to = square.device(0, True) if along_x else square.device(j, False)
        return remote(
            source,
            target,
            self.send.at[kind, j],
            self.receive.at[kind, j if along_x else square.back(j)],
            "ctx",
            to,
        )

    def arrival(self, kind, j):
        h = kind % 2
        if kind < 2:
            block = (self.along_x if kind == 0 else self.along_y).at[j - 1]
        else:
            block = self.half(self.landed.at[0 if kind < 4 else j], h)
        return remote(
            block, block, self.send.at[kind, j], self.receive.at[kind, j], "ctx", self.square.sibling
        )

    def rows(self, first, count, body):
        def one(index, carried):
            offset = pl.multiple_of(index * self.step, self.step)
            for block in range(self.hold.shape[1]):
                body(block, offset)
            return carried

        lax.fori_loop(first // self.step, (first + count) // self.step, one, 0)

    def pair(self, j, turn):
        self.near(j, turn).wait_recv()
        index = self.index(j, turn)
        part = self.part(self.square.device(j, turn))

        def add(block, offset):
            rows = pl.ds(offset, self.step)
            total = part[block, rows, :].astype(FULL)
            total = total + self.first[index, block, rows, :].astype(FULL)
            self.hold[index, block, rows, :] = total.astype(self.hold.dtype)

        self.rows(0, self.hold.shape[2], add)

    def start(self):
        others = self.square.others()
        for j in others:
            self.near(j, True).start()
        self.near(0, True).start()
        for j in others:
            self.near(j, False).start()
        self.near(0, False).start()

    def diagonal(self):
        for j in self.square.others():
            self.pair(j, True)
            self.far(0, j).start()
            self.far(1, j).start()

    def neighbours(self):
        self.pair(0, True)
        self.far(2, 0).start()
        for j in self.square.others():
            self.pair(j, False)
            self.far(5, j).start()

    def add_passing(self, index, h, block_of):
        first, count = self.bounds[h]

        def add(block, offset):
            rows = pl.ds(offset, self.step)
            local = pl.ds(pl.multiple_of(offset - first, self.step), self.step)
            total = self.hold[index, block, rows, :].astype(FULL)
            for passing in block_of:
                total = total + passing[block, local, :].astype(FULL)
            self.hold[index, block, rows, :] = total.astype(self.hold.dtype)

        self.rows(first, count, add)

    def passing(self):
        others = self.square.others()
        for j in others:
            self.arrival(0, j).wait_recv()
            self.add_passing(self.index(j, False), 0, [self.along_x.at[j - 1]])
            self.far(4, j).start()
        for j in others:
            self.arrival(1, j).wait_recv()
        self.add_passing(self.index(0, True), 1, [self.along_y.at[j - 1] for j in others])
        self.far(3, 0).start()

    def finish(self, store):
        others = self.square.others()
        self.near(0, False).wait_recv()
        for kind in (2, 3):
            self.arrival(kind, 0).wait_recv()
        for j in others:
            for kind in (5, 4):
                self.arrival(kind, j).wait_recv()
        part = self.part(self.square.at)

        def add(block, offset):
            rows = pl.ds(offset, self.step)
            total = part[block, rows, :].astype(FULL) + self.first[0, block, rows, :].astype(FULL)
            for index in range(self.landed.shape[0]):
                total = total + self.landed[index, block, rows, :].astype(FULL)
            store(block, rows, total)

        self.rows(0, self.hold.shape[2], add)

    def drain(self):
        for j in range(self.square.column):
            for turn in (False, True):
                self.near(j, turn).wait_send()
        for kind in (2, 3):
            self.far(kind, 0).wait_send()
        for j in self.square.others():
            for kind in (0, 1, 4, 5):
                self.far(kind, j).wait_send()


SCATTER = 9


def ctx_scatter_scratch(size, blocks, rows, width, kind):
    chips, column = size // 2, size // 4
    cut = cut_of(rows)
    dma = pltpu.SemaphoreType.DMA
    return [
        pltpu.VMEM((chips, blocks, rows, width), kind),
        pltpu.VMEM((chips, blocks, rows, width), kind),
        pltpu.VMEM((column - 1, blocks, cut, width), kind),
        pltpu.VMEM((column - 1, blocks, rows - cut, width), kind),
        pltpu.VMEM((column, blocks, rows, width), kind),
        dma((chips,)),
        dma((chips,)),
        dma((6, column)),
        dma((6, column)),
    ]


def ctx_scatter(at, size, part, scratch):
    return CtxScatter(at, size, part, *scratch[:5], scratch[5:9])


def rows_of_ctx(ref):
    return lambda c: ref.at[pl.ds(c, 1)]


VMEM_SPEC = pl.BlockSpec(memory_space=pltpu.VMEM)
ANY_SPEC = pl.BlockSpec(memory_space=pl.ANY)


def head_places(fsdp):
    heads = QUERY_HEADS // fsdp
    pairs = max(1, KEY_VALUE_HEADS // fsdp)
    stored = (QUERY_HEADS + 2 * KEY_VALUE_HEADS) // fsdp
    places = []
    for user in range(fsdp):
        first = (user * heads) // (QUERY_HEADS // KEY_VALUE_HEADS)
        used = [user * heads + h for h in range(heads)]
        used += [QUERY_HEADS + first + p for p in range(pairs)]
        used += [QUERY_HEADS + KEY_VALUE_HEADS + first + p for p in range(pairs)]
        places.append([(matrix // stored, matrix % stored) for matrix in used])
    return places


def prepare_kernel(
    ctx, fsdp, in_ref, out_ref, ffn_ref, x_ref, gains, mine, out_all, ffn_low, normed, *scratch
):
    at, line_at = lax.axis_index("ctx"), lax.axis_index("fsdp")
    in_low, out_low, wide, wide_sem, move_send, move_receive = scratch[:6]
    places = head_places(fsdp)
    head = in_ref.shape[2]
    greet(ctx_peers(at, ctx) + [("fsdp", (line_at + k) % fsdp) for k in range(1, fsdp)])

    def move(user, slot):
        owner, index = places[user][slot]
        return remote(
            in_low.at[index],
            mine.at[:, pl.ds(slot * head, head)],
            move_send.at[user, slot],
            move_receive.at[slot],
            "fsdp",
            user,
        )

    def load(matrix):
        return pltpu.make_async_copy(
            ffn_ref.at[matrix], wide.at[matrix % 2], wide_sem.at[matrix % 2]
        )

    load(0).start()
    for index in range(in_ref.shape[1]):
        in_low[index] = in_ref[:, index, :].astype(LOW)
    for user in range(fsdp):
        for slot in range(len(places[0])):
            owner, index = places[user][slot]

            @pl.when(line_at == owner)
            def _(user=user, slot=slot, owner=owner, index=index):
                if user == owner:
                    mine[:, slot * head : (slot + 1) * head] = in_low[index]
                else:
                    move(user, slot).start()

    for index in range(out_ref.shape[1]):
        out_low[:, index * head : (index + 1) * head] = out_ref[:, index, :].astype(LOW)
    gather = CtxGather(at, ctx, out_low, lambda c: out_all.at[c], 0, scratch[6:11])
    gather.start()
    x = x_ref[...].astype(FULL)
    normed[...] = (x * rms_scale(x) * (1.0 + gains[0:1, :])).astype(LOW)
    for matrix in range(3):
        load(matrix).wait()
        if matrix < 2:
            load(matrix + 1).start()
        ffn_low[matrix] = wide[matrix % 2].astype(LOW)
    gather.forward()
    gather.rest()
    for user in range(fsdp):

        @pl.when(line_at == user)
        def _(user=user):
            for slot in range(len(places[0])):
                if places[user][slot][0] != user:
                    move(user, slot).wait_recv()

        for slot in range(len(places[0])):
            owner, index = places[user][slot]
            if user != owner:

                @pl.when(line_at == owner)
                def _(user=user, slot=slot):
                    move(user, slot).wait_send()

    gather.finish()


def prepare(weights_in, weights_out, ffn, x, gains, ctx, fsdp):
    local_rows, in_local, head = weights_in.shape
    out_local = weights_out.shape[1]
    mine = len(head_places(fsdp)[0])
    dma = pltpu.SemaphoreType.DMA
    return pl.pallas_call(
        functools.partial(prepare_kernel, ctx, fsdp),
        in_specs=[VMEM_SPEC] * 2 + [ANY_SPEC] + [VMEM_SPEC] * 2,
        out_specs=[VMEM_SPEC, ANY_SPEC, VMEM_SPEC, VMEM_SPEC],
        out_shape=[
            jax.ShapeDtypeStruct((local_rows, mine * head), LOW),
            jax.ShapeDtypeStruct((ctx, local_rows, out_local * head), LOW),
            jax.ShapeDtypeStruct(ffn.shape, LOW),
            jax.ShapeDtypeStruct(x.shape, LOW),
        ],
        scratch_shapes=[
            pltpu.VMEM((in_local, local_rows, head), LOW),
            pltpu.VMEM((local_rows, out_local * head), LOW),
            pltpu.VMEM((2,) + ffn.shape[1:], FULL),
            dma((2,)),
            dma((fsdp, mine)),
            dma((mine,)),
        ]
        + ctx_gather_sems(ctx),
        compiler_params=pltpu.CompilerParams(vmem_limit_bytes=VMEM_LIMIT, collective_id=0),
        name="prepare",
    )(weights_in, weights_out, ffn, x, gains)


def project_kernel(
    ctx, fsdp, span, heads, own, mine, cosine, sine, normed, in_all, query, key_all, value_all, *scratch
):
    at, line_at = lax.axis_index("ctx"), lax.axis_index("fsdp")
    key, value, low_send, low_receive = scratch[:4]
    tokens = own.shape[0]
    rows = key.shape[1]
    local_rows = mine.shape[0]
    head = 2 * cosine.shape[1]
    pairs = key.shape[2] // head
    chunks = tokens // span
    greet(ctx_peers(at, ctx) + [("fsdp", (line_at + k) % fsdp) for k in range(1, fsdp)])
    line = LineGather(line_at, fsdp, span, normed, low_send, low_receive)
    normed[line_at] = own[...]
    for chunk in range(chunks):
        line.start(chunk)
    step = 16

    def slot(c):
        return in_all.at[pl.ds(pl.multiple_of(c * local_rows, step), local_rows)]

    gather_in = CtxGather(at, ctx, mine, slot, 0, scratch[4:9])
    gather_in.start()
    for chunk in range(chunks):
        line.forward(chunk, 1)
    gather_in.forward()
    for gap in range(2, fsdp):
        for chunk in range(chunks):
            line.forward(chunk, gap)
    gather_in.rest()
    gather_in.finish()

    def projected(index, write, turn, scale):
        weights = in_all[:, index * head : (index + 1) * head]
        for sequence in range(fsdp):
            result = dot(normed[sequence], weights, 1, 0)
            if turn:
                first, second = result[:, : head // 2], result[:, head // 2 :]
                result = jnp.concatenate(
                    [
                        first * cosine[...] - second * sine[...],
                        second * cosine[...] + first * sine[...],
                    ],
                    1,
                )
            write(sequence, (result * scale).astype(LOW))

    per_device = tokens // rows
    for pair in range(pairs):
        columns = slice(pair * head, (pair + 1) * head)
        for matrix, target, turn in (
            (heads + pair, key, True),
            (heads + pairs + pair, value, False),
        ):

            def write(sequence, result, target=target, columns=columns):
                for inner in range(per_device):
                    target[sequence * per_device + inner, :, columns] = result[
                        inner * rows : (inner + 1) * rows
                    ]

            projected(matrix, write, turn, 1.0)

    keys = CtxGather(at, ctx, key, lambda c: key_all.at[:, c], 1, scratch[9:14])
    values = CtxGather(at, ctx, value, lambda c: value_all.at[:, c], 1, scratch[14:19])
    keys.start()
    values.start()
    for index in range(heads):

        def write(sequence, result, index=index):
            query[sequence * tokens : (sequence + 1) * tokens, index * head : (index + 1) * head] = result

        projected(index, write, True, head ** (-0.5))
    keys.forward()
    values.forward()
    keys.rest()
    values.rest()
    for chunk in range(chunks):
        line.drain(chunk)
    keys.finish()
    values.finish()


def project(own, mine, cosine, sine, sequences, heads, pairs, ctx, fsdp):
    tokens, width = own.shape
    local_rows = mine.shape[0]
    head = 2 * cosine.shape[1]
    rows = tokens // sequences
    chunks = 4
    dma = pltpu.SemaphoreType.DMA
    block = (fsdp * sequences, rows, pairs * head)
    spread = (fsdp * sequences, ctx, rows, pairs * head)
    return pl.pallas_call(
        functools.partial(project_kernel, ctx, fsdp, tokens // chunks, heads),
        in_specs=[VMEM_SPEC] * 4,
        out_specs=[VMEM_SPEC] * 3 + [ANY_SPEC] * 2,
        out_shape=[
            jax.ShapeDtypeStruct((fsdp, tokens, width), LOW),
            jax.ShapeDtypeStruct((ctx * local_rows, mine.shape[1]), LOW),
            jax.ShapeDtypeStruct((fsdp * tokens, heads * head), LOW),
            jax.ShapeDtypeStruct(spread, LOW),
            jax.ShapeDtypeStruct(spread, LOW),
        ],
        scratch_shapes=[
            pltpu.VMEM(block, LOW),
            pltpu.VMEM(block, LOW),
            dma((2, fsdp, chunks)),
            dma((fsdp, chunks)),
        ]
        + ctx_gather_sems(ctx) * 3,
        compiler_params=pltpu.CompilerParams(vmem_limit_bytes=VMEM_LIMIT, collective_id=1),
        name="project",
    )(own, mine, cosine, sine)


class LineExchange:
    def __init__(self, at, size, span, part, low_all, mid, scratch):
        self.at, self.size, self.span, self.part, self.mid = at, size, span, part, mid
        self.hold, self.landed, self.total, self.send, self.receive = scratch[:5]
        self.chunks = part.shape[1] // span
        self.low_all = low_all
        if low_all is not None:
            self.line = LineGather(at, size, span, low_all, *scratch[5:7])
        self.steps = self.chunks + (size - 1) * (1 if low_all is None else 2)

    def hop(self, source, target, chunk, side):
        to = (self.at + (1 if side == 0 else self.size - 1)) % self.size
        rows = pl.ds(pl.multiple_of(chunk * self.span, self.span), self.span)
        return remote(
            source.at[target, rows],
            self.landed.at[side, target, rows],
            self.send.at[target, chunk],
            self.receive.at[side, target, chunk],
            "fsdp",
            to,
        )

    def pass_on(self, target, chunk, side):
        rows = pl.ds(pl.multiple_of(chunk * self.span, self.span), self.span)
        origin = self.at == 0 if side == 0 else self.at == self.size - 1

        @pl.when(origin)
        def _():
            self.hop(self.part, target, chunk, side).start()

        @pl.when(jnp.logical_not(origin))
        def _():
            self.hop(self.part, target, chunk, side).wait_recv()
            added = self.part[target, rows, :].astype(FULL)
            added = added + self.landed[side, target, rows, :].astype(FULL)
            self.hold[target, rows, :] = added.astype(LOW)
            self.hop(self.hold, target, chunk, side).start()

    def step(self, index):
        at, size, chunks = self.at, self.size, self.chunks
        for gap in range(size - 1, 0, -1):
            chunk = index - at

            @pl.when((at + gap < size) & (chunk >= 0) & (chunk < chunks))
            def _(target=at + gap, chunk=chunk):
                self.pass_on(target, chunk, 0)

            chunk = index - (size - 1 - at)

            @pl.when((at >= gap) & (chunk >= 0) & (chunk < chunks))
            def _(target=at - gap, chunk=chunk):
                self.pass_on(target, chunk, 1)

        chunk = index - (size - 1)

        @pl.when((chunk >= 0) & (chunk < chunks))
        def _():
            rows = pl.ds(pl.multiple_of(chunk * self.span, self.span), self.span)
            self.total[...] = self.part[at, rows, :].astype(FULL)
            for side, ok in ((0, at > 0), (1, at < size - 1)):

                @pl.when(ok)
                def _(side=side):
                    self.hop(self.part, at, chunk, side).wait_recv()
                    self.total[...] += self.landed[side, at, rows, :].astype(FULL)

            low = self.mid(chunk, rows, self.total[...])
            if self.low_all is not None:
                self.low_all[at, rows, :] = low
                self.line.start(chunk)

        if self.low_all is not None:
            for gap in range(1, size):
                chunk = index - (size - 1) - gap

                @pl.when((chunk >= 0) & (chunk < chunks))
                def _(gap=gap, chunk=chunk):
                    self.line.forward(chunk, gap)

    def run(self, first, last):
        def one(index, carried):
            self.step(index)
            return carried

        lax.fori_loop(first, last, one, 0)

    def drain(self):
        at, size = self.at, self.size

        def one(chunk, carried):
            for gap in range(1, size):

                @pl.when(at + gap < size)
                def _(target=at + gap):
                    self.hop(self.part, target, chunk, 0).wait_send()

                @pl.when(at >= gap)
                def _(target=at - gap):
                    self.hop(self.part, target, chunk, 1).wait_send()

            if self.low_all is not None:
                self.line.drain(chunk)
            return carried

        lax.fori_loop(0, self.chunks, one, 0)


def line_span(tokens):
    return 16


def line_scratch(fsdp, tokens, width, gather):
    span = line_span(tokens)
    chunks = tokens // span
    dma = pltpu.SemaphoreType.DMA
    return [
        pltpu.VMEM((fsdp, tokens, width), LOW),
        pltpu.VMEM((2, fsdp, tokens, width), LOW),
        pltpu.VMEM((span, width), FULL),
        dma((fsdp, chunks)),
        dma((2, fsdp, chunks)),
    ] + ([dma((2, fsdp, chunks)), dma((fsdp, chunks))] if gather else [])


def exchange_kernel(mid, size, inputs, part, *refs):
    at = lax.axis_index("fsdp")
    ins, gains, low_all, refs = refs[:inputs], refs[inputs], refs[inputs + 1], refs[inputs + 2 :]
    outs, scratch = refs[:-7], refs[-7:]
    line_greet(at, size)
    line = LineExchange(
        at,
        size,
        line_span(part.shape[1]),
        part,
        low_all,
        lambda chunk, rows, total: mid(chunk, rows, total, ins, gains, outs),
        scratch,
    )
    line.run(0, line.steps)
    line.drain()


def exchange(part, ins, gains, mid, out_shape, fsdp, collective_id, name):
    _, tokens, width = part.shape
    return pl.pallas_call(
        functools.partial(exchange_kernel, mid, fsdp, len(ins)),
        in_specs=[VMEM_SPEC] * (len(ins) + 2),
        out_specs=[VMEM_SPEC] * (len(out_shape) + 1),
        out_shape=[jax.ShapeDtypeStruct(part.shape, LOW)] + out_shape,
        scratch_shapes=line_scratch(fsdp, tokens, width, True),
        compiler_params=pltpu.CompilerParams(
            vmem_limit_bytes=VMEM_LIMIT, collective_id=collective_id
        ),
        name=name,
    )(part, *ins, gains)


def spread(step, steps, work, body):
    def one(index, carried):
        body(index)
        return carried

    lax.fori_loop((step * work) // steps, ((step + 1) * work) // steps, one, 0)


class Copies:
    def __init__(self, copies):
        self.copies = [pltpu.make_async_copy(*copy) for copy in copies]

    def start(self):
        for copy in self.copies:
            copy.start()

    def wait(self):
        for copy in self.copies:
            copy.wait()


class Forward:
    def __init__(self, mid, weights, results, part, scratch):
        self.source, self.weights, self.results, self.part = mid, weights, results, part
        self.mid, self.hidden, self.pair, self.down = scratch[:4]
        self.pair_sem, self.down_sem, self.mid_sem, self.result_sem = scratch[4:8]
        self.outs = scratch[8:]
        self.sequences, self.tokens, _ = mid.shape
        self.half = self.tokens // 2
        self.span, self.reach = self.pair.shape[3], self.down.shape[1]
        self.tiles = weights.shape[2] // self.span
        self.ends = weights.shape[1] // self.reach
        self.count = self.tiles + self.ends

    def fetch_rows(self, half, s):
        return pltpu.make_async_copy(
            self.source.at[s, self.rows(half)],
            self.mid.at[half, pl.ds(s * self.half, self.half)],
            self.mid_sem.at[half, s],
        )

    def begin(self):
        for half in range(2):
            for s in range(self.sequences):
                self.fetch_rows(half, s).start()
        self.fetch(0)

    def give(self, index):
        return pltpu.make_async_copy(
            self.outs[index], self.results[index], self.result_sem.at[index]
        )

    def fetch_pair(self, half, tile):
        slot = (half * self.tiles + tile) % 2
        columns = pl.ds(pl.multiple_of(tile * self.span, self.span), self.span)
        return pltpu.make_async_copy(
            self.weights.at[pl.ds(0, 2), :, columns], self.pair.at[slot], self.pair_sem.at[slot]
        )

    def fetch_down(self, half, tile):
        slot = (half * self.ends + tile) % 2
        rows = pl.ds(pl.multiple_of(tile * self.reach, self.reach), self.reach)
        return pltpu.make_async_copy(
            self.weights.at[2, rows], self.down.at[slot], self.down_sem.at[slot]
        )

    def fetch(self, index):
        half, tile = index // self.count, index % self.count

        @pl.when(tile < self.tiles)
        def _():
            self.fetch_pair(half, tile).start()

        @pl.when(tile >= self.tiles)
        def _():
            self.fetch_down(half, tile - self.tiles).start()

    def rows(self, half):
        return pl.ds(pl.multiple_of(half * self.half, 16), self.half)

    def run(self, index):
        half, tile = index // self.count, index % self.count

        @pl.when(index + 1 < 2 * self.count)
        def _():
            self.fetch(index + 1)

        @pl.when(tile == 0)
        def _():
            for s in range(self.sequences):
                self.fetch_rows(half, s).wait()

        @pl.when(tile < self.tiles)
        def _():
            self.fetch_pair(half, tile).wait()
            slot = (half * self.tiles + tile) % 2
            mid = self.mid[half]
            gate = dot(mid, self.pair[slot, 0], 1, 0)
            up = dot(mid, self.pair[slot, 1], 1, 0)
            columns = pl.ds(pl.multiple_of(tile * self.span, self.span), self.span)
            results = [value.astype(LOW) for value in activate(gate, up)]
            self.hidden[half, :, columns] = results[0]
            for out, value in zip(self.outs, results):
                for sequence in range(self.sequences):
                    out[sequence, self.rows(half), columns] = value[
                        sequence * self.half : (sequence + 1) * self.half
                    ]

        @pl.when(tile >= self.tiles)
        def _():
            end = tile - self.tiles
            self.fetch_down(half, end).wait()
            slot = (half * self.ends + end) % 2
            value = dot(self.hidden[half], self.down[slot], 1, 1).astype(LOW)
            columns = pl.ds(pl.multiple_of(end * self.reach, self.reach), self.reach)
            for sequence in range(self.sequences):
                self.part[sequence, self.rows(half), columns] = value[
                    sequence * self.half : (sequence + 1) * self.half
                ]


def activate(gate, up):
    square = gate * gate
    squashed = jnp.tanh(GELU_SCALE * gate * (1.0 + GELU_CUBE * square))
    half = 0.5 + 0.5 * squashed
    act = gate * half
    slope = half + act * (1.0 - squashed) * (GELU_SCALE + 3.0 * GELU_SCALE * GELU_CUBE * square)
    return act * up, up * slope, act


def late_kernel(
    size, gains, mid, mixed_in, cotangent_in, weights,
    late, out, gain, hidden, gate_factor, up_factor, *scratch
):
    at = lax.axis_index("fsdp")
    line_greet(at, size)
    part, line_parts, (mixed, cotangent, side_sem) = scratch[0], scratch[1:8], scratch[8:11]
    line = LineExchange(
        at,
        size,
        line_span(part.shape[1]),
        part,
        late,
        lambda chunk, rows, total: late_mid(
            chunk, rows, total, (mixed, cotangent), gains, (out, gain)
        ),
        line_parts,
    )
    forward = Forward(mid, weights, (hidden, gate_factor, up_factor), part, scratch[11:])
    forward.begin()
    sides = [
        pltpu.make_async_copy(source, target, side_sem.at[index])
        for index, (source, target) in enumerate(((mixed_in, mixed), (cotangent_in, cotangent)))
    ]
    for copy in sides:
        copy.start()

    def one(index, carried):
        forward.run(index)
        return carried

    lax.fori_loop(0, forward.count, one, 0)
    for copy in sides:
        copy.wait()
    ahead = line.chunks // 2

    def both(index, carried):
        line.step(index)
        spread(index, ahead, forward.count, lambda tile: forward.run(forward.count + tile))
        return carried

    lax.fori_loop(0, ahead, both, 0)
    for index in range(3):
        forward.give(index).start()
    line.run(ahead, line.steps)
    line.drain()
    for index in range(3):
        forward.give(index).wait()


def late_exchange(mid, weights, mixed, cotangent, gains, collective_id):
    fsdp, tokens, width = mid.shape
    units = weights.shape[2]
    span, reach = tile_of(units), tile_of(width)
    rows = fsdp * tokens // 2
    dma = pltpu.SemaphoreType.DMA
    low = jax.ShapeDtypeStruct((fsdp, tokens, units), LOW)
    return pl.pallas_call(
        functools.partial(late_kernel, fsdp),
        in_specs=[VMEM_SPEC] + [ANY_SPEC] * 4,
        out_specs=[VMEM_SPEC] * 3 + [ANY_SPEC] * 3,
        out_shape=[
            jax.ShapeDtypeStruct(mid.shape, LOW),
            jax.ShapeDtypeStruct((tokens, width), LOW),
            jax.ShapeDtypeStruct((1, width), FULL),
            low,
            low,
            low,
        ],
        scratch_shapes=[pltpu.VMEM(mid.shape, LOW)]
        + line_scratch(fsdp, tokens, width, True)
        + [
            pltpu.VMEM((tokens, width), FULL),
            pltpu.VMEM((tokens, width), LOW),
            dma((2,)),
            pltpu.VMEM((2, rows, width), LOW),
            pltpu.VMEM((2, rows, units), LOW),
            pltpu.VMEM((2, 2, width, span), LOW),
            pltpu.VMEM((2, reach, units), LOW),
            dma((2,)),
            dma((2,)),
            dma((2, fsdp)),
            dma((3,)),
        ]
        + [pltpu.VMEM((fsdp, tokens, units), LOW)] * 3,
        compiler_params=pltpu.CompilerParams(
            vmem_limit_bytes=VMEM_LIMIT, collective_id=collective_id
        ),
        name="late_exchange",
    )(gains, mid, mixed, cotangent, weights)


class Backward:
    def __init__(self, late, mid, weights, factors, part, grads, scratch):
        self.weights, self.part, self.grads = weights, part, grads
        self.late, self.mid, self.factors = late, mid, factors
        self.rows_in, self.turned, self.pairs, self.wide, self.tall, self.stage = scratch[:6]
        self.wide_sem, self.tall_sem, self.stage_sem, self.row_sem, self.factor_sem = scratch[6:11]
        self.block, self.block_sem = scratch[11:13]
        self.own_factors = scratch[13:]
        self.sequences, self.tokens, self.width = late.shape
        self.half = self.tokens // 2
        self.span, self.reach = self.wide.shape[2], self.tall.shape[2]
        self.units = weights.shape[2]
        self.tiles = self.units // self.span
        self.ends = self.width // self.reach
        self.count = self.tiles + self.ends
        self.sums = 2 * self.units // self.stage.shape[2]
        self.pieces = 2 * self.ends
        self.work = self.sums * (self.width // 768)

    def rows(self, half):
        return pl.ds(pl.multiple_of(half * self.half, 16), self.half)

    def fetch_rows(self, half, s):
        return pltpu.make_async_copy(
            self.late.at[s, self.rows(half)],
            self.rows_in.at[half, pl.ds(s * self.half, self.half)],
            self.row_sem.at[half, s],
        )

    def begin(self):
        for half in range(2):
            for s in range(self.sequences):
                self.fetch_rows(half, s).start()
        self.fetch(0)
        self.fetch_block(0).start()

    def fetch_block(self, piece):
        half, block = piece // self.ends, piece % self.ends
        span = pl.ds(pl.multiple_of(block * self.reach, self.reach), self.reach)
        return Copies(
            (
                self.mid.at[s, self.rows(half), span],
                self.block.at[piece % 2, pl.ds(s * self.half, self.half)],
                self.block_sem.at[piece % 2, s],
            )
            for s in range(self.sequences)
        )

    def turn(self, piece):
        @pl.when(piece + 1 < self.pieces)
        def _():
            self.fetch_block(piece + 1).start()

        self.fetch_block(piece).wait()
        rows = self.sequences * self.half
        half, block = piece // self.ends, piece % self.ends
        span = pl.ds(pl.multiple_of(block * self.reach, self.reach), self.reach)
        columns = pl.ds(pl.multiple_of(half * rows, 128), rows)
        self.turned[span, columns] = self.block[piece % 2].T

    def fetch_wide(self, half, tile):
        slot = (half * self.tiles + tile) % 2
        columns = pl.ds(pl.multiple_of(tile * self.span, self.span), self.span)
        rows = self.rows(half)
        return Copies(
            [(self.weights.at[2, :, columns], self.wide.at[slot], self.wide_sem.at[slot])]
            + [
                (
                    self.factors[side].at[:, rows, columns],
                    self.own_factors[side].at[:, rows, columns],
                    self.factor_sem.at[slot, side],
                )
                for side in range(2)
            ]
        )

    def fetch_tall(self, half, tile):
        slot = (half * self.ends + tile) % 2
        rows = pl.ds(pl.multiple_of(tile * self.reach, self.reach), self.reach)
        return pltpu.make_async_copy(
            self.weights.at[pl.ds(0, 2), rows], self.tall.at[slot], self.tall_sem.at[slot]
        )

    def fetch(self, index):
        half, tile = index // self.count, index % self.count

        @pl.when(tile < self.tiles)
        def _():
            self.fetch_wide(half, tile).start()

        @pl.when(tile >= self.tiles)
        def _():
            self.fetch_tall(half, tile - self.tiles).start()

    def run(self, index):
        half, tile = index // self.count, index % self.count
        rows = self.rows(half)

        @pl.when(index + 1 < 2 * self.count)
        def _():
            self.fetch(index + 1)

        @pl.when(tile == 0)
        def _():
            for s in range(self.sequences):
                self.fetch_rows(half, s).wait()

        @pl.when(tile < self.tiles)
        def _():
            self.fetch_wide(half, tile).wait()
            slot = (half * self.tiles + tile) % 2
            hidden_grad = dot(self.rows_in[half], self.wide[slot], 1, 0)
            columns = pl.ds(pl.multiple_of(tile * self.span, self.span), self.span)
            for side, factor in enumerate(self.own_factors):
                target = pl.ds(
                    pl.multiple_of(side * self.units + tile * self.span, self.span), self.span
                )
                for s in range(self.sequences):
                    own = slice(s * self.half, (s + 1) * self.half)
                    value = hidden_grad[own] * factor[s, rows, columns].astype(FULL)
                    self.pairs[half, own, target] = value.astype(LOW)

        @pl.when(tile >= self.tiles)
        def _():
            end = tile - self.tiles
            self.fetch_tall(half, end).wait()
            slot = (half * self.ends + end) % 2
            value = dot(self.pairs[half, :, : self.units], self.tall[slot, 0], 1, 1)
            value = value + dot(self.pairs[half, :, self.units :], self.tall[slot, 1], 1, 1)
            value = value.astype(LOW)
            columns = pl.ds(pl.multiple_of(end * self.reach, self.reach), self.reach)
            for s in range(self.sequences):
                self.part[s, rows, columns] = value[s * self.half : (s + 1) * self.half]

    def put(self, index):
        span = self.stage.shape[2]
        columns = pl.ds(pl.multiple_of(index * span, span), span)
        return pltpu.make_async_copy(
            self.stage.at[index % 2], self.grads.at[:, columns], self.stage_sem.at[index % 2]
        )

    def sum(self, unit):
        thirds = self.width // 768
        index, third = unit // thirds, unit % thirds

        @pl.when((third == 0) & (index >= 2))
        def _():
            self.put(index - 2).wait()

        span = self.stage.shape[2]
        columns = pl.ds(pl.multiple_of(index * span, span), span)
        rows = self.sequences * self.half
        own = pl.ds(pl.multiple_of(third * 768, 768), 768)
        value = dot(self.turned[own, :rows], self.pairs[0, :, columns], 1, 0)
        value = value + dot(self.turned[own, rows:], self.pairs[1, :, columns], 1, 0)
        self.stage[index % 2, own, :] = value.astype(LOW)

        @pl.when(third == thirds - 1)
        def _():
            self.put(index).start()


def mid_kernel(
    size, gains, late, mixed_in, branch_in, cotangent_in, gate_factor, up_factor, mid, weights,
    low, mixed_grad, gain, grads, *scratch
):
    at = lax.axis_index("fsdp")
    line_greet(at, size)
    part, line_parts, sides = scratch[0], scratch[1:8], scratch[8:11]
    side_sem = scratch[11]
    line = LineExchange(
        at,
        size,
        line_span(part.shape[1]),
        part,
        low,
        lambda chunk, rows, total: mid_mid(
            chunk, rows, total, sides, gains, (mixed_grad, gain)
        ),
        line_parts,
    )
    backward = Backward(late, mid, weights, (gate_factor, up_factor), part, grads, scratch[12:])
    backward.begin()
    copies = [
        pltpu.make_async_copy(source, target, side_sem.at[index])
        for index, (source, target) in enumerate(zip((mixed_in, branch_in, cotangent_in), sides))
    ]
    for copy in copies:
        copy.start()

    def one(index, carried):
        backward.run(index)
        spread(index, backward.count, backward.pieces, backward.turn)
        return carried

    lax.fori_loop(0, backward.count, one, 0)
    for copy in copies:
        copy.wait()
    ahead = line.chunks // 2

    def both(index, carried):
        line.step(index)
        spread(index, ahead, backward.count, lambda tile: backward.run(backward.count + tile))
        return carried

    lax.fori_loop(0, ahead, both, 0)
    busy = 6

    def more(index, carried):
        line.step(ahead + index)
        spread(index, busy, backward.work, backward.sum)
        return carried

    lax.fori_loop(0, busy, more, 0)
    line.run(ahead + busy, line.steps)
    line.drain()
    backward.put(backward.sums - 2).wait()
    backward.put(backward.sums - 1).wait()


def mid_exchange(
    late, mid, mixed, branch, cotangent, gains, gate_factor, up_factor, weights, collective_id
):
    fsdp, tokens, width = mid.shape
    units = weights.shape[2]
    span, reach, stage = tile_of(units), 384, 384 if fsdp <= 4 else 256
    rows = fsdp * tokens // 2
    dma = pltpu.SemaphoreType.DMA
    return pl.pallas_call(
        functools.partial(mid_kernel, fsdp),
        in_specs=[VMEM_SPEC] + [ANY_SPEC] * 8,
        out_specs=[VMEM_SPEC] * 3 + [ANY_SPEC],
        out_shape=[
            jax.ShapeDtypeStruct(mid.shape, LOW),
            jax.ShapeDtypeStruct((tokens, width), FULL),
            jax.ShapeDtypeStruct((2, width), FULL),
            jax.ShapeDtypeStruct((width, 2 * units), LOW),
        ],
        scratch_shapes=[pltpu.VMEM(mid.shape, LOW)]
        + line_scratch(fsdp, tokens, width, True)
        + [
            pltpu.VMEM((tokens, width), FULL),
            pltpu.VMEM((tokens, width), FULL),
            pltpu.VMEM((tokens, width), LOW),
            dma((3,)),
            pltpu.VMEM((2, rows, width), LOW),
            pltpu.VMEM((width, 2 * rows), LOW),
            pltpu.VMEM((2, rows, 2 * units), LOW),
            pltpu.VMEM((2, width, span), LOW),
            pltpu.VMEM((2, 2, reach, units), LOW),
            pltpu.VMEM((2, width, stage), LOW),
            dma((2,)),
            dma((2,)),
            dma((2,)),
            dma((2, fsdp)),
            dma((2, 2)),
            pltpu.VMEM((2, rows, reach), LOW),
            dma((2, fsdp)),
        ]
        + [pltpu.VMEM((fsdp, tokens, units), LOW)] * 2,
        compiler_params=pltpu.CompilerParams(
            vmem_limit_bytes=VMEM_LIMIT, collective_id=collective_id
        ),
        name="mid_exchange",
    )(gains, late, mixed, branch, cotangent, gate_factor, up_factor, mid, weights)


def row_sum(values):
    return jnp.sum(values, 0, keepdims=True)


def add_gain(ref, chunk, index, values):
    @pl.when(chunk == 0)
    def _():
        ref[index : index + 1, :] = row_sum(values)

    @pl.when(chunk > 0)
    def _():
        ref[index : index + 1, :] += row_sum(values)


def branch_mid(chunk, rows, branch, ins, gains, outs):
    (x,), (branch_out, mixed_out) = ins, outs
    branch_out[rows, :] = branch
    post_hat = branch * rms_scale(branch)
    mixed = x[rows, :].astype(FULL) + post_hat * (1.0 + gains[1:2, :])
    mixed_out[rows, :] = mixed
    return (mixed * rms_scale(mixed) * (1.0 + gains[2:3, :])).astype(LOW)


def late_mid(chunk, rows, ffn_branch, ins, gains, outs):
    (mixed, cotangent), (out, gain) = ins, outs
    inv_late = rms_scale(ffn_branch)
    late_hat = ffn_branch * inv_late
    scale = 1.0 + gains[3:4, :]
    out[rows, :] = (mixed[rows, :] + late_hat * scale).astype(LOW)
    upstream = cotangent[rows, :].astype(FULL)
    add_gain(gain, chunk, 0, upstream * late_hat)
    scaled = upstream * scale
    grad = inv_late * (scaled - late_hat * jnp.mean(scaled * late_hat, -1, keepdims=True))
    return grad.astype(LOW)


def mid_mid(chunk, rows, mid_grad, ins, gains, outs):
    (mixed, branch, cotangent), (mixed_grad_out, gain) = ins, outs
    mixed = mixed[rows, :]
    inv_mid = rms_scale(mixed)
    mid_hat = mixed * inv_mid
    add_gain(gain, chunk, 1, mid_grad * mid_hat)
    scaled = mid_grad * (1.0 + gains[2:3, :])
    mixed_grad = cotangent[rows, :].astype(FULL) + inv_mid * (
        scaled - mid_hat * jnp.mean(scaled * mid_hat, -1, keepdims=True)
    )
    mixed_grad_out[rows, :] = mixed_grad
    branch = branch[rows, :]
    inv_post = rms_scale(branch)
    post_hat = branch * inv_post
    add_gain(gain, chunk, 0, mixed_grad * post_hat)
    hat = mixed_grad * (1.0 + gains[1:2, :])
    grad = inv_post * (hat - post_hat * jnp.mean(hat * post_hat, -1, keepdims=True))
    return grad.astype(LOW)


def pre_mid(chunk, rows, normed_grad, ins, gains, outs):
    (x, mixed_grad), (out, gain) = ins, outs
    x = x[rows, :].astype(FULL)
    inv_pre = rms_scale(x)
    normed = x * inv_pre
    add_gain(gain, chunk, 0, normed_grad * normed)
    scaled = normed_grad * (1.0 + gains[0:1, :])
    out[rows, :] = mixed_grad[rows, :] + inv_pre * (
        scaled - normed * jnp.mean(scaled * normed, -1, keepdims=True)
    )


def pair_sums_kernel(ctx, key, value, key_sum, value_sum, *scratch):
    at = lax.axis_index("ctx")
    greet(ctx_peers(at, ctx))
    keys = ctx_scatter(at, ctx, lambda c: key.at[:, c], scratch)
    values = ctx_scatter(at, ctx, lambda c: value.at[:, c], scratch[SCATTER:])
    keys.start()
    values.start()
    keys.diagonal()
    values.diagonal()
    keys.neighbours()
    values.neighbours()
    keys.passing()
    values.passing()
    for scatter, out in ((keys, key_sum), (values, value_sum)):

        def store(block, rows, total, out=out):
            out[block, rows, :] = total

        scatter.finish(store)
    keys.drain()
    values.drain()


def scatter_pairs(key, value):
    sequences, ctx, rows, width = key.shape
    return pl.pallas_call(
        functools.partial(pair_sums_kernel, ctx),
        in_specs=[VMEM_SPEC] * 2,
        out_specs=[VMEM_SPEC] * 2,
        out_shape=[jax.ShapeDtypeStruct((sequences, rows, width), FULL)] * 2,
        scratch_shapes=ctx_scatter_scratch(ctx, sequences, rows, width, LOW) * 2,
        compiler_params=pltpu.CompilerParams(vmem_limit_bytes=VMEM_LIMIT, collective_id=2),
        name="scatter_pairs",
    )(key, value)


def tail_kernel(
    ctx, fsdp, in_part, out_part, pre_part, x, mixed_grad, gains, in_old, out_old, *refs
):
    at, line_at = lax.axis_index("ctx"), lax.axis_index("fsdp")
    in_new, out_new, update, gram, input_grad, gain = refs[:6]
    scratch = refs[6:]
    places = head_places(fsdp)
    mine = len(places[0])
    scratch, others = scratch[: 2 * SCATTER], scratch[2 * SCATTER :]
    mine_sum, arrived, move_send, move_receive, out_sum = others[:5]
    head = arrived.shape[-1]
    greet(ctx_peers(at, ctx) + [("fsdp", (line_at + k) % fsdp) for k in range(1, fsdp)])
    ins = ctx_scatter(at, ctx, rows_of_ctx(in_part), scratch)
    outs = ctx_scatter(at, ctx, rows_of_ctx(out_part), scratch[SCATTER:])
    line = LineExchange(
        line_at,
        fsdp,
        line_span(pre_part.shape[1]),
        pre_part,
        None,
        lambda chunk, rows, total: pre_mid(
            chunk, rows, total, (x, mixed_grad), gains, (input_grad, gain)
        ),
        others[5:10],
    )
    ins.start()
    outs.start()
    ins.diagonal()
    ins.neighbours()
    line.run(0, 3)
    ins.passing()
    outs.diagonal()
    outs.neighbours()
    line.run(3, 6)
    outs.passing()
    line.run(6, 8)

    def store_in(block, rows, total):
        mine_sum[rows, :] = total.astype(LOW)

    def store_out(block, rows, total):
        out_sum[rows, :] = total

    ins.finish(store_in)

    def copies_of(owner, index):
        return [
            (user, slot)
            for user in range(fsdp)
            for slot in range(mine)
            if places[user][slot] == (owner, index)
        ]

    def move(user, slot):
        owner, index = places[user][slot]
        copy = copies_of(owner, index).index((user, slot))
        return remote(
            mine_sum.at[:, pl.ds(slot * head, head)],
            arrived.at[index, copy],
            move_send.at[slot],
            move_receive.at[index, copy],
            "fsdp",
            owner,
        )

    for user in range(fsdp):
        for slot in range(mine):

            @pl.when(line_at == user)
            def _(user=user, slot=slot):
                owner, index = places[user][slot]
                if owner == user:
                    copy = copies_of(owner, index).index((user, slot))
                    arrived[index, copy] = mine_sum[:, slot * head : (slot + 1) * head]
                else:
                    move(user, slot).start()

    line.run(8, line.steps)
    outs.finish(store_out)

    def step_of(index, grad, old_ref, new_ref, at):
        new = MOMENTUM_DECAY * old_ref[:, at, :] + grad
        new_ref[:, at, :] = new
        low = (grad + MOMENTUM_DECAY * new).astype(LOW)
        update[index] = low
        gram[index] = dot(low, low, 0, 0)

    stored = in_old.shape[1]
    for index in range(out_old.shape[1]):
        grad = out_sum[:, index * head : (index + 1) * head]
        step_of(stored + index, grad, out_old, out_new, index)
    for index in range(stored + out_old.shape[1], gram.shape[0]):
        gram[index] = jnp.zeros((head, head), FULL)
    for owner in range(fsdp):

        @pl.when(line_at == owner)
        def _(owner=owner):
            for index in range(stored):
                for user, slot in copies_of(owner, index):
                    if user != owner:
                        move(user, slot).wait_recv()

    for index in range(stored):
        grad = arrived[index, 0].astype(FULL)
        for copy in range(1, arrived.shape[1]):
            more = arrived[index, copy].astype(FULL)
            paired = line_at * stored + index >= QUERY_HEADS
            grad = grad + jnp.where(paired, more, 0.0)
        step_of(index, grad, in_old, in_new, index)
    for user in range(fsdp):
        for slot in range(mine):
            if places[user][slot][0] != user:

                @pl.when(line_at == user)
                def _(user=user, slot=slot):
                    move(user, slot).wait_send()

    ins.drain()
    outs.drain()
    line.drain()


def tail(in_part, out_part, pre_part, x, mixed_grad, gains, in_old, out_old):
    _, stored, head = in_old.shape
    matrices = stored + out_old.shape[1]
    ctx, rows, in_width = in_part.shape
    out_width = out_part.shape[2]
    fsdp, tokens, width = pre_part.shape
    mine = len(head_places(fsdp)[0])
    copies = max(1, fsdp // KEY_VALUE_HEADS)
    dma = pltpu.SemaphoreType.DMA
    return pl.pallas_call(
        functools.partial(tail_kernel, ctx, fsdp),
        in_specs=[VMEM_SPEC] * 8,
        out_specs=[VMEM_SPEC] * 6,
        out_shape=[
            jax.ShapeDtypeStruct(in_old.shape, FULL),
            jax.ShapeDtypeStruct(out_old.shape, FULL),
            jax.ShapeDtypeStruct((matrices, rows, head), LOW),
            jax.ShapeDtypeStruct((ctx * (-(-matrices // ctx)), head, head), FULL),
            jax.ShapeDtypeStruct((tokens, width), FULL),
            jax.ShapeDtypeStruct((1, width), FULL),
        ],
        scratch_shapes=ctx_scatter_scratch(ctx, 1, rows, in_width, LOW)
        + ctx_scatter_scratch(ctx, 1, rows, out_width, LOW)
        + [
            pltpu.VMEM((rows, in_width), LOW),
            pltpu.VMEM((stored, copies, rows, head), LOW),
            dma((mine,)),
            dma((stored, copies)),
            pltpu.VMEM((rows, out_width), FULL),
        ]
        + line_scratch(fsdp, tokens, width, False),
        compiler_params=pltpu.CompilerParams(vmem_limit_bytes=VMEM_LIMIT, collective_id=3),
        name="tail",
    )(in_part, out_part, pre_part, x, mixed_grad, gains, in_old, out_old)


def packed_rows(small, large):
    squares = -(-small // 2)
    return squares * FBLK + large * 2 * FBLK + 16 * (-(-(squares + large) // 16))


def grid_of(size):
    rows = lax.broadcasted_iota(jnp.int32, (size, size), 0)
    return rows, lax.broadcasted_iota(jnp.int32, (size, size), 1)


def pack_two(first, second):
    rows, columns = grid_of(FBLK)
    if second is None:
        return first, jnp.zeros((1, FBLK), FULL)
    diagonal = jnp.sum(jnp.where(rows == columns, second, 0.0), 0, keepdims=True)
    return jnp.where(rows <= columns, first, second), diagonal


def unpack_two(square, diagonal, both):
    rows, columns = grid_of(FBLK)
    if not both:
        return square, None
    turned = square.T
    first = jnp.where(rows <= columns, square, turned)
    second = jnp.where(rows > columns, square, jnp.where(rows < columns, turned, diagonal))
    return first, second


def pack_all(blocks, heads, write):
    small, large = blocks[0], heads[0]
    squares = -(-small // 2)
    edge = squares * FBLK + large * 2 * FBLK
    for index in range(squares):
        second = blocks[1](2 * index + 1) if 2 * index + 1 < small else None
        square, diagonal = pack_two(blocks[1](2 * index), second)
        write(index * FBLK, square)
        write(edge + index, diagonal)
    for index in range(large):
        head = heads[1](index)
        square, diagonal = pack_two(head[:FBLK, :FBLK], head[FBLK:, FBLK:])
        base = squares * FBLK + index * 2 * FBLK
        write(base, square)
        write(base + FBLK, head[:FBLK, FBLK:])
        write(edge + squares + index, diagonal)


def unpack_all(small, large, read):
    squares = -(-small // 2)
    edge = squares * FBLK + large * 2 * FBLK
    blocks, heads = [], []
    for index in range(squares):
        both = 2 * index + 1 < small
        first, second = unpack_two(read(index * FBLK, FBLK), read(edge + index, 1), both)
        blocks += [first, second] if both else [first]
    for index in range(large):
        base = squares * FBLK + index * 2 * FBLK
        first, second = unpack_two(read(base, FBLK), read(edge + squares + index, 1), True)
        corner = read(base + FBLK, FBLK)
        heads.append(
            jnp.concatenate(
                [
                    jnp.concatenate([first, corner], 1),
                    jnp.concatenate([corner.T, second], 1),
                ],
                0,
            )
        )
    return blocks, heads


def newton_kernel(
    ctx, fsdp, head_rate, ffn_rate, heads, blocks, gains, head_update, in_old, out_old, ffn_update,
    ffn_old, in_new, out_new, ffn_new, gains_all, *scratch
):
    at, line_at = lax.axis_index("ctx"), lax.axis_index("fsdp")
    small, large = blocks.shape[1], heads.shape[1]
    packed, gram, poly, poly_all, gains_line, gains_sum, gain_send, gain_receive = scratch[:8]
    update, weights, update_sem, weight_sem, out_sem = scratch[8:13]
    scratch = scratch[13:]
    matrices, _, width = weights.shape
    per_matrix = width // FBLK
    count = matrices * per_matrix
    greet(ctx_peers(at, ctx) + [("fsdp", (line_at + k) % fsdp) for k in range(1, fsdp)])

    def gain_copy(k):
        return remote(
            gains,
            gains_line.at[k],
            gain_send.at[k],
            gain_receive.at[k],
            "fsdp",
            (line_at + k) % fsdp,
        )

    def fetches(matrix):
        return [
            pltpu.make_async_copy(
                ffn_update.at[matrix], update.at[matrix], update_sem.at[matrix]
            ),
            pltpu.make_async_copy(ffn_old.at[matrix], weights.at[matrix], weight_sem.at[matrix]),
        ]

    for k in range(1, fsdp):
        gain_copy(k).start()
    edge = packed_rows(small, large) - 16 * (-(-(-(-small // 2) + large) // 16))

    def pack_for(index, carried):
        packed[index, edge:, :] = jnp.zeros((packed.shape[1] - edge, FBLK), FULL)

        def write(first, rows):
            packed[index, first : first + rows.shape[0], :] = rows

        pack_all((small, lambda i: blocks[index, i]), (large, lambda i: heads[index, i]), write)
        return carried

    lax.fori_loop(0, ctx, pack_for, 0)
    scatter = ctx_scatter(at, ctx, rows_of_ctx(packed), scratch)
    scatter.start()
    for matrix in range(matrices):
        for copy in fetches(matrix):
            copy.start()
    scatter.diagonal()
    scatter.neighbours()
    scatter.passing()
    total = gains[...]
    for k in range(1, fsdp):
        gain_copy(k).wait_recv()
        total = total + gains_line[k]
    gains_sum[...] = total
    scratch = scratch[SCATTER:]
    gather_gains = CtxGather(at, ctx, gains_sum, lambda c: gains_all.at[c], 0, scratch[:5])
    gather = CtxGather(at, ctx, poly, lambda c: poly_all.at[c], 0, scratch[5:10])

    def store(block, rows, total):
        gram[rows, :] = total

    scatter.finish(store)
    gather_gains.start()
    block_grams, head_grams = unpack_all(
        small, large, lambda first, count: gram[first : first + count, :]
    )
    polys = polys_of(head_grams + block_grams)
    head_polys, block_polys = polys[:large], polys[large:]
    poly[edge:, :] = jnp.zeros((poly.shape[0] - edge, FBLK), FULL)

    def write(first, rows):
        poly[first : first + rows.shape[0], :] = rows

    pack_all((small, lambda i: block_polys[i]), (large, lambda i: head_polys[i]), write)
    gather.start()
    for matrix in range(matrices):
        for copy in fetches(matrix):
            copy.wait()

    def place(block):
        matrix = block // per_matrix
        columns = pl.ds(pl.multiple_of((block % per_matrix) * FBLK, FBLK), FBLK)
        return matrix, columns

    def put(block):
        matrix, columns = place(block)
        return pltpu.make_async_copy(
            weights.at[matrix, :, columns], ffn_new.at[matrix, :, columns], out_sem.at[block]
        )

    def apply(source, first):
        found, _ = unpack_all(small, 0, lambda row, count: source(row, count))
        for index, found_poly in enumerate(found):
            block = first * small + index

            @pl.when(block < count)
            def _(block=block, found_poly=found_poly):
                matrix, columns = place(block)
                step = moved(update[matrix, :, columns], found_poly)
                weights[matrix, :, columns] = weights[matrix, :, columns] * SHRINK - ffn_rate * step
                put(block).start()

    shift = large * 2 * FBLK

    def reader(view):
        edge_small = -(-small // 2) * FBLK

        def read(row, count):
            row = row + shift if row >= edge_small else row
            return view[row : row + count, :]

        return read

    apply(reader(poly), at)
    gather_gains.forward()
    gather.forward()
    gather_gains.rest()
    gather.rest()
    square = gather.square
    for j in range(square.column):
        for turn in (False, True):
            if j > 0 or turn:
                device = square.device(j, turn)
                apply(reader(poly_all.at[device]), device)
    for k in range(1, fsdp):
        gain_copy(k).wait_send()
    gather_gains.finish()
    gather.finish()
    for j in range(square.column):
        for turn in (False, True):
            device = square.device(j, turn, 1 - square.core)
            apply(reader(poly_all.at[device]), device)
    stored = in_old.shape[1]
    for device in range(ctx):
        first = device * large
        if first < head_update.shape[0]:
            _, found = unpack_all(
                small, large, lambda row, count: poly_all[device, row : row + count, :]
            )
            for index in range(first, min(first + large, head_update.shape[0])):
                step = head_rate * moved(head_update[index], found[index - first])
                if index < stored:
                    in_new[:, index, :] = in_old[:, index, :] * SHRINK - step
                else:
                    out_new[:, index - stored, :] = out_old[:, index - stored, :] * SHRINK - step
    scatter.drain()

    def finish(block, carried):
        put(block).wait()
        return carried

    lax.fori_loop(0, count, finish, 0)


def newton(
    heads, blocks, gains, head_update, in_old, out_old, ffn_update, ffn_old, head_rate, ffn_rate, fsdp
):
    ctx, large = heads.shape[:2]
    small = blocks.shape[1]
    rows = packed_rows(small, large)
    dma = pltpu.SemaphoreType.DMA
    matrices = ffn_old.shape[0]
    return pl.pallas_call(
        functools.partial(newton_kernel, ctx, fsdp, head_rate, ffn_rate),
        in_specs=[VMEM_SPEC] * 6 + [ANY_SPEC] * 2,
        out_specs=[VMEM_SPEC] * 2 + [ANY_SPEC, VMEM_SPEC],
        out_shape=[
            jax.ShapeDtypeStruct(in_old.shape, FULL),
            jax.ShapeDtypeStruct(out_old.shape, FULL),
            jax.ShapeDtypeStruct(ffn_old.shape, FULL),
            jax.ShapeDtypeStruct((ctx,) + gains.shape, FULL),
        ],
        scratch_shapes=[
            pltpu.VMEM((ctx, rows, FBLK), FULL),
            pltpu.VMEM((rows, FBLK), FULL),
            pltpu.VMEM((rows, FBLK), FULL),
            pltpu.VMEM((ctx, rows, FBLK), FULL),
            pltpu.VMEM((fsdp,) + gains.shape, FULL),
            pltpu.VMEM(gains.shape, FULL),
            dma((fsdp,)),
            dma((fsdp,)),
            pltpu.VMEM(ffn_update.shape, LOW),
            pltpu.VMEM(ffn_old.shape, FULL),
            dma((matrices,)),
            dma((matrices,)),
            dma((ctx * small,)),
        ]
        + ctx_scatter_scratch(ctx, 1, rows, FBLK, FULL)
        + ctx_gather_sems(ctx) * 2,
        compiler_params=pltpu.CompilerParams(vmem_limit_bytes=VMEM_LIMIT, collective_id=4),
        name="newton",
    )(heads, blocks, gains, head_update, in_old, out_old, ffn_update, ffn_old)


def local(
    inputs,
    cotangent,
    weights_in,
    weights_out,
    ffn_weights,
    norm_gains,
    momentum_in,
    momentum_out,
    ffn_momentum,
    gain_first,
    gain_second,
    stretch_order,
):
    sequences, rows, width = inputs.shape
    stretch_rows = rows // 2
    local_rows, in_local, head = weights_in.shape
    out_local = weights_out.shape[1]
    ffn_local = ffn_weights.shape[2]
    ctx, fsdp = lax.axis_size("ctx"), lax.axis_size("fsdp")
    ctx_at = lax.axis_index("ctx")
    tokens = sequences * rows
    all_sequences = sequences * fsdp
    heads = QUERY_HEADS // fsdp
    pairs = max(1, KEY_VALUE_HEADS // fsdp)
    shared = heads // pairs
    mine = heads + 2 * pairs

    ffn_mine = jnp.transpose(ffn_weights, (1, 0, 2))

    flat = inputs.reshape(tokens, width)
    mine_in, w_out, ffn_cut, own_normed = prepare(
        weights_in, weights_out, ffn_mine, flat, norm_gains, ctx, fsdp
    )
    ffn_low = lax.all_gather(ffn_cut, "ctx", axis=1, tiled=True)
    own_places = positions_of(
        ctx_at * rows + jnp.arange(rows, dtype=jnp.int32), stretch_order, stretch_rows
    )
    all_places = positions_of(
        jnp.arange(ctx * rows, dtype=jnp.int32), stretch_order, stretch_rows
    )
    cosine, sine = rope_tables(own_places, head)
    normed_low, w_in, query, key_all, value_all = project(
        own_normed,
        mine_in,
        jnp.tile(cosine, (sequences, 1)),
        jnp.tile(sine, (sequences, 1)),
        sequences,
        heads,
        pairs,
        ctx,
        fsdp,
    )
    normed_low = normed_low.reshape(fsdp * tokens, width)
    w_out = w_out.reshape(width, out_local * head)
    cosine, sine = jnp.tile(cosine, (all_sequences, 1)), jnp.tile(sine, (all_sequences, 1))
    scale = head ** (-0.5)

    def column(values, index):
        return values[:, index * head : (index + 1) * head]

    def by_sequence(columns):
        return jnp.concatenate([c.reshape(all_sequences, rows, head) for c in columns], 1)

    def flat_heads(values, count):
        return [
            values[:, g * rows : (g + 1) * rows].reshape(all_sequences * rows, head)
            for g in range(count)
        ]

    def heads_of(pair):
        return range(pair * shared, (pair + 1) * shared)

    query = [by_sequence([column(query, h) for h in heads_of(pair)]) for pair in range(pairs)]
    key_all = key_all.reshape(all_sequences, ctx * rows, pairs * head)
    value_all = value_all.reshape(all_sequences, ctx * rows, pairs * head)
    key_of = [key_all[:, :, p * head : (p + 1) * head] for p in range(pairs)]
    value_of = [value_all[:, :, p * head : (p + 1) * head] for p in range(pairs)]
    visible = jnp.tile(all_places[None, :] <= own_places[:, None], (shared, 1))[None]
    exponent, slope, exponent_low, row_total, attended = [], [], [], [], []
    for p in range(pairs):
        scores = batched(query[p], key_of[p], 2, 2)
        squashed = jnp.tanh(scores / SOFT_CAP)
        exponent.append(jnp.where(visible, jnp.exp(SOFT_CAP * squashed - EXP_SHIFT), 0.0))
        slope.append(exponent[p] * (1.0 - squashed * squashed))
        row_total.append(jnp.sum(exponent[p], -1, keepdims=True))
        exponent_low.append(exponent[p].astype(LOW))
        attended.append(batched(exponent_low[p], value_of[p], 2, 1) / row_total[p])
    attended_low = jnp.concatenate(
        sum([flat_heads(attended[p].astype(LOW), shared) for p in range(pairs)], []), 1
    )

    def parts(values):
        return values.astype(LOW).reshape(fsdp, tokens, width)

    full_rows = jax.ShapeDtypeStruct((tokens, width), FULL)
    low_rows = jax.ShapeDtypeStruct((tokens, width), LOW)

    def gain_rows(count):
        return jax.ShapeDtypeStruct((count, width), FULL)

    upstream = cotangent.reshape(tokens, width)
    mid_low, branch, mixed = exchange(
        parts(dot(attended_low, w_out, 1, 1)),
        [flat],
        norm_gains,
        branch_mid,
        [full_rows, full_rows],
        fsdp,
        5,
        "branch_exchange",
    )

    late_low, outputs, gain_late, hidden_low, gate_factor, up_factor = late_exchange(
        mid_low, ffn_low, mixed, upstream, norm_gains, 6
    )
    down_grads = lax.psum_scatter(
        dot(
            late_low.reshape(fsdp * tokens, width),
            hidden_low.reshape(fsdp * tokens, ffn_local),
            0,
            0,
        ).astype(LOW),
        "ctx",
        scatter_dimension=0,
        tiled=True,
    )
    branch_low, mixed_grad, gain_middle, pair_part = mid_exchange(
        late_low, mid_low, mixed, branch, upstream, norm_gains, gate_factor, up_factor, ffn_low, 7
    )
    pair_grads = lax.psum_scatter(pair_part, "ctx", scatter_dimension=0, tiled=True)

    branch_low = branch_low.reshape(fsdp * tokens, width)
    attended_grad = dot(branch_low, w_out, 1, 0)
    query_grad, key_part, value_part = [], [], []
    for p in range(pairs):
        grad = by_sequence([column(attended_grad, h) for h in heads_of(p)])
        numerator_low = (grad / row_total[p]).astype(LOW)
        row_term = jnp.sum(grad * attended[p], -1, keepdims=True) / row_total[p]
        pulled = batched(numerator_low, value_of[p], 2, 2)
        score_low = (slope[p] * (pulled - row_term)).astype(LOW)
        query_grad += flat_heads(batched(score_low, key_of[p], 2, 1), shared)
        key_part.append(batched(score_low, query[p], 1, 1).astype(LOW))
        value_part.append(batched(exponent_low[p], numerator_low, 1, 1).astype(LOW))
    spread = (all_sequences, ctx, rows, pairs * head)
    key_grad, value_grad = scatter_pairs(
        jnp.concatenate(key_part, 2).reshape(spread), jnp.concatenate(value_part, 2).reshape(spread)
    )
    key_grad = key_grad.reshape(all_sequences * rows, pairs * head)
    value_grad = value_grad.reshape(all_sequences * rows, pairs * head)
    projected_grad = jnp.concatenate(
        [rotate(grad * scale, cosine, -sine) for grad in query_grad]
        + [rotate(column(key_grad, p), cosine, -sine) for p in range(pairs)]
        + [value_grad],
        1,
    ).astype(LOW)
    momentum = jnp.transpose(ffn_momentum, (1, 0, 2))
    small = -(-3 * (ffn_local // FBLK) // ctx)
    earlier = ffn_gram(down_grads, momentum, 2, ctx * small, [])
    momentum_new_in, momentum_new_out, head_update, head_gram, input_grad, gain_pre = tail(
        dot(normed_low, projected_grad, 0, 0).astype(LOW).reshape(ctx, local_rows, mine * head),
        dot(branch_low, attended_low, 0, 0).astype(LOW).reshape(ctx, local_rows, out_local * head),
        parts(dot(projected_grad, w_in, 1, 1)),
        flat,
        mixed_grad,
        norm_gains,
        momentum_in,
        momentum_out,
    )
    input_grad = input_grad.reshape(inputs.shape)
    outputs = outputs.reshape(inputs.shape)
    gain_parts = jnp.concatenate([gain_pre, gain_middle, gain_late], 0)

    new_ffn, ffn_update, block_gram = ffn_gram(pair_grads, momentum, 0, ctx * small, earlier)
    new_weights_in, new_weights_out, new_ffn_weights, gain_every = newton(
        head_gram.reshape(ctx, -1, head, head),
        block_gram.reshape(ctx, small, FBLK, FBLK),
        gain_parts,
        head_update,
        weights_in,
        weights_out,
        ffn_update,
        ffn_mine,
        LEARN_RATE * (width / head) ** 0.5,
        LEARN_RATE * (width / FBLK) ** 0.5,
        fsdp,
    )
    gain_grad = jnp.sum(gain_every, 0)
    new_gain_first = BETA_ONE * gain_first + (1.0 - BETA_ONE) * gain_grad
    new_gain_second = BETA_TWO * gain_second + (1.0 - BETA_TWO) * gain_grad * gain_grad
    corrected_one = new_gain_first / (1.0 - BETA_ONE**STEP)
    corrected_two = new_gain_second / (1.0 - BETA_TWO**STEP)
    new_norm_gains = norm_gains - GAIN_RATE * corrected_one / (jnp.sqrt(corrected_two) + ADAM_EPS)
    return (
        outputs,
        input_grad,
        new_weights_in,
        new_weights_out,
        jnp.transpose(new_ffn_weights, (1, 0, 2)),
        momentum_new_in,
        momentum_new_out,
        jnp.transpose(new_ffn, (1, 0, 2)),
        new_norm_gains,
        new_gain_first,
        new_gain_second,
    )


def solution(mesh):
    return jax.shard_map(
        local,
        mesh=mesh,
        in_specs=(
            P("fsdp", "ctx", None),
            P("fsdp", "ctx", None),
            P("ctx", "fsdp", None),
            P("ctx", "fsdp", None),
            P("ctx", None, "fsdp"),
            P(),
            P("ctx", "fsdp", None),
            P("ctx", "fsdp", None),
            P("ctx", None, "fsdp"),
            P(),
            P(),
            P(),
        ),
        out_specs=(
            P("fsdp", "ctx", None),
            P("fsdp", "ctx", None),
            P("ctx", "fsdp", None),
            P("ctx", "fsdp", None),
            P("ctx", None, "fsdp"),
            P("ctx", "fsdp", None),
            P("ctx", "fsdp", None),
            P("ctx", None, "fsdp"),
            P(),
            P(),
            P(),
        ),
        check_vma=False,
    )
```

```python
import functools

import jax
import jax.numpy as jnp
from jax import lax
from jax.experimental import pallas as pl
from jax.experimental.pallas import tpu as pltpu
from jax.sharding import PartitionSpec as P

QUERY_HEADS = 8
KEY_VALUE_HEADS = 4
FBLK = 128
ITERS = 5
STEP = 10

SOFT_CAP = 50.0
EXP_SHIFT = 20.0
NORM_EPS = 1e-06
ROPE_THETA = 10000.0
MOMENTUM_DECAY = 0.95
LEARN_RATE = 0.3
WEIGHT_DECAY = 0.01
BETA_ONE = 0.9
BETA_TWO = 0.95
GAIN_RATE = 0.3
ADAM_EPS = 1e-08
NEWTON_A = 3.4445
NEWTON_B = -4.775
NEWTON_C = 2.0315
GELU_SCALE = 0.7978845608028654
GELU_CUBE = 0.044715
LOW = jnp.bfloat16
FULL = jnp.float32
SHRINK = 1.0 - LEARN_RATE * WEIGHT_DECAY
VMEM_LIMIT = 60 * 1024 * 1024


def rms_scale(values):
    return lax.rsqrt(jnp.mean(values * values, -1, keepdims=True) + NORM_EPS)


def positions_of(row_index, stretch_order, stretch_rows):
    stretch_slot = row_index // stretch_rows
    slot_table = jnp.arange(stretch_order.shape[0], dtype=jnp.int32)
    picked = jnp.sum(
        jnp.where(stretch_slot[:, None] == slot_table[None, :], stretch_order[None, :], 0), axis=1
    )
    return picked * stretch_rows + row_index % stretch_rows


def rope_tables(places, width):
    half_width = width // 2
    frequency = ROPE_THETA ** (-(2.0 * jnp.arange(half_width, dtype=jnp.float32)) / width)
    angles = places.astype(jnp.float32)[:, None] * frequency[None, :]
    return (jnp.cos(angles), jnp.sin(angles))


def rotate(values, cosine, sine):
    half = values.shape[-1] // 2
    first, second = values[..., :half], values[..., half:]
    return jnp.concatenate([first * cosine - second * sine, second * cosine + first * sine], -1)


def batched(left, right, left_dim, right_dim):
    return lax.dot_general(
        left, right, (((left_dim,), (right_dim,)), ((0,), (0,))), preferred_element_type=FULL
    )


def dot(left, right, left_dim, right_dim):
    return lax.dot_general(
        left, right, (((left_dim,), (right_dim,)), ((), ())), preferred_element_type=FULL
    )


def gram_kernel(blocks, grad_ref, old_ref, *refs):
    new_ref, update_ref, gram_ref = refs[-3:]
    grad = grad_ref[...].astype(FULL)
    new = MOMENTUM_DECAY * old_ref[0] + grad
    new_ref[0] = new
    update = (grad + MOMENTUM_DECAY * new).astype(LOW)
    update_ref[0] = update
    for block in range(blocks):
        piece = update[:, block * FBLK : (block + 1) * FBLK]
        gram_ref[block] = dot(piece, piece, 0, 0)


def ffn_gram(grads, momentum, first, blocks, earlier):
    _, rows, width = momentum.shape
    per_step = 6 if (width // FBLK) % 6 == 0 else 3
    span = per_step * FBLK
    steps = width // span
    spec = pl.BlockSpec((1, rows, span), lambda m, b: (m + first, 0, b))
    return pl.pallas_call(
        functools.partial(gram_kernel, per_step),
        grid=(grads.shape[1] // width, steps),
        in_specs=[pl.BlockSpec((rows, span), lambda m, b: (0, m * steps + b)), spec]
        + [ANY_SPEC] * len(earlier),
        out_specs=[
            spec,
            spec,
            pl.BlockSpec((per_step, FBLK, FBLK), lambda m, b: ((m + first) * steps + b, 0, 0)),
        ],
        out_shape=[
            jax.ShapeDtypeStruct(momentum.shape, FULL),
            jax.ShapeDtypeStruct(momentum.shape, LOW),
            jax.ShapeDtypeStruct((blocks, FBLK, FBLK), FULL),
        ],
        input_output_aliases={2 + index: index for index in range(len(earlier))},
        compiler_params=pltpu.CompilerParams(vmem_limit_bytes=VMEM_LIMIT),
        name="ffn_gram",
    )(grads, momentum, *earlier)


def split(values):
    high = values.astype(LOW)
    return high, (values - high.astype(FULL)).astype(LOW)


def fine_dot(left, right):
    (high, low), (right_high, right_low) = left, right
    return jnp.dot(
        jnp.concatenate([high, high, low], 1),
        jnp.concatenate([right_high, right_low, right_high], 0),
        preferred_element_type=FULL,
    )


def polys_of(grams):
    eyes = {}
    for gram in grams:
        rows, columns = grid_of(gram.shape[0])
        eyes[gram.shape[0]] = (rows == columns).astype(FULL)
    factors, totals = [], [None] * len(grams)
    for index, gram in enumerate(grams):
        eye = eyes[gram.shape[0]]
        trace = jnp.sum(jnp.sum(gram * eye, 0, keepdims=True), 1, keepdims=True)
        factors.append(1.0 / (jnp.sqrt(trace) + 1e-07))
        grams[index] = gram * (factors[index] * factors[index])
    for step in range(ITERS):
        parts = [split(gram) for gram in grams]
        squares = [fine_dot(part, part) for part in parts]
        quads = [
            NEWTON_A * eyes[gram.shape[0]] + NEWTON_B * gram + NEWTON_C * square
            for gram, square in zip(grams, squares)
        ]
        quad_parts = [split(quad) for quad in quads]
        totals = [
            quad if total is None else fine_dot(split(total), part)
            for total, quad, part in zip(totals, quads, quad_parts)
        ]
        if step < ITERS - 1:
            halves = [fine_dot(quad, part) for quad, part in zip(quad_parts, parts)]
            grams = [fine_dot(split(half), quad) for half, quad in zip(halves, quad_parts)]
    return [total * factor for total, factor in zip(totals, factors)]


def moved(update, poly):
    high, low = split(poly)
    return jnp.dot(
        jnp.concatenate([update, update], 1),
        jnp.concatenate([high, low], 0),
        preferred_element_type=FULL,
    )


def tile_of(size):
    return 768 if size % 768 == 0 else 384


def remote(source, target, send, receive, axis, to):
    return pltpu.make_async_remote_copy(
        src_ref=source,
        dst_ref=target,
        send_sem=send,
        recv_sem=receive,
        device_id={axis: to},
        device_id_type=pl.DeviceIdType.MESH,
    )


def greet(peers):
    barrier = pltpu.get_barrier_semaphore()
    for axis, to in peers:
        pl.semaphore_signal(
            barrier, inc=1, device_id={axis: to}, device_id_type=pl.DeviceIdType.MESH
        )
    pl.semaphore_wait(barrier, len(peers))


def line_greet(at, size):
    barrier = pltpu.get_barrier_semaphore()
    for ok, to in ((at > 0, at - 1), (at < size - 1, at + 1)):

        @pl.when(ok)
        def _(to=to):
            pl.semaphore_signal(
                barrier, inc=1, device_id={"fsdp": to}, device_id_type=pl.DeviceIdType.MESH
            )

    inside = (at > 0) & (at < size - 1)
    for ok, peers in ((inside, 2), (jnp.logical_not(inside), 1)):

        @pl.when(ok)
        def _(peers=peers):
            pl.semaphore_wait(barrier, peers)


class LineGather:
    def __init__(self, at, size, span, out, send, receive):
        self.at, self.size, self.span = at, size, span
        self.out, self.send_sem, self.receive_sem = out, send, receive

    def piece(self, owner, chunk):
        return self.out.at[owner, pl.ds(pl.multiple_of(chunk * self.span, self.span), self.span)]

    def copy(self, owner, chunk, side):
        piece = self.piece(owner, chunk)
        to = (self.at + (1 if side == 0 else self.size - 1)) % self.size
        return remote(
            piece,
            piece,
            self.send_sem.at[side, owner, chunk],
            self.receive_sem.at[owner, chunk],
            "fsdp",
            to,
        )

    def start(self, chunk):
        @pl.when(self.at < self.size - 1)
        def _():
            self.copy(self.at, chunk, 0).start()

        @pl.when(self.at > 0)
        def _():
            self.copy(self.at, chunk, 1).start()

    def forward(self, chunk, gap):
        at, size = self.at, self.size

        @pl.when(at >= gap)
        def _(owner=at - gap):
            copy = self.copy(owner, chunk, 0)
            copy.wait_recv()

            @pl.when(at < size - 1)
            def _():
                copy.start()

        @pl.when(at + gap < size)
        def _(owner=at + gap):
            copy = self.copy(owner, chunk, 1)
            copy.wait_recv()

            @pl.when(at > 0)
            def _():
                copy.start()

    def drain(self, chunk):
        at, size = self.at, self.size
        for gap in range(size):

            @pl.when((at >= gap) & (at < size - 1))
            def _(owner=at - gap):
                self.copy(owner, chunk, 0).wait_send()

            @pl.when((at + gap < size) & (at > 0))
            def _(owner=at + gap):
                self.copy(owner, chunk, 1).wait_send()


def cut_of(rows):
    return 16 * (-(-rows // 32)) if rows >= 32 else rows


class Square:
    def __init__(self, at, size):
        self.at, self.column = at, size // 4
        self.core, self.x, self.y = at % 2, (at // 2) % 2, at // 4
        self.sibling = at + 1 - 2 * self.core

    def device(self, j, turn, core=None):
        x = 1 - self.x if turn else self.x
        core = self.core if core is None else core
        return (((self.y + j) % self.column) * 2 + x) * 2 + core

    def others(self):
        return range(1, self.column)

    def back(self, j):
        return (self.column - j) % self.column


def ctx_peers(at, size):
    square = Square(at, size)
    peers = [square.sibling, square.device(0, True)]
    return [("ctx", to) for to in peers + [square.device(j, False) for j in square.others()]]


class CtxGather:
    def __init__(self, at, size, source, slot, axis, sems):
        self.square = Square(at, size)
        self.source, self.slot, self.axis = source, slot, axis
        self.send, self.receive, self.pass_send, self.pass_receive, self.own = sems
        rows = source.shape[axis]
        cut = cut_of(rows)
        self.halves = (0, 1) if cut < rows else (0,)
        self.bounds = ((0, cut), (cut, rows - cut))

    def half(self, view, h):
        first, count = self.bounds[h]
        return view.at[(slice(None),) * self.axis + (pl.ds(first, count),)]

    def block(self, j, turn, h, core=None):
        return self.half(self.slot(self.square.device(j, turn, core)), h)

    def copy(self, source, target, h, send, j, turn, to):
        return remote(
            source,
            target,
            self.send.at[h, send],
            self.receive.at[h, j, int(turn)],
            "ctx",
            to,
        )

    def direct(self, h, j):
        square = self.square
        return self.copy(
            self.half(self.source, h),
            self.half(self.slot(square.at), h),
            h,
            j,
            square.back(j),
            j == 0,
            square.device(j, j == 0),
        )

    def onward(self, h, j):
        square = self.square
        block = self.block(0, True, 0) if h == 0 else self.block(j, False, 1)
        to = square.device(j, False) if h == 0 else square.device(0, True)
        origin = square.back(j) if h == 0 else j
        return self.copy(block, block, h, square.column + j, origin, True, to)

    def arrival(self, h, j, turn):
        block = self.block(j, turn, h)
        return remote(
            block, block, self.send.at[h, 0], self.receive.at[h, j, int(turn)], "ctx", self.square.sibling
        )

    def across(self, h, j, turn):
        block = self.block(j, turn, h)
        sems = (self.pass_send.at[h, j, int(turn)], self.pass_receive.at[h, j, int(turn)])
        return remote(block, block, *sems, "ctx", self.square.sibling)

    def crossed(self, h, j, turn):
        block = self.block(j, turn, h, 1 - self.square.core)
        sems = (self.pass_send.at[h, j, int(turn)], self.pass_receive.at[h, j, int(turn)])
        return remote(block, block, *sems, "ctx", self.square.sibling)

    def mine(self, h):
        sems = (self.pass_send.at[h, 0, 0], self.pass_receive.at[h, 0, 0])
        target = self.half(self.slot(self.square.at), h)
        return remote(self.half(self.source, h), target, *sems, "ctx", self.square.sibling)

    def keep(self):
        return pltpu.make_async_copy(self.source, self.slot(self.square.at), self.own)

    def start(self):
        others, halves = self.square.others(), self.halves
        self.direct(0, 0).start()
        for j in others:
            self.direct(halves[-1], j).start()
        if len(halves) > 1:
            self.direct(1, 0).start()
            for j in others:
                self.direct(0, j).start()
        for h in halves:
            self.mine(h).start()
        self.keep().start()

    def land(self, h, j, turn):
        self.arrival(h, j, turn).wait_recv()
        self.across(h, j, turn).start()

    def forward(self):
        others, halves = self.square.others(), self.halves
        self.land(0, 0, True)
        for j in others:
            self.onward(0, j).start()
        if len(halves) > 1:
            for j in others:
                self.land(1, j, False)
                self.onward(1, j).start()

    def rest(self):
        others, halves = self.square.others(), self.halves
        if len(halves) > 1:
            self.land(1, 0, True)
        for j in others:
            self.land(0, j, False)
        for j in others:
            for h in halves:
                self.land(h, j, True)

    def finish(self):
        square, halves = self.square, self.halves
        for h in halves:
            for j in range(square.column):
                self.direct(h, j).wait_send()
                if j > 0:
                    self.onward(h, j).wait_send()
                for turn in (False, True):
                    self.crossed(h, j, turn).wait_recv()
                    if j > 0 or turn:
                        self.across(h, j, turn).wait_send()
            self.mine(h).wait_send()
        self.keep().wait()


def ctx_gather_sems(size):
    column = size // 4
    dma = pltpu.SemaphoreType.DMA
    return [dma((2, 2 * column)), dma((2, column, 2)), dma((2, column, 2)), dma((2, column, 2)), dma]


class CtxScatter:
    def __init__(self, at, size, part, first, hold, along_x, along_y, landed, sems):
        self.square = Square(at, size)
        self.part, self.first, self.hold = part, first, hold
        self.along_x, self.along_y, self.landed = along_x, along_y, landed
        self.near_send, self.near_receive, self.send, self.receive = sems
        self.step = 16 if first.dtype == LOW else 8
        rows = hold.shape[2]
        cut = cut_of(rows)
        self.bounds = ((0, cut), (cut, rows - cut))

    def index(self, j, turn):
        return j * 2 + int(turn)

    def near(self, j, turn):
        index = self.index(j, turn)
        return remote(
            self.part(self.square.device(j, turn, 1 - self.square.core)),
            self.first.at[index],
            self.near_send.at[index],
            self.near_receive.at[index],
            "ctx",
            self.square.sibling,
        )

    def half(self, view, h):
        return view.at[:, pl.ds(*self.bounds[h])]

    def far(self, kind, j):
        square, h = self.square, kind % 2
        if kind < 2:
            source = self.half(self.hold.at[self.index(j, True)], h)
            target = self.along_x.at[j - 1] if kind == 0 else self.along_y.at[square.back(j) - 1]
        elif kind < 4:
            source = self.half(self.hold.at[self.index(0, True)], h)
            target = self.half(self.landed.at[0], h)
        else:
            source = self.half(self.hold.at[self.index(j, False)], h)
            target = self.half(self.landed.at[square.back(j)], h)
        along_x = kind in (0, 2, 3)
        to = square.device(0, True) if along_x else square.device(j, False)
        return remote(
            source,
            target,
            self.send.at[kind, j],
            self.receive.at[kind, j if along_x else square.back(j)],
            "ctx",
            to,
        )

    def arrival(self, kind, j):
        h = kind % 2
        if kind < 2:
            block = (self.along_x if kind == 0 else self.along_y).at[j - 1]
        else:
            block = self.half(self.landed.at[0 if kind < 4 else j], h)
        return remote(
            block, block, self.send.at[kind, j], self.receive.at[kind, j], "ctx", self.square.sibling
        )

    def rows(self, first, count, body):
        def one(index, carried):
            offset = pl.multiple_of(index * self.step, self.step)
            for block in range(self.hold.shape[1]):
                body(block, offset)
            return carried

        lax.fori_loop(first // self.step, (first + count) // self.step, one, 0)

    def pair(self, j, turn):
        self.near(j, turn).wait_recv()
        index = self.index(j, turn)
        part = self.part(self.square.device(j, turn))

        def add(block, offset):
            rows = pl.ds(offset, self.step)
            total = part[block, rows, :].astype(FULL)
            total = total + self.first[index, block, rows, :].astype(FULL)
            self.hold[index, block, rows, :] = total.astype(self.hold.dtype)

        self.rows(0, self.hold.shape[2], add)

    def start(self):
        others = self.square.others()
        for j in others:
            self.near(j, True).start()
        self.near(0, True).start()
        for j in others:
            self.near(j, False).start()
        self.near(0, False).start()

    def diagonal(self):
        for j in self.square.others():
            self.pair(j, True)
            self.far(0, j).start()
            self.far(1, j).start()

    def neighbours(self):
        self.pair(0, True)
        self.far(2, 0).start()
        for j in self.square.others():
            self.pair(j, False)
            self.far(5, j).start()

    def add_passing(self, index, h, block_of):
        first, count = self.bounds[h]

        def add(block, offset):
            rows = pl.ds(offset, self.step)
            local = pl.ds(pl.multiple_of(offset - first, self.step), self.step)
            total = self.hold[index, block, rows, :].astype(FULL)
            for passing in block_of:
                total = total + passing[block, local, :].astype(FULL)
            self.hold[index, block, rows, :] = total.astype(self.hold.dtype)

        self.rows(first, count, add)

    def passing(self):
        others = self.square.others()
        for j in others:
            self.arrival(0, j).wait_recv()
            self.add_passing(self.index(j, False), 0, [self.along_x.at[j - 1]])
            self.far(4, j).start()
        for j in others:
            self.arrival(1, j).wait_recv()
        self.add_passing(self.index(0, True), 1, [self.along_y.at[j - 1] for j in others])
        self.far(3, 0).start()

    def finish(self, store):
        others = self.square.others()
        self.near(0, False).wait_recv()
        for kind in (2, 3):
            self.arrival(kind, 0).wait_recv()
        for j in others:
            for kind in (5, 4):
                self.arrival(kind, j).wait_recv()
        part = self.part(self.square.at)

        def add(block, offset):
            rows = pl.ds(offset, self.step)
            total = part[block, rows, :].astype(FULL) + self.first[0, block, rows, :].astype(FULL)
            for index in range(self.landed.shape[0]):
                total = total + self.landed[index, block, rows, :].astype(FULL)
            store(block, rows, total)

        self.rows(0, self.hold.shape[2], add)

    def drain(self):
        for j in range(self.square.column):
            for turn in (False, True):
                self.near(j, turn).wait_send()
        for kind in (2, 3):
            self.far(kind, 0).wait_send()
        for j in self.square.others():
            for kind in (0, 1, 4, 5):
                self.far(kind, j).wait_send()


SCATTER = 9


def ctx_scatter_scratch(size, blocks, rows, width, kind):
    chips, column = size // 2, size // 4
    cut = cut_of(rows)
    dma = pltpu.SemaphoreType.DMA
    return [
        pltpu.VMEM((chips, blocks, rows, width), kind),
        pltpu.VMEM((chips, blocks, rows, width), kind),
        pltpu.VMEM((column - 1, blocks, cut, width), kind),
        pltpu.VMEM((column - 1, blocks, rows - cut, width), kind),
        pltpu.VMEM((column, blocks, rows, width), kind),
        dma((chips,)),
        dma((chips,)),
        dma((6, column)),
        dma((6, column)),
    ]


def ctx_scatter(at, size, part, scratch):
    return CtxScatter(at, size, part, *scratch[:5], scratch[5:9])


def rows_of_ctx(ref):
    return lambda c: ref.at[pl.ds(c, 1)]


VMEM_SPEC = pl.BlockSpec(memory_space=pltpu.VMEM)
ANY_SPEC = pl.BlockSpec(memory_space=pl.ANY)


def head_places(fsdp):
    heads = QUERY_HEADS // fsdp
    pairs = max(1, KEY_VALUE_HEADS // fsdp)
    stored = (QUERY_HEADS + 2 * KEY_VALUE_HEADS) // fsdp
    places = []
    for user in range(fsdp):
        first = (user * heads) // (QUERY_HEADS // KEY_VALUE_HEADS)
        used = [user * heads + h for h in range(heads)]
        used += [QUERY_HEADS + first + p for p in range(pairs)]
        used += [QUERY_HEADS + KEY_VALUE_HEADS + first + p for p in range(pairs)]
        places.append([(matrix // stored, matrix % stored) for matrix in used])
    return places


def prepare_kernel(
    ctx, fsdp, in_ref, out_ref, ffn_ref, x_ref, gains, mine, out_all, ffn_low, normed, *scratch
):
    at, line_at = lax.axis_index("ctx"), lax.axis_index("fsdp")
    in_low, out_low, wide, wide_sem, move_send, move_receive = scratch[:6]
    places = head_places(fsdp)
    head = in_ref.shape[2]
    greet(ctx_peers(at, ctx) + [("fsdp", (line_at + k) % fsdp) for k in range(1, fsdp)])

    def move(user, slot):
        owner, index = places[user][slot]
        return remote(
            in_low.at[index],
            mine.at[:, pl.ds(slot * head, head)],
            move_send.at[user, slot],
            move_receive.at[slot],
            "fsdp",
            user,
        )

    def load(matrix):
        return pltpu.make_async_copy(
            ffn_ref.at[matrix], wide.at[matrix % 2], wide_sem.at[matrix % 2]
        )

    load(0).start()
    for index in range(in_ref.shape[1]):
        in_low[index] = in_ref[:, index, :].astype(LOW)
    for user in range(fsdp):
        for slot in range(len(places[0])):
            owner, index = places[user][slot]

            @pl.when(line_at == owner)
            def _(user=user, slot=slot, owner=owner, index=index):
                if user == owner:
                    mine[:, slot * head : (slot + 1) * head] = in_low[index]
                else:
                    move(user, slot).start()

    for index in range(out_ref.shape[1]):
        out_low[:, index * head : (index + 1) * head] = out_ref[:, index, :].astype(LOW)
    gather = CtxGather(at, ctx, out_low, lambda c: out_all.at[c], 0, scratch[6:11])
    gather.start()
    x = x_ref[...].astype(FULL)
    normed[...] = (x * rms_scale(x) * (1.0 + gains[0:1, :])).astype(LOW)
    for matrix in range(3):
        load(matrix).wait()
        if matrix < 2:
            load(matrix + 1).start()
        ffn_low[matrix] = wide[matrix % 2].astype(LOW)
    gather.forward()
    gather.rest()
    for user in range(fsdp):

        @pl.when(line_at == user)
        def _(user=user):
            for slot in range(len(places[0])):
                if places[user][slot][0] != user:
                    move(user, slot).wait_recv()

        for slot in range(len(places[0])):
            owner, index = places[user][slot]
            if user != owner:

                @pl.when(line_at == owner)
                def _(user=user, slot=slot):
                    move(user, slot).wait_send()

    gather.finish()


def prepare(weights_in, weights_out, ffn, x, gains, ctx, fsdp):
    local_rows, in_local, head = weights_in.shape
    out_local = weights_out.shape[1]
    mine = len(head_places(fsdp)[0])
    dma = pltpu.SemaphoreType.DMA
    return pl.pallas_call(
        functools.partial(prepare_kernel, ctx, fsdp),
        in_specs=[VMEM_SPEC] * 2 + [ANY_SPEC] + [VMEM_SPEC] * 2,
        out_specs=[VMEM_SPEC, ANY_SPEC, VMEM_SPEC, VMEM_SPEC],
        out_shape=[
            jax.ShapeDtypeStruct((local_rows, mine * head), LOW),
            jax.ShapeDtypeStruct((ctx, local_rows, out_local * head), LOW),
            jax.ShapeDtypeStruct(ffn.shape, LOW),
            jax.ShapeDtypeStruct(x.shape, LOW),
        ],
        scratch_shapes=[
            pltpu.VMEM((in_local, local_rows, head), LOW),
            pltpu.VMEM((local_rows, out_local * head), LOW),
            pltpu.VMEM((2,) + ffn.shape[1:], FULL),
            dma((2,)),
            dma((fsdp, mine)),
            dma((mine,)),
        ]
        + ctx_gather_sems(ctx),
        compiler_params=pltpu.CompilerParams(vmem_limit_bytes=VMEM_LIMIT, collective_id=0),
        name="prepare",
    )(weights_in, weights_out, ffn, x, gains)


def project_kernel(
    ctx, fsdp, span, heads, own, mine, cosine, sine, normed, in_all, query, key_all, value_all, *scratch
):
    at, line_at = lax.axis_index("ctx"), lax.axis_index("fsdp")
    key, value, low_send, low_receive = scratch[:4]
    tokens = own.shape[0]
    rows = key.shape[1]
    local_rows = mine.shape[0]
    head = 2 * cosine.shape[1]
    pairs = key.shape[2] // head
    chunks = tokens // span
    greet(ctx_peers(at, ctx) + [("fsdp", (line_at + k) % fsdp) for k in range(1, fsdp)])
    line = LineGather(line_at, fsdp, span, normed, low_send, low_receive)
    normed[line_at] = own[...]
    for chunk in range(chunks):
        line.start(chunk)
    step = 16

    def slot(c):
        return in_all.at[pl.ds(pl.multiple_of(c * local_rows, step), local_rows)]

    gather_in = CtxGather(at, ctx, mine, slot, 0, scratch[4:9])
    gather_in.start()
    for chunk in range(chunks):
        line.forward(chunk, 1)
    gather_in.forward()
    for gap in range(2, fsdp):
        for chunk in range(chunks):
            line.forward(chunk, gap)
    gather_in.rest()
    gather_in.finish()

    def projected(index, write, turn, scale):
        weights = in_all[:, index * head : (index + 1) * head]
        for sequence in range(fsdp):
            result = dot(normed[sequence], weights, 1, 0)
            if turn:
                first, second = result[:, : head // 2], result[:, head // 2 :]
                result = jnp.concatenate(
                    [
                        first * cosine[...] - second * sine[...],
                        second * cosine[...] + first * sine[...],
                    ],
                    1,
                )
            write(sequence, (result * scale).astype(LOW))

    per_device = tokens // rows
    for pair in range(pairs):
        columns = slice(pair * head, (pair + 1) * head)
        for matrix, target, turn in (
            (heads + pair, key, True),
            (heads + pairs + pair, value, False),
        ):

            def write(sequence, result, target=target, columns=columns):
                for inner in range(per_device):
                    target[sequence * per_device + inner, :, columns] = result[
                        inner * rows : (inner + 1) * rows
                    ]

            projected(matrix, write, turn, 1.0)

    keys = CtxGather(at, ctx, key, lambda c: key_all.at[:, c], 1, scratch[9:14])
    values = CtxGather(at, ctx, value, lambda c: value_all.at[:, c], 1, scratch[14:19])
    keys.start()
    values.start()
    for index in range(heads):

        def write(sequence, result, index=index):
            query[sequence * tokens : (sequence + 1) * tokens, index * head : (index + 1) * head] = result

        projected(index, write, True, head ** (-0.5))
    keys.forward()
    values.forward()
    keys.rest()
    values.rest()
    for chunk in range(chunks):
        line.drain(chunk)
    keys.finish()
    values.finish()


def project(own, mine, cosine, sine, sequences, heads, pairs, ctx, fsdp):
    tokens, width = own.shape
    local_rows = mine.shape[0]
    head = 2 * cosine.shape[1]
    rows = tokens // sequences
    chunks = 4
    dma = pltpu.SemaphoreType.DMA
    block = (fsdp * sequences, rows, pairs * head)
    spread = (fsdp * sequences, ctx, rows, pairs * head)
    return pl.pallas_call(
        functools.partial(project_kernel, ctx, fsdp, tokens // chunks, heads),
        in_specs=[VMEM_SPEC] * 4,
        out_specs=[VMEM_SPEC] * 3 + [ANY_SPEC] * 2,
        out_shape=[
            jax.ShapeDtypeStruct((fsdp, tokens, width), LOW),
            jax.ShapeDtypeStruct((ctx * local_rows, mine.shape[1]), LOW),
            jax.ShapeDtypeStruct((fsdp * tokens, heads * head), LOW),
            jax.ShapeDtypeStruct(spread, LOW),
            jax.ShapeDtypeStruct(spread, LOW),
        ],
        scratch_shapes=[
            pltpu.VMEM(block, LOW),
            pltpu.VMEM(block, LOW),
            dma((2, fsdp, chunks)),
            dma((fsdp, chunks)),
        ]
        + ctx_gather_sems(ctx) * 3,
        compiler_params=pltpu.CompilerParams(vmem_limit_bytes=VMEM_LIMIT, collective_id=1),
        name="project",
    )(own, mine, cosine, sine)


class LineExchange:
    def __init__(self, at, size, span, part, low_all, mid, scratch):
        self.at, self.size, self.span, self.part, self.mid = at, size, span, part, mid
        self.hold, self.landed, self.total, self.send, self.receive = scratch[:5]
        self.chunks = part.shape[1] // span
        self.low_all = low_all
        if low_all is not None:
            self.line = LineGather(at, size, span, low_all, *scratch[5:7])
        self.steps = self.chunks + (size - 1) * (1 if low_all is None else 2)

    def hop(self, source, target, chunk, side):
        to = (self.at + (1 if side == 0 else self.size - 1)) % self.size
        rows = pl.ds(pl.multiple_of(chunk * self.span, self.span), self.span)
        return remote(
            source.at[target, rows],
            self.landed.at[side, target, rows],
            self.send.at[target, chunk],
            self.receive.at[side, target, chunk],
            "fsdp",
            to,
        )

    def pass_on(self, target, chunk, side):
        rows = pl.ds(pl.multiple_of(chunk * self.span, self.span), self.span)
        origin = self.at == 0 if side == 0 else self.at == self.size - 1

        @pl.when(origin)
        def _():
            self.hop(self.part, target, chunk, side).start()

        @pl.when(jnp.logical_not(origin))
        def _():
            self.hop(self.part, target, chunk, side).wait_recv()
            added = self.part[target, rows, :].astype(FULL)
            added = added + self.landed[side, target, rows, :].astype(FULL)
            self.hold[target, rows, :] = added.astype(LOW)
            self.hop(self.hold, target, chunk, side).start()

    def step(self, index):
        at, size, chunks = self.at, self.size, self.chunks
        for gap in range(size - 1, 0, -1):
            chunk = index - at

            @pl.when((at + gap < size) & (chunk >= 0) & (chunk < chunks))
            def _(target=at + gap, chunk=chunk):
                self.pass_on(target, chunk, 0)

            chunk = index - (size - 1 - at)

            @pl.when((at >= gap) & (chunk >= 0) & (chunk < chunks))
            def _(target=at - gap, chunk=chunk):
                self.pass_on(target, chunk, 1)

        chunk = index - (size - 1)

        @pl.when((chunk >= 0) & (chunk < chunks))
        def _():
            rows = pl.ds(pl.multiple_of(chunk * self.span, self.span), self.span)
            self.total[...] = self.part[at, rows, :].astype(FULL)
            for side, ok in ((0, at > 0), (1, at < size - 1)):

                @pl.when(ok)
                def _(side=side):
                    self.hop(self.part, at, chunk, side).wait_recv()
                    self.total[...] += self.landed[side, at, rows, :].astype(FULL)

            low = self.mid(chunk, rows, self.total[...])
            if self.low_all is not None:
                self.low_all[at, rows, :] = low
                self.line.start(chunk)

        if self.low_all is not None:
            for gap in range(1, size):
                chunk = index - (size - 1) - gap

                @pl.when((chunk >= 0) & (chunk < chunks))
                def _(gap=gap, chunk=chunk):
                    self.line.forward(chunk, gap)

    def run(self, first, last):
        def one(index, carried):
            self.step(index)
            return carried

        lax.fori_loop(first, last, one, 0)

    def drain(self):
        at, size = self.at, self.size

        def one(chunk, carried):
            for gap in range(1, size):

                @pl.when(at + gap < size)
                def _(target=at + gap):
                    self.hop(self.part, target, chunk, 0).wait_send()

                @pl.when(at >= gap)
                def _(target=at - gap):
                    self.hop(self.part, target, chunk, 1).wait_send()

            if self.low_all is not None:
                self.line.drain(chunk)
            return carried

        lax.fori_loop(0, self.chunks, one, 0)


def line_span(tokens):
    return 16


def line_scratch(fsdp, tokens, width, gather):
    span = line_span(tokens)
    chunks = tokens // span
    dma = pltpu.SemaphoreType.DMA
    return [
        pltpu.VMEM((fsdp, tokens, width), LOW),
        pltpu.VMEM((2, fsdp, tokens, width), LOW),
        pltpu.VMEM((span, width), FULL),
        dma((fsdp, chunks)),
        dma((2, fsdp, chunks)),
    ] + ([dma((2, fsdp, chunks)), dma((fsdp, chunks))] if gather else [])


def exchange_kernel(mid, size, inputs, part, *refs):
    at = lax.axis_index("fsdp")
    ins, gains, low_all, refs = refs[:inputs], refs[inputs], refs[inputs + 1], refs[inputs + 2 :]
    outs, scratch = refs[:-7], refs[-7:]
    line_greet(at, size)
    line = LineExchange(
        at,
        size,
        line_span(part.shape[1]),
        part,
        low_all,
        lambda chunk, rows, total: mid(chunk, rows, total, ins, gains, outs),
        scratch,
    )
    line.run(0, line.steps)
    line.drain()


def exchange(part, ins, gains, mid, out_shape, fsdp, collective_id, name):
    _, tokens, width = part.shape
    return pl.pallas_call(
        functools.partial(exchange_kernel, mid, fsdp, len(ins)),
        in_specs=[VMEM_SPEC] * (len(ins) + 2),
        out_specs=[VMEM_SPEC] * (len(out_shape) + 1),
        out_shape=[jax.ShapeDtypeStruct(part.shape, LOW)] + out_shape,
        scratch_shapes=line_scratch(fsdp, tokens, width, True),
        compiler_params=pltpu.CompilerParams(
            vmem_limit_bytes=VMEM_LIMIT, collective_id=collective_id
        ),
        name=name,
    )(part, *ins, gains)


def spread(step, steps, work, body):
    def one(index, carried):
        body(index)
        return carried

    lax.fori_loop((step * work) // steps, ((step + 1) * work) // steps, one, 0)


class Copies:
    def __init__(self, copies):
        self.copies = [pltpu.make_async_copy(*copy) for copy in copies]

    def start(self):
        for copy in self.copies:
            copy.start()

    def wait(self):
        for copy in self.copies:
            copy.wait()


class Forward:
    def __init__(self, mid, weights, results, part, scratch):
        self.source, self.weights, self.results, self.part = mid, weights, results, part
        self.mid, self.hidden, self.pair, self.down = scratch[:4]
        self.pair_sem, self.down_sem, self.mid_sem, self.result_sem = scratch[4:8]
        self.outs = scratch[8:]
        self.sequences, self.tokens, _ = mid.shape
        self.half = self.tokens // 2
        self.span, self.reach = self.pair.shape[3], self.down.shape[1]
        self.tiles = weights.shape[2] // self.span
        self.ends = weights.shape[1] // self.reach
        self.count = self.tiles + self.ends

    def fetch_rows(self, half, s):
        return pltpu.make_async_copy(
            self.source.at[s, self.rows(half)],
            self.mid.at[half, pl.ds(s * self.half, self.half)],
            self.mid_sem.at[half, s],
        )

    def begin(self):
        for half in range(2):
            for s in range(self.sequences):
                self.fetch_rows(half, s).start()
        self.fetch(0)

    def give(self, index):
        return pltpu.make_async_copy(
            self.outs[index], self.results[index], self.result_sem.at[index]
        )

    def fetch_pair(self, half, tile):
        slot = (half * self.tiles + tile) % 2
        columns = pl.ds(pl.multiple_of(tile * self.span, self.span), self.span)
        return pltpu.make_async_copy(
            self.weights.at[pl.ds(0, 2), :, columns], self.pair.at[slot], self.pair_sem.at[slot]
        )

    def fetch_down(self, half, tile):
        slot = (half * self.ends + tile) % 2
        rows = pl.ds(pl.multiple_of(tile * self.reach, self.reach), self.reach)
        return pltpu.make_async_copy(
            self.weights.at[2, rows], self.down.at[slot], self.down_sem.at[slot]
        )

    def fetch(self, index):
        half, tile = index // self.count, index % self.count

        @pl.when(tile < self.tiles)
        def _():
            self.fetch_pair(half, tile).start()

        @pl.when(tile >= self.tiles)
        def _():
            self.fetch_down(half, tile - self.tiles).start()

    def rows(self, half):
        return pl.ds(pl.multiple_of(half * self.half, 16), self.half)

    def run(self, index):
        half, tile = index // self.count, index % self.count

        @pl.when(index + 1 < 2 * self.count)
        def _():
            self.fetch(index + 1)

        @pl.when(tile == 0)
        def _():
            for s in range(self.sequences):
                self.fetch_rows(half, s).wait()

        @pl.when(tile < self.tiles)
        def _():
            self.fetch_pair(half, tile).wait()
            slot = (half * self.tiles + tile) % 2
            mid = self.mid[half]
            gate = dot(mid, self.pair[slot, 0], 1, 0)
            up = dot(mid, self.pair[slot, 1], 1, 0)
            columns = pl.ds(pl.multiple_of(tile * self.span, self.span), self.span)
            results = [value.astype(LOW) for value in activate(gate, up)]
            self.hidden[half, :, columns] = results[0]
            for out, value in zip(self.outs, results):
                for sequence in range(self.sequences):
                    out[sequence, self.rows(half), columns] = value[
                        sequence * self.half : (sequence + 1) * self.half
                    ]

        @pl.when(tile >= self.tiles)
        def _():
            end = tile - self.tiles
            self.fetch_down(half, end).wait()
            slot = (half * self.ends + end) % 2
            value = dot(self.hidden[half], self.down[slot], 1, 1).astype(LOW)
            columns = pl.ds(pl.multiple_of(end * self.reach, self.reach), self.reach)
            for sequence in range(self.sequences):
                self.part[sequence, self.rows(half), columns] = value[
                    sequence * self.half : (sequence + 1) * self.half
                ]


def activate(gate, up):
    square = gate * gate
    squashed = jnp.tanh(GELU_SCALE * gate * (1.0 + GELU_CUBE * square))
    half = 0.5 + 0.5 * squashed
    act = gate * half
    slope = half + act * (1.0 - squashed) * (GELU_SCALE + 3.0 * GELU_SCALE * GELU_CUBE * square)
    return act * up, up * slope, act


def late_kernel(
    size, gains, mid, mixed_in, cotangent_in, weights,
    late, out, gain, hidden, gate_factor, up_factor, *scratch
):
    at = lax.axis_index("fsdp")
    line_greet(at, size)
    part, line_parts, (mixed, cotangent, side_sem) = scratch[0], scratch[1:8], scratch[8:11]
    line = LineExchange(
        at,
        size,
        line_span(part.shape[1]),
        part,
        late,
        lambda chunk, rows, total: late_mid(
            chunk, rows, total, (mixed, cotangent), gains, (out, gain)
        ),
        line_parts,
    )
    forward = Forward(mid, weights, (hidden, gate_factor, up_factor), part, scratch[11:])
    forward.begin()
    sides = [
        pltpu.make_async_copy(source, target, side_sem.at[index])
        for index, (source, target) in enumerate(((mixed_in, mixed), (cotangent_in, cotangent)))
    ]
    for copy in sides:
        copy.start()

    def one(index, carried):
        forward.run(index)
        return carried

    lax.fori_loop(0, forward.count, one, 0)
    for copy in sides:
        copy.wait()
    ahead = line.chunks // 2

    def both(index, carried):
        line.step(index)
        spread(index, ahead, forward.count, lambda tile: forward.run(forward.count + tile))
        return carried

    lax.fori_loop(0, ahead, both, 0)
    for index in range(3):
        forward.give(index).start()
    line.run(ahead, line.steps)
    line.drain()
    for index in range(3):
        forward.give(index).wait()


def late_exchange(mid, weights, mixed, cotangent, gains, collective_id):
    fsdp, tokens, width = mid.shape
    units = weights.shape[2]
    span, reach = tile_of(units), tile_of(width)
    rows = fsdp * tokens // 2
    dma = pltpu.SemaphoreType.DMA
    low = jax.ShapeDtypeStruct((fsdp, tokens, units), LOW)
    return pl.pallas_call(
        functools.partial(late_kernel, fsdp),
        in_specs=[VMEM_SPEC] + [ANY_SPEC] * 4,
        out_specs=[VMEM_SPEC] * 3 + [ANY_SPEC] * 3,
        out_shape=[
            jax.ShapeDtypeStruct(mid.shape, LOW),
            jax.ShapeDtypeStruct((tokens, width), LOW),
            jax.ShapeDtypeStruct((1, width), FULL),
            low,
            low,
            low,
        ],
        scratch_shapes=[pltpu.VMEM(mid.shape, LOW)]
        + line_scratch(fsdp, tokens, width, True)
        + [
            pltpu.VMEM((tokens, width), FULL),
            pltpu.VMEM((tokens, width), LOW),
            dma((2,)),
            pltpu.VMEM((2, rows, width), LOW),
            pltpu.VMEM((2, rows, units), LOW),
            pltpu.VMEM((2, 2, width, span), LOW),
            pltpu.VMEM((2, reach, units), LOW),
            dma((2,)),
            dma((2,)),
            dma((2, fsdp)),
            dma((3,)),
        ]
        + [pltpu.VMEM((fsdp, tokens, units), LOW)] * 3,
        compiler_params=pltpu.CompilerParams(
            vmem_limit_bytes=VMEM_LIMIT, collective_id=collective_id
        ),
        name="late_exchange",
    )(gains, mid, mixed, cotangent, weights)


class Backward:
    def __init__(self, late, mid, weights, factors, part, grads, scratch):
        self.weights, self.part, self.grads = weights, part, grads
        self.late, self.mid, self.factors = late, mid, factors
        self.rows_in, self.turned, self.pairs, self.wide, self.tall, self.stage = scratch[:6]
        self.wide_sem, self.tall_sem, self.stage_sem, self.row_sem, self.factor_sem = scratch[6:11]
        self.block, self.block_sem = scratch[11:13]
        self.own_factors = scratch[13:]
        self.sequences, self.tokens, self.width = late.shape
        self.half = self.tokens // 2
        self.span, self.reach = self.wide.shape[2], self.tall.shape[2]
        self.units = weights.shape[2]
        self.tiles = self.units // self.span
        self.ends = self.width // self.reach
        self.count = self.tiles + self.ends
        self.sums = 2 * self.units // self.stage.shape[2]
        self.pieces = 2 * self.ends
        self.work = self.sums * (self.width // 768)

    def rows(self, half):
        return pl.ds(pl.multiple_of(half * self.half, 16), self.half)

    def fetch_rows(self, half, s):
        return pltpu.make_async_copy(
            self.late.at[s, self.rows(half)],
            self.rows_in.at[half, pl.ds(s * self.half, self.half)],
            self.row_sem.at[half, s],
        )

    def begin(self):
        for half in range(2):
            for s in range(self.sequences):
                self.fetch_rows(half, s).start()
        self.fetch(0)
        self.fetch_block(0).start()

    def fetch_block(self, piece):
        half, block = piece // self.ends, piece % self.ends
        span = pl.ds(pl.multiple_of(block * self.reach, self.reach), self.reach)
        return Copies(
            (
                self.mid.at[s, self.rows(half), span],
                self.block.at[piece % 2, pl.ds(s * self.half, self.half)],
                self.block_sem.at[piece % 2, s],
            )
            for s in range(self.sequences)
        )

    def turn(self, piece):
        @pl.when(piece + 1 < self.pieces)
        def _():
            self.fetch_block(piece + 1).start()

        self.fetch_block(piece).wait()
        rows = self.sequences * self.half
        half, block = piece // self.ends, piece % self.ends
        span = pl.ds(pl.multiple_of(block * self.reach, self.reach), self.reach)
        columns = pl.ds(pl.multiple_of(half * rows, 128), rows)
        self.turned[span, columns] = self.block[piece % 2].T

    def fetch_wide(self, half, tile):
        slot = (half * self.tiles + tile) % 2
        columns = pl.ds(pl.multiple_of(tile * self.span, self.span), self.span)
        rows = self.rows(half)
        return Copies(
            [(self.weights.at[2, :, columns], self.wide.at[slot], self.wide_sem.at[slot])]
            + [
                (
                    self.factors[side].at[:, rows, columns],
                    self.own_factors[side].at[:, rows, columns],
                    self.factor_sem.at[slot, side],
                )
                for side in range(2)
            ]
        )

    def fetch_tall(self, half, tile):
        slot = (half * self.ends + tile) % 2
        rows = pl.ds(pl.multiple_of(tile * self.reach, self.reach), self.reach)
        return pltpu.make_async_copy(
            self.weights.at[pl.ds(0, 2), rows], self.tall.at[slot], self.tall_sem.at[slot]
        )

    def fetch(self, index):
        half, tile = index // self.count, index % self.count

        @pl.when(tile < self.tiles)
        def _():
            self.fetch_wide(half, tile).start()

        @pl.when(tile >= self.tiles)
        def _():
            self.fetch_tall(half, tile - self.tiles).start()

    def run(self, index):
        half, tile = index // self.count, index % self.count
        rows = self.rows(half)

        @pl.when(index + 1 < 2 * self.count)
        def _():
            self.fetch(index + 1)

        @pl.when(tile == 0)
        def _():
            for s in range(self.sequences):
                self.fetch_rows(half, s).wait()

        @pl.when(tile < self.tiles)
        def _():
            self.fetch_wide(half, tile).wait()
            slot = (half * self.tiles + tile) % 2
            hidden_grad = dot(self.rows_in[half], self.wide[slot], 1, 0)
            columns = pl.ds(pl.multiple_of(tile * self.span, self.span), self.span)
            for side, factor in enumerate(self.own_factors):
                target = pl.ds(
                    pl.multiple_of(side * self.units + tile * self.span, self.span), self.span
                )
                for s in range(self.sequences):
                    own = slice(s * self.half, (s + 1) * self.half)
                    value = hidden_grad[own] * factor[s, rows, columns].astype(FULL)
                    self.pairs[half, own, target] = value.astype(LOW)

        @pl.when(tile >= self.tiles)
        def _():
            end = tile - self.tiles
            self.fetch_tall(half, end).wait()
            slot = (half * self.ends + end) % 2
            value = dot(self.pairs[half, :, : self.units], self.tall[slot, 0], 1, 1)
            value = value + dot(self.pairs[half, :, self.units :], self.tall[slot, 1], 1, 1)
            value = value.astype(LOW)
            columns = pl.ds(pl.multiple_of(end * self.reach, self.reach), self.reach)
            for s in range(self.sequences):
                self.part[s, rows, columns] = value[s * self.half : (s + 1) * self.half]

    def put(self, index):
        span = self.stage.shape[2]
        columns = pl.ds(pl.multiple_of(index * span, span), span)
        return pltpu.make_async_copy(
            self.stage.at[index % 2], self.grads.at[:, columns], self.stage_sem.at[index % 2]
        )

    def sum(self, unit):
        thirds = self.width // 768
        index, third = unit // thirds, unit % thirds

        @pl.when((third == 0) & (index >= 2))
        def _():
            self.put(index - 2).wait()

        span = self.stage.shape[2]
        columns = pl.ds(pl.multiple_of(index * span, span), span)
        rows = self.sequences * self.half
        own = pl.ds(pl.multiple_of(third * 768, 768), 768)
        value = dot(self.turned[own, :rows], self.pairs[0, :, columns], 1, 0)
        value = value + dot(self.turned[own, rows:], self.pairs[1, :, columns], 1, 0)
        self.stage[index % 2, own, :] = value.astype(LOW)

        @pl.when(third == thirds - 1)
        def _():
            self.put(index).start()


def mid_kernel(
    size, gains, late, mixed_in, branch_in, cotangent_in, gate_factor, up_factor, mid, weights,
    low, mixed_grad, gain, grads, *scratch
):
    at = lax.axis_index("fsdp")
    line_greet(at, size)
    part, line_parts, sides = scratch[0], scratch[1:8], scratch[8:11]
    side_sem = scratch[11]
    line = LineExchange(
        at,
        size,
        line_span(part.shape[1]),
        part,
        low,
        lambda chunk, rows, total: mid_mid(
            chunk, rows, total, sides, gains, (mixed_grad, gain)
        ),
        line_parts,
    )
    backward = Backward(late, mid, weights, (gate_factor, up_factor), part, grads, scratch[12:])
    backward.begin()
    copies = [
        pltpu.make_async_copy(source, target, side_sem.at[index])
        for index, (source, target) in enumerate(zip((mixed_in, branch_in, cotangent_in), sides))
    ]
    for copy in copies:
        copy.start()

    def one(index, carried):
        backward.run(index)
        spread(index, backward.count, backward.pieces, backward.turn)
        return carried

    lax.fori_loop(0, backward.count, one, 0)
    for copy in copies:
        copy.wait()
    ahead = line.chunks // 2

    def both(index, carried):
        line.step(index)
        spread(index, ahead, backward.count, lambda tile: backward.run(backward.count + tile))
        return carried

    lax.fori_loop(0, ahead, both, 0)
    busy = 6

    def more(index, carried):
        line.step(ahead + index)
        spread(index, busy, backward.work, backward.sum)
        return carried

    lax.fori_loop(0, busy, more, 0)
    line.run(ahead + busy, line.steps)
    line.drain()
    backward.put(backward.sums - 2).wait()
    backward.put(backward.sums - 1).wait()


def mid_exchange(
    late, mid, mixed, branch, cotangent, gains, gate_factor, up_factor, weights, collective_id
):
    fsdp, tokens, width = mid.shape
    units = weights.shape[2]
    span, reach, stage = tile_of(units), 384, 384 if fsdp <= 4 else 256
    rows = fsdp * tokens // 2
    dma = pltpu.SemaphoreType.DMA
    return pl.pallas_call(
        functools.partial(mid_kernel, fsdp),
        in_specs=[VMEM_SPEC] + [ANY_SPEC] * 8,
        out_specs=[VMEM_SPEC] * 3 + [ANY_SPEC],
        out_shape=[
            jax.ShapeDtypeStruct(mid.shape, LOW),
            jax.ShapeDtypeStruct((tokens, width), FULL),
            jax.ShapeDtypeStruct((2, width), FULL),
            jax.ShapeDtypeStruct((width, 2 * units), LOW),
        ],
        scratch_shapes=[pltpu.VMEM(mid.shape, LOW)]
        + line_scratch(fsdp, tokens, width, True)
        + [
            pltpu.VMEM((tokens, width), FULL),
            pltpu.VMEM((tokens, width), FULL),
            pltpu.VMEM((tokens, width), LOW),
            dma((3,)),
            pltpu.VMEM((2, rows, width), LOW),
            pltpu.VMEM((width, 2 * rows), LOW),
            pltpu.VMEM((2, rows, 2 * units), LOW),
            pltpu.VMEM((2, width, span), LOW),
            pltpu.VMEM((2, 2, reach, units), LOW),
            pltpu.VMEM((2, width, stage), LOW),
            dma((2,)),
            dma((2,)),
            dma((2,)),
            dma((2, fsdp)),
            dma((2, 2)),
            pltpu.VMEM((2, rows, reach), LOW),
            dma((2, fsdp)),
        ]
        + [pltpu.VMEM((fsdp, tokens, units), LOW)] * 2,
        compiler_params=pltpu.CompilerParams(
            vmem_limit_bytes=VMEM_LIMIT, collective_id=collective_id
        ),
        name="mid_exchange",
    )(gains, late, mixed, branch, cotangent, gate_factor, up_factor, mid, weights)


def row_sum(values):
    return jnp.sum(values, 0, keepdims=True)


def add_gain(ref, chunk, index, values):
    @pl.when(chunk == 0)
    def _():
        ref[index : index + 1, :] = row_sum(values)

    @pl.when(chunk > 0)
    def _():
        ref[index : index + 1, :] += row_sum(values)


def branch_mid(chunk, rows, branch, ins, gains, outs):
    (x,), (branch_out, mixed_out) = ins, outs
    branch_out[rows, :] = branch
    post_hat = branch * rms_scale(branch)
    mixed = x[rows, :].astype(FULL) + post_hat * (1.0 + gains[1:2, :])
    mixed_out[rows, :] = mixed
    return (mixed * rms_scale(mixed) * (1.0 + gains[2:3, :])).astype(LOW)


def late_mid(chunk, rows, ffn_branch, ins, gains, outs):
    (mixed, cotangent), (out, gain) = ins, outs
    inv_late = rms_scale(ffn_branch)
    late_hat = ffn_branch * inv_late
    scale = 1.0 + gains[3:4, :]
    out[rows, :] = (mixed[rows, :] + late_hat * scale).astype(LOW)
    upstream = cotangent[rows, :].astype(FULL)
    add_gain(gain, chunk, 0, upstream * late_hat)
    scaled = upstream * scale
    grad = inv_late * (scaled - late_hat * jnp.mean(scaled * late_hat, -1, keepdims=True))
    return grad.astype(LOW)


def mid_mid(chunk, rows, mid_grad, ins, gains, outs):
    (mixed, branch, cotangent), (mixed_grad_out, gain) = ins, outs
    mixed = mixed[rows, :]
    inv_mid = rms_scale(mixed)
    mid_hat = mixed * inv_mid
    add_gain(gain, chunk, 1, mid_grad * mid_hat)
    scaled = mid_grad * (1.0 + gains[2:3, :])
    mixed_grad = cotangent[rows, :].astype(FULL) + inv_mid * (
        scaled - mid_hat * jnp.mean(scaled * mid_hat, -1, keepdims=True)
    )
    mixed_grad_out[rows, :] = mixed_grad
    branch = branch[rows, :]
    inv_post = rms_scale(branch)
    post_hat = branch * inv_post
    add_gain(gain, chunk, 0, mixed_grad * post_hat)
    hat = mixed_grad * (1.0 + gains[1:2, :])
    grad = inv_post * (hat - post_hat * jnp.mean(hat * post_hat, -1, keepdims=True))
    return grad.astype(LOW)


def pre_mid(chunk, rows, normed_grad, ins, gains, outs):
    (x, mixed_grad), (out, gain) = ins, outs
    x = x[rows, :].astype(FULL)
    inv_pre = rms_scale(x)
    normed = x * inv_pre
    add_gain(gain, chunk, 0, normed_grad * normed)
    scaled = normed_grad * (1.0 + gains[0:1, :])
    out[rows, :] = mixed_grad[rows, :] + inv_pre * (
        scaled - normed * jnp.mean(scaled * normed, -1, keepdims=True)
    )


def pair_sums_kernel(ctx, key, value, key_sum, value_sum, *scratch):
    at = lax.axis_index("ctx")
    greet(ctx_peers(at, ctx))
    keys = ctx_scatter(at, ctx, lambda c: key.at[:, c], scratch)
    values = ctx_scatter(at, ctx, lambda c: value.at[:, c], scratch[SCATTER:])
    keys.start()
    values.start()
    keys.diagonal()
    values.diagonal()
    keys.neighbours()
    values.neighbours()
    keys.passing()
    values.passing()
    for scatter, out in ((keys, key_sum), (values, value_sum)):

        def store(block, rows, total, out=out):
            out[block, rows, :] = total

        scatter.finish(store)
    keys.drain()
    values.drain()


def scatter_pairs(key, value):
    sequences, ctx, rows, width = key.shape
    return pl.pallas_call(
        functools.partial(pair_sums_kernel, ctx),
        in_specs=[VMEM_SPEC] * 2,
        out_specs=[VMEM_SPEC] * 2,
        out_shape=[jax.ShapeDtypeStruct((sequences, rows, width), FULL)] * 2,
        scratch_shapes=ctx_scatter_scratch(ctx, sequences, rows, width, LOW) * 2,
        compiler_params=pltpu.CompilerParams(vmem_limit_bytes=VMEM_LIMIT, collective_id=2),
        name="scatter_pairs",
    )(key, value)


def tail_kernel(
    ctx, fsdp, in_part, out_part, pre_part, x, mixed_grad, gains, in_old, out_old, *refs
):
    at, line_at = lax.axis_index("ctx"), lax.axis_index("fsdp")
    in_new, out_new, update, head_sum, input_grad, gain = refs[:6]
    scratch = refs[6:]
    places = head_places(fsdp)
    mine = len(places[0])
    scratch, others = scratch[: 2 * SCATTER], scratch[2 * SCATTER :]
    mine_sum, arrived, move_send, move_receive, out_sum = others[:5]
    gram, packed = others[10:12]
    head = arrived.shape[-1]
    greet(ctx_peers(at, ctx) + [("fsdp", (line_at + k) % fsdp) for k in range(1, fsdp)])
    ins = ctx_scatter(at, ctx, rows_of_ctx(in_part), scratch)
    outs = ctx_scatter(at, ctx, rows_of_ctx(out_part), scratch[SCATTER:])
    line = LineExchange(
        line_at,
        fsdp,
        line_span(pre_part.shape[1]),
        pre_part,
        None,
        lambda chunk, rows, total: pre_mid(
            chunk, rows, total, (x, mixed_grad), gains, (input_grad, gain)
        ),
        others[5:10],
    )
    ins.start()
    outs.start()
    ins.diagonal()
    ins.neighbours()
    line.run(0, 3)
    ins.passing()
    outs.diagonal()
    outs.neighbours()
    line.run(3, 6)
    outs.passing()
    line.run(6, 8)

    def store_in(block, rows, total):
        mine_sum[rows, :] = total.astype(LOW)

    def store_out(block, rows, total):
        out_sum[rows, :] = total

    ins.finish(store_in)

    def copies_of(owner, index):
        return [
            (user, slot)
            for user in range(fsdp)
            for slot in range(mine)
            if places[user][slot] == (owner, index)
        ]

    def move(user, slot):
        owner, index = places[user][slot]
        copy = copies_of(owner, index).index((user, slot))
        return remote(
            mine_sum.at[:, pl.ds(slot * head, head)],
            arrived.at[index, copy],
            move_send.at[slot],
            move_receive.at[index, copy],
            "fsdp",
            owner,
        )

    for user in range(fsdp):
        for slot in range(mine):

            @pl.when(line_at == user)
            def _(user=user, slot=slot):
                owner, index = places[user][slot]
                if owner == user:
                    copy = copies_of(owner, index).index((user, slot))
                    arrived[index, copy] = mine_sum[:, slot * head : (slot + 1) * head]
                else:
                    move(user, slot).start()

    line.run(8, line.steps)
    outs.finish(store_out)

    def step_of(index, grad, old_ref, new_ref, at):
        new = MOMENTUM_DECAY * old_ref[:, at, :] + grad
        new_ref[:, at, :] = new
        low = (grad + MOMENTUM_DECAY * new).astype(LOW)
        update[index] = low
        gram[index] = dot(low, low, 0, 0)

    stored = in_old.shape[1]
    for index in range(out_old.shape[1]):
        grad = out_sum[:, index * head : (index + 1) * head]
        step_of(stored + index, grad, out_old, out_new, index)
    for index in range(stored + out_old.shape[1], gram.shape[0]):
        gram[index] = jnp.zeros((head, head), FULL)
    for owner in range(fsdp):

        @pl.when(line_at == owner)
        def _(owner=owner):
            for index in range(stored):
                for user, slot in copies_of(owner, index):
                    if user != owner:
                        move(user, slot).wait_recv()

    for index in range(stored):
        grad = arrived[index, 0].astype(FULL)
        for copy in range(1, arrived.shape[1]):
            more = arrived[index, copy].astype(FULL)
            paired = line_at * stored + index >= QUERY_HEADS
            grad = grad + jnp.where(paired, more, 0.0)
        step_of(index, grad, in_old, in_new, index)
    large = gram.shape[0] // ctx
    edge = large * 2 * FBLK

    def pack_for(index, carried):
        packed[index, edge:, :] = jnp.zeros((packed.shape[1] - edge, FBLK), FULL)

        def write(first, rows):
            packed[index, first : first + rows.shape[0], :] = rows

        pack_all((0, None), (large, lambda i: gram[index * large + i]), write)
        return carried

    lax.fori_loop(0, ctx, pack_for, 0)
    heads = ctx_scatter(at, ctx, rows_of_ctx(packed), others[12:])
    heads.start()
    heads.diagonal()
    heads.neighbours()
    heads.passing()

    def store_head(block, rows, total):
        head_sum[rows, :] = total

    heads.finish(store_head)
    heads.drain()
    for user in range(fsdp):
        for slot in range(mine):
            if places[user][slot][0] != user:

                @pl.when(line_at == user)
                def _(user=user, slot=slot):
                    move(user, slot).wait_send()

    ins.drain()
    outs.drain()
    line.drain()


def tail(in_part, out_part, pre_part, x, mixed_grad, gains, in_old, out_old):
    _, stored, head = in_old.shape
    matrices = stored + out_old.shape[1]
    large = -(-matrices // in_part.shape[0])
    ctx, rows, in_width = in_part.shape
    out_width = out_part.shape[2]
    fsdp, tokens, width = pre_part.shape
    mine = len(head_places(fsdp)[0])
    copies = max(1, fsdp // KEY_VALUE_HEADS)
    dma = pltpu.SemaphoreType.DMA
    return pl.pallas_call(
        functools.partial(tail_kernel, ctx, fsdp),
        in_specs=[VMEM_SPEC] * 8,
        out_specs=[VMEM_SPEC] * 6,
        out_shape=[
            jax.ShapeDtypeStruct(in_old.shape, FULL),
            jax.ShapeDtypeStruct(out_old.shape, FULL),
            jax.ShapeDtypeStruct((matrices, rows, head), LOW),
            jax.ShapeDtypeStruct((packed_rows(0, large), FBLK), FULL),
            jax.ShapeDtypeStruct((tokens, width), FULL),
            jax.ShapeDtypeStruct((1, width), FULL),
        ],
        scratch_shapes=ctx_scatter_scratch(ctx, 1, rows, in_width, LOW)
        + ctx_scatter_scratch(ctx, 1, rows, out_width, LOW)
        + [
            pltpu.VMEM((rows, in_width), LOW),
            pltpu.VMEM((stored, copies, rows, head), LOW),
            dma((mine,)),
            dma((stored, copies)),
            pltpu.VMEM((rows, out_width), FULL),
        ]
        + line_scratch(fsdp, tokens, width, False)
        + [
            pltpu.VMEM((ctx * large, head, head), FULL),
            pltpu.VMEM((ctx, packed_rows(0, large), FBLK), FULL),
        ]
        + ctx_scatter_scratch(ctx, 1, packed_rows(0, large), FBLK, FULL),
        compiler_params=pltpu.CompilerParams(vmem_limit_bytes=VMEM_LIMIT, collective_id=3),
        name="tail",
    )(in_part, out_part, pre_part, x, mixed_grad, gains, in_old, out_old)


def packed_rows(small, large):
    squares = -(-small // 2)
    return squares * FBLK + large * 2 * FBLK + 16 * (-(-(squares + large) // 16))


def grid_of(size):
    rows = lax.broadcasted_iota(jnp.int32, (size, size), 0)
    return rows, lax.broadcasted_iota(jnp.int32, (size, size), 1)


def pack_two(first, second):
    rows, columns = grid_of(FBLK)
    if second is None:
        return first, jnp.zeros((1, FBLK), FULL)
    diagonal = jnp.sum(jnp.where(rows == columns, second, 0.0), 0, keepdims=True)
    return jnp.where(rows <= columns, first, second), diagonal


def unpack_two(square, diagonal, both):
    rows, columns = grid_of(FBLK)
    if not both:
        return square, None
    turned = square.T
    first = jnp.where(rows <= columns, square, turned)
    second = jnp.where(rows > columns, square, jnp.where(rows < columns, turned, diagonal))
    return first, second


def pack_all(blocks, heads, write):
    small, large = blocks[0], heads[0]
    squares = -(-small // 2)
    edge = squares * FBLK + large * 2 * FBLK
    for index in range(squares):
        second = blocks[1](2 * index + 1) if 2 * index + 1 < small else None
        square, diagonal = pack_two(blocks[1](2 * index), second)
        write(index * FBLK, square)
        write(edge + index, diagonal)
    for index in range(large):
        head = heads[1](index)
        square, diagonal = pack_two(head[:FBLK, :FBLK], head[FBLK:, FBLK:])
        base = squares * FBLK + index * 2 * FBLK
        write(base, square)
        write(base + FBLK, head[:FBLK, FBLK:])
        write(edge + squares + index, diagonal)


def unpack_all(small, large, read):
    squares = -(-small // 2)
    edge = squares * FBLK + large * 2 * FBLK
    blocks, heads = [], []
    for index in range(squares):
        both = 2 * index + 1 < small
        first, second = unpack_two(read(index * FBLK, FBLK), read(edge + index, 1), both)
        blocks += [first, second] if both else [first]
    for index in range(large):
        base = squares * FBLK + index * 2 * FBLK
        first, second = unpack_two(read(base, FBLK), read(edge + squares + index, 1), True)
        corner = read(base + FBLK, FBLK)
        heads.append(
            jnp.concatenate(
                [
                    jnp.concatenate([first, corner], 1),
                    jnp.concatenate([corner.T, second], 1),
                ],
                0,
            )
        )
    return blocks, heads


def newton_kernel(
    ctx, fsdp, large, head_rate, ffn_rate, heads, blocks, gains, head_update_in, in_old_in, out_old_in,
    ffn_update, ffn_old, in_new, out_new, ffn_new, gains_all, *scratch
):
    at, line_at = lax.axis_index("ctx"), lax.axis_index("fsdp")
    small = blocks.shape[1]
    packed, gram, poly, poly_all, gains_line, gains_sum, gain_send, gain_receive = scratch[:8]
    update, weights, update_sem, weight_sem, out_sem = scratch[8:13]
    head_update, in_old, out_old, side_sem = scratch[13:17]
    scratch = scratch[17:]
    sides = [
        pltpu.make_async_copy(source, target, side_sem.at[index])
        for index, (source, target) in enumerate(
            ((head_update_in, head_update), (in_old_in, in_old), (out_old_in, out_old))
        )
    ]
    matrices, _, width = weights.shape
    per_matrix = width // FBLK
    count = matrices * per_matrix
    greet(ctx_peers(at, ctx) + [("fsdp", (line_at + k) % fsdp) for k in range(1, fsdp)])

    def gain_copy(k):
        return remote(
            gains,
            gains_line.at[k],
            gain_send.at[k],
            gain_receive.at[k],
            "fsdp",
            (line_at + k) % fsdp,
        )

    def fetches(matrix):
        return [
            pltpu.make_async_copy(
                ffn_update.at[matrix], update.at[matrix], update_sem.at[matrix]
            ),
            pltpu.make_async_copy(ffn_old.at[matrix], weights.at[matrix], weight_sem.at[matrix]),
        ]

    for k in range(1, fsdp):
        gain_copy(k).start()
    edge = -(-small // 2) * FBLK

    def pack_for(index, carried):
        packed[index, edge:, :] = jnp.zeros((packed.shape[1] - edge, FBLK), FULL)

        def write(first, rows):
            packed[index, first : first + rows.shape[0], :] = rows

        pack_all((small, lambda i: blocks[index, i]), (0, None), write)
        return carried

    lax.fori_loop(0, ctx, pack_for, 0)
    scatter = ctx_scatter(at, ctx, rows_of_ctx(packed), scratch)
    scatter.start()
    for matrix in range(matrices):
        for copy in fetches(matrix):
            copy.start()
    for copy in sides:
        copy.start()
    scatter.diagonal()
    scatter.neighbours()
    _, head_grams = unpack_all(0, large, lambda first, count: heads[first : first + count, :])
    head_polys = polys_of(head_grams)
    scatter.passing()
    total = gains[...]
    for k in range(1, fsdp):
        gain_copy(k).wait_recv()
        total = total + gains_line[k]
    gains_sum[...] = total
    scratch = scratch[SCATTER:]
    gather_gains = CtxGather(at, ctx, gains_sum, lambda c: gains_all.at[c], 0, scratch[:5])
    gather = CtxGather(at, ctx, poly, lambda c: poly_all.at[c], 0, scratch[5:10])

    def store(block, rows, total):
        gram[rows, :] = total

    scatter.finish(store)
    gather_gains.start()
    block_grams, _ = unpack_all(small, 0, lambda first, count: gram[first : first + count, :])
    block_polys = polys_of(block_grams)
    last = edge + large * 2 * FBLK
    poly[last:, :] = jnp.zeros((poly.shape[0] - last, FBLK), FULL)

    def write(first, rows):
        poly[first : first + rows.shape[0], :] = rows

    pack_all((small, lambda i: block_polys[i]), (large, lambda i: head_polys[i]), write)
    gather.start()
    for matrix in range(matrices):
        for copy in fetches(matrix):
            copy.wait()

    def place(block):
        matrix = block // per_matrix
        columns = pl.ds(pl.multiple_of((block % per_matrix) * FBLK, FBLK), FBLK)
        return matrix, columns

    def put(block):
        matrix, columns = place(block)
        return pltpu.make_async_copy(
            weights.at[matrix, :, columns], ffn_new.at[matrix, :, columns], out_sem.at[block]
        )

    def apply(source, first):
        found, _ = unpack_all(small, 0, lambda row, count: source(row, count))
        for index, found_poly in enumerate(found):
            block = first * small + index

            @pl.when(block < count)
            def _(block=block, found_poly=found_poly):
                matrix, columns = place(block)
                step = moved(update[matrix, :, columns], found_poly)
                weights[matrix, :, columns] = weights[matrix, :, columns] * SHRINK - ffn_rate * step
                put(block).start()

    shift = large * 2 * FBLK

    def reader(view):
        edge_small = -(-small // 2) * FBLK

        def read(row, count):
            row = row + shift if row >= edge_small else row
            return view[row : row + count, :]

        return read

    apply(reader(poly), at)
    gather_gains.forward()
    gather.forward()
    gather_gains.rest()
    gather.rest()
    square = gather.square
    for j in range(square.column):
        for turn in (False, True):
            if j > 0 or turn:
                device = square.device(j, turn)
                apply(reader(poly_all.at[device]), device)
    for k in range(1, fsdp):
        gain_copy(k).wait_send()
    gather_gains.finish()
    gather.finish()
    for j in range(square.column):
        for turn in (False, True):
            device = square.device(j, turn, 1 - square.core)
            apply(reader(poly_all.at[device]), device)
    stored = in_old.shape[1]
    for copy in sides:
        copy.wait()
    for device in range(ctx):
        first = device * large
        if first < head_update.shape[0]:
            _, found = unpack_all(
                small, large, lambda row, count: poly_all[device, row : row + count, :]
            )
            for index in range(first, min(first + large, head_update.shape[0])):
                step = head_rate * moved(head_update[index], found[index - first])
                if index < stored:
                    in_new[:, index, :] = in_old[:, index, :] * SHRINK - step
                else:
                    out_new[:, index - stored, :] = out_old[:, index - stored, :] * SHRINK - step
    scatter.drain()

    def finish(block, carried):
        put(block).wait()
        return carried

    lax.fori_loop(0, count, finish, 0)


def newton(
    heads, blocks, gains, head_update, in_old, out_old, ffn_update, ffn_old, head_rate, ffn_rate, fsdp
):
    ctx, small = blocks.shape[:2]
    large = -(-head_update.shape[0] // ctx)
    rows, block_rows = packed_rows(small, large), packed_rows(small, 0)
    dma = pltpu.SemaphoreType.DMA
    matrices = ffn_old.shape[0]
    return pl.pallas_call(
        functools.partial(newton_kernel, ctx, fsdp, large, head_rate, ffn_rate),
        in_specs=[VMEM_SPEC] * 3 + [ANY_SPEC] * 5,
        out_specs=[VMEM_SPEC] * 2 + [ANY_SPEC, VMEM_SPEC],
        out_shape=[
            jax.ShapeDtypeStruct(in_old.shape, FULL),
            jax.ShapeDtypeStruct(out_old.shape, FULL),
            jax.ShapeDtypeStruct(ffn_old.shape, FULL),
            jax.ShapeDtypeStruct((ctx,) + gains.shape, FULL),
        ],
        scratch_shapes=[
            pltpu.VMEM((ctx, block_rows, FBLK), FULL),
            pltpu.VMEM((block_rows, FBLK), FULL),
            pltpu.VMEM((rows, FBLK), FULL),
            pltpu.VMEM((ctx, rows, FBLK), FULL),
            pltpu.VMEM((fsdp,) + gains.shape, FULL),
            pltpu.VMEM(gains.shape, FULL),
            dma((fsdp,)),
            dma((fsdp,)),
            pltpu.VMEM(ffn_update.shape, LOW),
            pltpu.VMEM(ffn_old.shape, FULL),
            dma((matrices,)),
            dma((matrices,)),
            dma((ctx * small,)),
            pltpu.VMEM(head_update.shape, LOW),
            pltpu.VMEM(in_old.shape, FULL),
            pltpu.VMEM(out_old.shape, FULL),
            dma((3,)),
        ]
        + ctx_scatter_scratch(ctx, 1, block_rows, FBLK, FULL)
        + ctx_gather_sems(ctx) * 2,
        compiler_params=pltpu.CompilerParams(vmem_limit_bytes=VMEM_LIMIT, collective_id=4),
        name="newton",
    )(heads, blocks, gains, head_update, in_old, out_old, ffn_update, ffn_old)


def local(
    inputs,
    cotangent,
    weights_in,
    weights_out,
    ffn_weights,
    norm_gains,
    momentum_in,
    momentum_out,
    ffn_momentum,
    gain_first,
    gain_second,
    stretch_order,
):
    sequences, rows, width = inputs.shape
    stretch_rows = rows // 2
    local_rows, in_local, head = weights_in.shape
    out_local = weights_out.shape[1]
    ffn_local = ffn_weights.shape[2]
    ctx, fsdp = lax.axis_size("ctx"), lax.axis_size("fsdp")
    ctx_at = lax.axis_index("ctx")
    tokens = sequences * rows
    all_sequences = sequences * fsdp
    heads = QUERY_HEADS // fsdp
    pairs = max(1, KEY_VALUE_HEADS // fsdp)
    shared = heads // pairs
    mine = heads + 2 * pairs

    ffn_mine = jnp.transpose(ffn_weights, (1, 0, 2))

    flat = inputs.reshape(tokens, width)
    mine_in, w_out, ffn_cut, own_normed = prepare(
        weights_in, weights_out, ffn_mine, flat, norm_gains, ctx, fsdp
    )
    ffn_low = lax.all_gather(ffn_cut, "ctx", axis=1, tiled=True)
    own_places = positions_of(
        ctx_at * rows + jnp.arange(rows, dtype=jnp.int32), stretch_order, stretch_rows
    )
    all_places = positions_of(
        jnp.arange(ctx * rows, dtype=jnp.int32), stretch_order, stretch_rows
    )
    cosine, sine = rope_tables(own_places, head)
    normed_low, w_in, query, key_all, value_all = project(
        own_normed,
        mine_in,
        jnp.tile(cosine, (sequences, 1)),
        jnp.tile(sine, (sequences, 1)),
        sequences,
        heads,
        pairs,
        ctx,
        fsdp,
    )
    normed_low = normed_low.reshape(fsdp * tokens, width)
    w_out = w_out.reshape(width, out_local * head)
    cosine, sine = jnp.tile(cosine, (all_sequences, 1)), jnp.tile(sine, (all_sequences, 1))
    scale = head ** (-0.5)

    def column(values, index):
        return values[:, index * head : (index + 1) * head]

    def by_sequence(columns):
        return jnp.concatenate([c.reshape(all_sequences, rows, head) for c in columns], 1)

    def flat_heads(values, count):
        return [
            values[:, g * rows : (g + 1) * rows].reshape(all_sequences * rows, head)
            for g in range(count)
        ]

    def heads_of(pair):
        return range(pair * shared, (pair + 1) * shared)

    query = [by_sequence([column(query, h) for h in heads_of(pair)]) for pair in range(pairs)]
    key_all = key_all.reshape(all_sequences, ctx * rows, pairs * head)
    value_all = value_all.reshape(all_sequences, ctx * rows, pairs * head)
    key_of = [key_all[:, :, p * head : (p + 1) * head] for p in range(pairs)]
    value_of = [value_all[:, :, p * head : (p + 1) * head] for p in range(pairs)]
    visible = jnp.tile(all_places[None, :] <= own_places[:, None], (shared, 1))[None]
    exponent, slope, exponent_low, row_total, attended = [], [], [], [], []
    for p in range(pairs):
        scores = batched(query[p], key_of[p], 2, 2)
        squashed = jnp.tanh(scores / SOFT_CAP)
        exponent.append(jnp.where(visible, jnp.exp(SOFT_CAP * squashed - EXP_SHIFT), 0.0))
        slope.append(exponent[p] * (1.0 - squashed * squashed))
        row_total.append(jnp.sum(exponent[p], -1, keepdims=True))
        exponent_low.append(exponent[p].astype(LOW))
        attended.append(batched(exponent_low[p], value_of[p], 2, 1) / row_total[p])
    attended_low = jnp.concatenate(
        sum([flat_heads(attended[p].astype(LOW), shared) for p in range(pairs)], []), 1
    )

    def parts(values):
        return values.astype(LOW).reshape(fsdp, tokens, width)

    full_rows = jax.ShapeDtypeStruct((tokens, width), FULL)
    low_rows = jax.ShapeDtypeStruct((tokens, width), LOW)

    def gain_rows(count):
        return jax.ShapeDtypeStruct((count, width), FULL)

    upstream = cotangent.reshape(tokens, width)
    mid_low, branch, mixed = exchange(
        parts(dot(attended_low, w_out, 1, 1)),
        [flat],
        norm_gains,
        branch_mid,
        [full_rows, full_rows],
        fsdp,
        5,
        "branch_exchange",
    )

    late_low, outputs, gain_late, hidden_low, gate_factor, up_factor = late_exchange(
        mid_low, ffn_low, mixed, upstream, norm_gains, 6
    )
    down_grads = lax.psum_scatter(
        dot(
            late_low.reshape(fsdp * tokens, width),
            hidden_low.reshape(fsdp * tokens, ffn_local),
            0,
            0,
        ).astype(LOW),
        "ctx",
        scatter_dimension=0,
        tiled=True,
    )
    branch_low, mixed_grad, gain_middle, pair_part = mid_exchange(
        late_low, mid_low, mixed, branch, upstream, norm_gains, gate_factor, up_factor, ffn_low, 7
    )
    pair_grads = lax.psum_scatter(pair_part, "ctx", scatter_dimension=0, tiled=True)

    branch_low = branch_low.reshape(fsdp * tokens, width)
    attended_grad = dot(branch_low, w_out, 1, 0)
    query_grad, key_part, value_part = [], [], []
    for p in range(pairs):
        grad = by_sequence([column(attended_grad, h) for h in heads_of(p)])
        numerator_low = (grad / row_total[p]).astype(LOW)
        row_term = jnp.sum(grad * attended[p], -1, keepdims=True) / row_total[p]
        pulled = batched(numerator_low, value_of[p], 2, 2)
        score_low = (slope[p] * (pulled - row_term)).astype(LOW)
        query_grad += flat_heads(batched(score_low, key_of[p], 2, 1), shared)
        key_part.append(batched(score_low, query[p], 1, 1).astype(LOW))
        value_part.append(batched(exponent_low[p], numerator_low, 1, 1).astype(LOW))
    spread = (all_sequences, ctx, rows, pairs * head)
    key_grad, value_grad = scatter_pairs(
        jnp.concatenate(key_part, 2).reshape(spread), jnp.concatenate(value_part, 2).reshape(spread)
    )
    key_grad = key_grad.reshape(all_sequences * rows, pairs * head)
    value_grad = value_grad.reshape(all_sequences * rows, pairs * head)
    projected_grad = jnp.concatenate(
        [rotate(grad * scale, cosine, -sine) for grad in query_grad]
        + [rotate(column(key_grad, p), cosine, -sine) for p in range(pairs)]
        + [value_grad],
        1,
    ).astype(LOW)
    momentum = jnp.transpose(ffn_momentum, (1, 0, 2))
    small = -(-3 * (ffn_local // FBLK) // ctx)
    earlier = ffn_gram(down_grads, momentum, 2, ctx * small, [])
    momentum_new_in, momentum_new_out, head_update, head_sum, input_grad, gain_pre = tail(
        dot(normed_low, projected_grad, 0, 0).astype(LOW).reshape(ctx, local_rows, mine * head),
        dot(branch_low, attended_low, 0, 0).astype(LOW).reshape(ctx, local_rows, out_local * head),
        parts(dot(projected_grad, w_in, 1, 1)),
        flat,
        mixed_grad,
        norm_gains,
        momentum_in,
        momentum_out,
    )
    input_grad = input_grad.reshape(inputs.shape)
    outputs = outputs.reshape(inputs.shape)
    gain_parts = jnp.concatenate([gain_pre, gain_middle, gain_late], 0)

    new_ffn, ffn_update, block_gram = ffn_gram(pair_grads, momentum, 0, ctx * small, earlier)
    new_weights_in, new_weights_out, new_ffn_weights, gain_every = newton(
        head_sum,
        block_gram.reshape(ctx, small, FBLK, FBLK),
        gain_parts,
        head_update,
        weights_in,
        weights_out,
        ffn_update,
        ffn_mine,
        LEARN_RATE * (width / head) ** 0.5,
        LEARN_RATE * (width / FBLK) ** 0.5,
        fsdp,
    )
    gain_grad = jnp.sum(gain_every, 0)
    new_gain_first = BETA_ONE * gain_first + (1.0 - BETA_ONE) * gain_grad
    new_gain_second = BETA_TWO * gain_second + (1.0 - BETA_TWO) * gain_grad * gain_grad
    corrected_one = new_gain_first / (1.0 - BETA_ONE**STEP)
    corrected_two = new_gain_second / (1.0 - BETA_TWO**STEP)
    new_norm_gains = norm_gains - GAIN_RATE * corrected_one / (jnp.sqrt(corrected_two) + ADAM_EPS)
    return (
        outputs,
        input_grad,
        new_weights_in,
        new_weights_out,
        jnp.transpose(new_ffn_weights, (1, 0, 2)),
        momentum_new_in,
        momentum_new_out,
        jnp.transpose(new_ffn, (1, 0, 2)),
        new_norm_gains,
        new_gain_first,
        new_gain_second,
    )


def solution(mesh):
    return jax.shard_map(
        local,
        mesh=mesh,
        in_specs=(
            P("fsdp", "ctx", None),
            P("fsdp", "ctx", None),
            P("ctx", "fsdp", None),
            P("ctx", "fsdp", None),
            P("ctx", None, "fsdp"),
            P(),
            P("ctx", "fsdp", None),
            P("ctx", "fsdp", None),
            P("ctx", None, "fsdp"),
            P(),
            P(),
            P(),
        ),
        out_specs=(
            P("fsdp", "ctx", None),
            P("fsdp", "ctx", None),
            P("ctx", "fsdp", None),
            P("ctx", "fsdp", None),
            P("ctx", None, "fsdp"),
            P("ctx", "fsdp", None),
            P("ctx", "fsdp", None),
            P("ctx", None, "fsdp"),
            P(),
            P(),
            P(),
        ),
        check_vma=False,
    )
```

```python
import functools

import jax
import jax.numpy as jnp
from jax import lax
from jax.experimental import pallas as pl
from jax.experimental.pallas import tpu as pltpu
from jax.sharding import PartitionSpec as P

QUERY_HEADS = 8
KEY_VALUE_HEADS = 4
FBLK = 128
ITERS = 5
STEP = 10

SOFT_CAP = 50.0
EXP_SHIFT = 20.0
NORM_EPS = 1e-06
ROPE_THETA = 10000.0
MOMENTUM_DECAY = 0.95
LEARN_RATE = 0.3
WEIGHT_DECAY = 0.01
BETA_ONE = 0.9
BETA_TWO = 0.95
GAIN_RATE = 0.3
ADAM_EPS = 1e-08
NEWTON_A = 3.4445
NEWTON_B = -4.775
NEWTON_C = 2.0315
GELU_SCALE = 0.7978845608028654
GELU_CUBE = 0.044715
LOW = jnp.bfloat16
FULL = jnp.float32
SHRINK = 1.0 - LEARN_RATE * WEIGHT_DECAY
VMEM_LIMIT = 60 * 1024 * 1024


def rms_scale(values):
    return lax.rsqrt(jnp.mean(values * values, -1, keepdims=True) + NORM_EPS)


def positions_of(row_index, stretch_order, stretch_rows):
    stretch_slot = row_index // stretch_rows
    slot_table = jnp.arange(stretch_order.shape[0], dtype=jnp.int32)
    picked = jnp.sum(
        jnp.where(stretch_slot[:, None] == slot_table[None, :], stretch_order[None, :], 0), axis=1
    )
    return picked * stretch_rows + row_index % stretch_rows


def rope_tables(places, width):
    half_width = width // 2
    frequency = ROPE_THETA ** (-(2.0 * jnp.arange(half_width, dtype=jnp.float32)) / width)
    angles = places.astype(jnp.float32)[:, None] * frequency[None, :]
    return (jnp.cos(angles), jnp.sin(angles))


def rotate(values, cosine, sine):
    half = values.shape[-1] // 2
    first, second = values[..., :half], values[..., half:]
    return jnp.concatenate([first * cosine - second * sine, second * cosine + first * sine], -1)


def batched(left, right, left_dim, right_dim):
    return lax.dot_general(
        left, right, (((left_dim,), (right_dim,)), ((0,), (0,))), preferred_element_type=FULL
    )


def dot(left, right, left_dim, right_dim):
    return lax.dot_general(
        left, right, (((left_dim,), (right_dim,)), ((), ())), preferred_element_type=FULL
    )


def gram_kernel(blocks, grad_ref, old_ref, *refs):
    new_ref, update_ref, gram_ref = refs[-3:]
    grad = grad_ref[...].astype(FULL)
    new = MOMENTUM_DECAY * old_ref[0] + grad
    new_ref[0] = new
    update = (grad + MOMENTUM_DECAY * new).astype(LOW)
    update_ref[0] = update
    for block in range(blocks):
        piece = update[:, block * FBLK : (block + 1) * FBLK]
        gram_ref[block] = dot(piece, piece, 0, 0)


def ffn_gram(grads, momentum, first, blocks, earlier):
    _, rows, width = momentum.shape
    per_step = 6 if (width // FBLK) % 6 == 0 else 3
    span = per_step * FBLK
    steps = width // span
    spec = pl.BlockSpec((1, rows, span), lambda m, b: (m + first, 0, b))
    return pl.pallas_call(
        functools.partial(gram_kernel, per_step),
        grid=(grads.shape[1] // width, steps),
        in_specs=[pl.BlockSpec((rows, span), lambda m, b: (0, m * steps + b)), spec]
        + [ANY_SPEC] * len(earlier),
        out_specs=[
            spec,
            spec,
            pl.BlockSpec((per_step, FBLK, FBLK), lambda m, b: ((m + first) * steps + b, 0, 0)),
        ],
        out_shape=[
            jax.ShapeDtypeStruct(momentum.shape, FULL),
            jax.ShapeDtypeStruct(momentum.shape, LOW),
            jax.ShapeDtypeStruct((blocks, FBLK, FBLK), FULL),
        ],
        input_output_aliases={2 + index: index for index in range(len(earlier))},
        compiler_params=pltpu.CompilerParams(vmem_limit_bytes=VMEM_LIMIT),
        name="ffn_gram",
    )(grads, momentum, *earlier)


def split(values):
    high = values.astype(LOW)
    return high, (values - high.astype(FULL)).astype(LOW)


def fine_dot(left, right):
    (high, low), (right_high, right_low) = left, right
    return jnp.dot(
        jnp.concatenate([high, high, low], 1),
        jnp.concatenate([right_high, right_low, right_high], 0),
        preferred_element_type=FULL,
    )


def polys_of(grams):
    eyes = {}
    for gram in grams:
        rows, columns = grid_of(gram.shape[0])
        eyes[gram.shape[0]] = (rows == columns).astype(FULL)
    factors, totals = [], [None] * len(grams)
    for index, gram in enumerate(grams):
        eye = eyes[gram.shape[0]]
        trace = jnp.sum(jnp.sum(gram * eye, 0, keepdims=True), 1, keepdims=True)
        factors.append(1.0 / (jnp.sqrt(trace) + 1e-07))
        grams[index] = gram * (factors[index] * factors[index])
    for step in range(ITERS):
        parts = [split(gram) for gram in grams]
        squares = [fine_dot(part, part) for part in parts]
        quads = [
            NEWTON_A * eyes[gram.shape[0]] + NEWTON_B * gram + NEWTON_C * square
            for gram, square in zip(grams, squares)
        ]
        quad_parts = [split(quad) for quad in quads]
        totals = [
            quad if total is None else fine_dot(split(total), part)
            for total, quad, part in zip(totals, quads, quad_parts)
        ]
        if step < ITERS - 1:
            halves = [fine_dot(quad, part) for quad, part in zip(quad_parts, parts)]
            grams = [fine_dot(split(half), quad) for half, quad in zip(halves, quad_parts)]
    return [total * factor for total, factor in zip(totals, factors)]


def moved(update, poly):
    high, low = split(poly)
    return jnp.dot(
        jnp.concatenate([update, update], 1),
        jnp.concatenate([high, low], 0),
        preferred_element_type=FULL,
    )


def tile_of(size):
    return 768 if size % 768 == 0 else 384


def remote(source, target, send, receive, axis, to):
    return pltpu.make_async_remote_copy(
        src_ref=source,
        dst_ref=target,
        send_sem=send,
        recv_sem=receive,
        device_id={axis: to},
        device_id_type=pl.DeviceIdType.MESH,
    )


def call(peers):
    barrier = pltpu.get_barrier_semaphore()
    for axis, to in peers:
        pl.semaphore_signal(
            barrier, inc=1, device_id={axis: to}, device_id_type=pl.DeviceIdType.MESH
        )


def greet(peers):
    call(peers)
    pl.semaphore_wait(pltpu.get_barrier_semaphore(), len(peers))


def line_greet(at, size):
    barrier = pltpu.get_barrier_semaphore()
    for ok, to in ((at > 0, at - 1), (at < size - 1, at + 1)):

        @pl.when(ok)
        def _(to=to):
            pl.semaphore_signal(
                barrier, inc=1, device_id={"fsdp": to}, device_id_type=pl.DeviceIdType.MESH
            )

    inside = (at > 0) & (at < size - 1)
    for ok, peers in ((inside, 2), (jnp.logical_not(inside), 1)):

        @pl.when(ok)
        def _(peers=peers):
            pl.semaphore_wait(barrier, peers)


class LineGather:
    def __init__(self, at, size, span, out, send, receive):
        self.at, self.size, self.span = at, size, span
        self.out, self.send_sem, self.receive_sem = out, send, receive

    def piece(self, owner, chunk):
        return self.out.at[owner, pl.ds(pl.multiple_of(chunk * self.span, self.span), self.span)]

    def copy(self, owner, chunk, side):
        piece = self.piece(owner, chunk)
        to = (self.at + (1 if side == 0 else self.size - 1)) % self.size
        return remote(
            piece,
            piece,
            self.send_sem.at[side, owner, chunk],
            self.receive_sem.at[owner, chunk],
            "fsdp",
            to,
        )

    def start(self, chunk):
        @pl.when(self.at < self.size - 1)
        def _():
            self.copy(self.at, chunk, 0).start()

        @pl.when(self.at > 0)
        def _():
            self.copy(self.at, chunk, 1).start()

    def forward(self, chunk, gap):
        at, size = self.at, self.size

        @pl.when(at >= gap)
        def _(owner=at - gap):
            copy = self.copy(owner, chunk, 0)
            copy.wait_recv()

            @pl.when(at < size - 1)
            def _():
                copy.start()

        @pl.when(at + gap < size)
        def _(owner=at + gap):
            copy = self.copy(owner, chunk, 1)
            copy.wait_recv()

            @pl.when(at > 0)
            def _():
                copy.start()

    def drain(self, chunk):
        at, size = self.at, self.size
        for gap in range(size):

            @pl.when((at >= gap) & (at < size - 1))
            def _(owner=at - gap):
                self.copy(owner, chunk, 0).wait_send()

            @pl.when((at + gap < size) & (at > 0))
            def _(owner=at + gap):
                self.copy(owner, chunk, 1).wait_send()


def cut_of(rows):
    return 16 * (-(-rows // 32)) if rows >= 32 else rows


class Square:
    def __init__(self, at, size):
        self.at, self.column = at, size // 4
        self.core, self.x, self.y = at % 2, (at // 2) % 2, at // 4
        self.sibling = at + 1 - 2 * self.core

    def device(self, j, turn, core=None):
        x = 1 - self.x if turn else self.x
        core = self.core if core is None else core
        return (((self.y + j) % self.column) * 2 + x) * 2 + core

    def others(self):
        return range(1, self.column)

    def back(self, j):
        return (self.column - j) % self.column


def ctx_peers(at, size):
    square = Square(at, size)
    peers = [square.sibling, square.device(0, True)]
    return [("ctx", to) for to in peers + [square.device(j, False) for j in square.others()]]


class CtxGather:
    def __init__(self, at, size, source, slot, axis, sems):
        self.square = Square(at, size)
        self.source, self.slot, self.axis = source, slot, axis
        self.send, self.receive, self.pass_send, self.pass_receive, self.own = sems
        rows = source.shape[axis]
        cut = cut_of(rows)
        self.halves = (0, 1) if cut < rows else (0,)
        self.bounds = ((0, cut), (cut, rows - cut))

    def half(self, view, h):
        first, count = self.bounds[h]
        return view.at[(slice(None),) * self.axis + (pl.ds(first, count),)]

    def block(self, j, turn, h, core=None):
        return self.half(self.slot(self.square.device(j, turn, core)), h)

    def copy(self, source, target, h, send, j, turn, to):
        return remote(
            source,
            target,
            self.send.at[h, send],
            self.receive.at[h, j, int(turn)],
            "ctx",
            to,
        )

    def direct(self, h, j):
        square = self.square
        return self.copy(
            self.half(self.source, h),
            self.half(self.slot(square.at), h),
            h,
            j,
            square.back(j),
            j == 0,
            square.device(j, j == 0),
        )

    def onward(self, h, j):
        square = self.square
        block = self.block(0, True, 0) if h == 0 else self.block(j, False, 1)
        to = square.device(j, False) if h == 0 else square.device(0, True)
        origin = square.back(j) if h == 0 else j
        return self.copy(block, block, h, square.column + j, origin, True, to)

    def arrival(self, h, j, turn):
        block = self.block(j, turn, h)
        return remote(
            block, block, self.send.at[h, 0], self.receive.at[h, j, int(turn)], "ctx", self.square.sibling
        )

    def across(self, h, j, turn):
        block = self.block(j, turn, h)
        sems = (self.pass_send.at[h, j, int(turn)], self.pass_receive.at[h, j, int(turn)])
        return remote(block, block, *sems, "ctx", self.square.sibling)

    def crossed(self, h, j, turn):
        block = self.block(j, turn, h, 1 - self.square.core)
        sems = (self.pass_send.at[h, j, int(turn)], self.pass_receive.at[h, j, int(turn)])
        return remote(block, block, *sems, "ctx", self.square.sibling)

    def mine(self, h):
        sems = (self.pass_send.at[h, 0, 0], self.pass_receive.at[h, 0, 0])
        target = self.half(self.slot(self.square.at), h)
        return remote(self.half(self.source, h), target, *sems, "ctx", self.square.sibling)

    def keep(self):
        return pltpu.make_async_copy(self.source, self.slot(self.square.at), self.own)

    def start(self):
        others, halves = self.square.others(), self.halves
        self.direct(0, 0).start()
        for j in others:
            self.direct(halves[-1], j).start()
        if len(halves) > 1:
            self.direct(1, 0).start()
            for j in others:
                self.direct(0, j).start()
        for h in halves:
            self.mine(h).start()
        self.keep().start()

    def land(self, h, j, turn):
        self.arrival(h, j, turn).wait_recv()
        self.across(h, j, turn).start()

    def forward(self):
        others, halves = self.square.others(), self.halves
        self.land(0, 0, True)
        for j in others:
            self.onward(0, j).start()
        if len(halves) > 1:
            for j in others:
                self.land(1, j, False)
                self.onward(1, j).start()

    def rest(self):
        others, halves = self.square.others(), self.halves
        if len(halves) > 1:
            self.land(1, 0, True)
        for j in others:
            self.land(0, j, False)
        for j in others:
            for h in halves:
                self.land(h, j, True)

    def finish(self):
        square, halves = self.square, self.halves
        for h in halves:
            for j in range(square.column):
                self.direct(h, j).wait_send()
                if j > 0:
                    self.onward(h, j).wait_send()
                for turn in (False, True):
                    self.crossed(h, j, turn).wait_recv()
                    if j > 0 or turn:
                        self.across(h, j, turn).wait_send()
            self.mine(h).wait_send()
        self.keep().wait()


def ctx_gather_sems(size):
    column = size // 4
    dma = pltpu.SemaphoreType.DMA
    return [dma((2, 2 * column)), dma((2, column, 2)), dma((2, column, 2)), dma((2, column, 2)), dma]


class CtxScatter:
    def __init__(self, at, size, part, first, hold, along_x, along_y, landed, sems):
        self.square = Square(at, size)
        self.part, self.first, self.hold = part, first, hold
        self.along_x, self.along_y, self.landed = along_x, along_y, landed
        self.near_send, self.near_receive, self.send, self.receive = sems
        self.step = 16 if first.dtype == LOW else 8
        rows = hold.shape[2]
        cut = cut_of(rows)
        self.bounds = ((0, cut), (cut, rows - cut))

    def index(self, j, turn):
        return j * 2 + int(turn)

    def near(self, j, turn):
        index = self.index(j, turn)
        return remote(
            self.part(self.square.device(j, turn, 1 - self.square.core)),
            self.first.at[index],
            self.near_send.at[index],
            self.near_receive.at[index],
            "ctx",
            self.square.sibling,
        )

    def half(self, view, h):
        return view.at[:, pl.ds(*self.bounds[h])]

    def far(self, kind, j):
        square, h = self.square, kind % 2
        if kind < 2:
            source = self.half(self.hold.at[self.index(j, True)], h)
            target = self.along_x.at[j - 1] if kind == 0 else self.along_y.at[square.back(j) - 1]
        elif kind < 4:
            source = self.half(self.hold.at[self.index(0, True)], h)
            target = self.half(self.landed.at[0], h)
        else:
            source = self.half(self.hold.at[self.index(j, False)], h)
            target = self.half(self.landed.at[square.back(j)], h)
        along_x = kind in (0, 2, 3)
        to = square.device(0, True) if along_x else square.device(j, False)
        return remote(
            source,
            target,
            self.send.at[kind, j],
            self.receive.at[kind, j if along_x else square.back(j)],
            "ctx",
            to,
        )

    def arrival(self, kind, j):
        h = kind % 2
        if kind < 2:
            block = (self.along_x if kind == 0 else self.along_y).at[j - 1]
        else:
            block = self.half(self.landed.at[0 if kind < 4 else j], h)
        return remote(
            block, block, self.send.at[kind, j], self.receive.at[kind, j], "ctx", self.square.sibling
        )

    def rows(self, first, count, body):
        def one(index, carried):
            offset = pl.multiple_of(index * self.step, self.step)
            for block in range(self.hold.shape[1]):
                body(block, offset)
            return carried

        lax.fori_loop(first // self.step, (first + count) // self.step, one, 0)

    def pair(self, j, turn):
        self.near(j, turn).wait_recv()
        index = self.index(j, turn)
        part = self.part(self.square.device(j, turn))

        def add(block, offset):
            rows = pl.ds(offset, self.step)
            total = part[block, rows, :].astype(FULL)
            total = total + self.first[index, block, rows, :].astype(FULL)
            self.hold[index, block, rows, :] = total.astype(self.hold.dtype)

        self.rows(0, self.hold.shape[2], add)

    def start(self):
        others = self.square.others()
        for j in others:
            self.near(j, True).start()
        self.near(0, True).start()
        for j in others:
            self.near(j, False).start()
        self.near(0, False).start()

    def diagonal(self):
        for j in self.square.others():
            self.pair(j, True)
            self.far(0, j).start()
            self.far(1, j).start()

    def neighbours(self):
        self.pair(0, True)
        self.far(2, 0).start()
        for j in self.square.others():
            self.pair(j, False)
            self.far(5, j).start()

    def add_passing(self, index, h, block_of):
        first, count = self.bounds[h]

        def add(block, offset):
            rows = pl.ds(offset, self.step)
            local = pl.ds(pl.multiple_of(offset - first, self.step), self.step)
            total = self.hold[index, block, rows, :].astype(FULL)
            for passing in block_of:
                total = total + passing[block, local, :].astype(FULL)
            self.hold[index, block, rows, :] = total.astype(self.hold.dtype)

        self.rows(first, count, add)

    def passing(self):
        others = self.square.others()
        for j in others:
            self.arrival(0, j).wait_recv()
            self.add_passing(self.index(j, False), 0, [self.along_x.at[j - 1]])
            self.far(4, j).start()
        for j in others:
            self.arrival(1, j).wait_recv()
        self.add_passing(self.index(0, True), 1, [self.along_y.at[j - 1] for j in others])
        self.far(3, 0).start()

    def finish(self, store):
        others = self.square.others()
        self.near(0, False).wait_recv()
        for kind in (2, 3):
            self.arrival(kind, 0).wait_recv()
        for j in others:
            for kind in (5, 4):
                self.arrival(kind, j).wait_recv()
        part = self.part(self.square.at)

        def add(block, offset):
            rows = pl.ds(offset, self.step)
            total = part[block, rows, :].astype(FULL) + self.first[0, block, rows, :].astype(FULL)
            for index in range(self.landed.shape[0]):
                total = total + self.landed[index, block, rows, :].astype(FULL)
            store(block, rows, total)

        self.rows(0, self.hold.shape[2], add)

    def drain(self):
        for j in range(self.square.column):
            for turn in (False, True):
                self.near(j, turn).wait_send()
        for kind in (2, 3):
            self.far(kind, 0).wait_send()
        for j in self.square.others():
            for kind in (0, 1, 4, 5):
                self.far(kind, j).wait_send()


SCATTER = 9


def ctx_scatter_scratch(size, blocks, rows, width, kind):
    chips, column = size // 2, size // 4
    cut = cut_of(rows)
    dma = pltpu.SemaphoreType.DMA
    return [
        pltpu.VMEM((chips, blocks, rows, width), kind),
        pltpu.VMEM((chips, blocks, rows, width), kind),
        pltpu.VMEM((column - 1, blocks, cut, width), kind),
        pltpu.VMEM((column - 1, blocks, rows - cut, width), kind),
        pltpu.VMEM((column, blocks, rows, width), kind),
        dma((chips,)),
        dma((chips,)),
        dma((6, column)),
        dma((6, column)),
    ]


def ctx_scatter(at, size, part, scratch):
    return CtxScatter(at, size, part, *scratch[:5], scratch[5:9])


def rows_of_ctx(ref):
    return lambda c: ref.at[pl.ds(c, 1)]


VMEM_SPEC = pl.BlockSpec(memory_space=pltpu.VMEM)
ANY_SPEC = pl.BlockSpec(memory_space=pl.ANY)


def head_places(fsdp):
    heads = QUERY_HEADS // fsdp
    pairs = max(1, KEY_VALUE_HEADS // fsdp)
    stored = (QUERY_HEADS + 2 * KEY_VALUE_HEADS) // fsdp
    places = []
    for user in range(fsdp):
        first = (user * heads) // (QUERY_HEADS // KEY_VALUE_HEADS)
        used = [user * heads + h for h in range(heads)]
        used += [QUERY_HEADS + first + p for p in range(pairs)]
        used += [QUERY_HEADS + KEY_VALUE_HEADS + first + p for p in range(pairs)]
        places.append([(matrix // stored, matrix % stored) for matrix in used])
    return places


def prepare_kernel(
    ctx, fsdp, in_ref, out_ref, ffn_ref, x_ref, gains, mine, out_all, ffn_low, normed, *scratch
):
    at, line_at = lax.axis_index("ctx"), lax.axis_index("fsdp")
    in_low, out_low, wide, wide_sem, move_send, move_receive = scratch[:6]
    cast, cast_sem = scratch[11:]
    places = head_places(fsdp)
    head = in_ref.shape[2]
    peers = ctx_peers(at, ctx) + [("fsdp", (line_at + k) % fsdp) for k in range(1, fsdp)]
    call(peers)

    def move(user, slot):
        owner, index = places[user][slot]
        return remote(
            in_low.at[index],
            mine.at[:, pl.ds(slot * head, head)],
            move_send.at[user, slot],
            move_receive.at[slot],
            "fsdp",
            user,
        )

    def load(matrix):
        return pltpu.make_async_copy(
            ffn_ref.at[matrix], wide.at[matrix % 2], wide_sem.at[matrix % 2]
        )

    def give(matrix):
        return pltpu.make_async_copy(cast.at[matrix], ffn_low.at[matrix], cast_sem.at[matrix])

    load(0).start()
    load(1).start()
    for index in range(in_ref.shape[1]):
        in_low[index] = in_ref[:, index, :].astype(LOW)
    for index in range(out_ref.shape[1]):
        out_low[:, index * head : (index + 1) * head] = out_ref[:, index, :].astype(LOW)
    pl.semaphore_wait(pltpu.get_barrier_semaphore(), len(peers))
    for user in range(fsdp):
        for slot in range(len(places[0])):
            owner, index = places[user][slot]

            @pl.when(line_at == owner)
            def _(user=user, slot=slot, owner=owner, index=index):
                if user == owner:
                    mine[:, slot * head : (slot + 1) * head] = in_low[index]
                else:
                    move(user, slot).start()

    gather = CtxGather(at, ctx, out_low, lambda c: out_all.at[c], 0, scratch[6:11])
    gather.start()
    for matrix in range(3):
        load(matrix).wait()
        cast[matrix] = wide[matrix % 2].astype(LOW)
        give(matrix).start()
        if matrix == 0:
            load(2).start()
    x = x_ref[...].astype(FULL)
    normed[...] = (x * rms_scale(x) * (1.0 + gains[0:1, :])).astype(LOW)
    gather.forward()
    gather.rest()
    for user in range(fsdp):

        @pl.when(line_at == user)
        def _(user=user):
            for slot in range(len(places[0])):
                if places[user][slot][0] != user:
                    move(user, slot).wait_recv()

        for slot in range(len(places[0])):
            owner, index = places[user][slot]
            if user != owner:

                @pl.when(line_at == owner)
                def _(user=user, slot=slot):
                    move(user, slot).wait_send()

    gather.finish()
    for matrix in range(3):
        give(matrix).wait()


def prepare(weights_in, weights_out, ffn, x, gains, ctx, fsdp):
    local_rows, in_local, head = weights_in.shape
    out_local = weights_out.shape[1]
    mine = len(head_places(fsdp)[0])
    dma = pltpu.SemaphoreType.DMA
    return pl.pallas_call(
        functools.partial(prepare_kernel, ctx, fsdp),
        in_specs=[VMEM_SPEC] * 2 + [ANY_SPEC] + [VMEM_SPEC] * 2,
        out_specs=[VMEM_SPEC, ANY_SPEC, ANY_SPEC, VMEM_SPEC],
        out_shape=[
            jax.ShapeDtypeStruct((local_rows, mine * head), LOW),
            jax.ShapeDtypeStruct((ctx, local_rows, out_local * head), LOW),
            jax.ShapeDtypeStruct(ffn.shape, LOW),
            jax.ShapeDtypeStruct(x.shape, LOW),
        ],
        scratch_shapes=[
            pltpu.VMEM((in_local, local_rows, head), LOW),
            pltpu.VMEM((local_rows, out_local * head), LOW),
            pltpu.VMEM((2,) + ffn.shape[1:], FULL),
            dma((2,)),
            dma((fsdp, mine)),
            dma((mine,)),
        ]
        + ctx_gather_sems(ctx)
        + [pltpu.VMEM(ffn.shape, LOW), dma((3,))],
        compiler_params=pltpu.CompilerParams(vmem_limit_bytes=VMEM_LIMIT, collective_id=0),
        name="prepare",
    )(weights_in, weights_out, ffn, x, gains)


def project_kernel(
    ctx, fsdp, span, heads, own, mine, cosine, sine, normed, in_all, query, key_all, value_all, *scratch
):
    at, line_at = lax.axis_index("ctx"), lax.axis_index("fsdp")
    key, value, low_send, low_receive = scratch[:4]
    tokens = own.shape[0]
    rows = key.shape[1]
    local_rows = mine.shape[0]
    head = 2 * cosine.shape[1]
    pairs = key.shape[2] // head
    chunks = tokens // span
    greet(ctx_peers(at, ctx) + [("fsdp", (line_at + k) % fsdp) for k in range(1, fsdp)])
    line = LineGather(line_at, fsdp, span, normed, low_send, low_receive)
    normed[line_at] = own[...]
    for chunk in range(chunks):
        line.start(chunk)
    step = 16

    def slot(c):
        return in_all.at[pl.ds(pl.multiple_of(c * local_rows, step), local_rows)]

    gather_in = CtxGather(at, ctx, mine, slot, 0, scratch[4:9])
    gather_in.start()
    for chunk in range(chunks):
        line.forward(chunk, 1)
    gather_in.forward()
    for gap in range(2, fsdp):
        for chunk in range(chunks):
            line.forward(chunk, gap)
    gather_in.rest()
    gather_in.finish()

    def projected(index, write, turn, scale):
        weights = in_all[:, index * head : (index + 1) * head]
        for sequence in range(fsdp):
            result = dot(normed[sequence], weights, 1, 0)
            if turn:
                first, second = result[:, : head // 2], result[:, head // 2 :]
                result = jnp.concatenate(
                    [
                        first * cosine[...] - second * sine[...],
                        second * cosine[...] + first * sine[...],
                    ],
                    1,
                )
            write(sequence, (result * scale).astype(LOW))

    per_device = tokens // rows
    for pair in range(pairs):
        columns = slice(pair * head, (pair + 1) * head)
        for matrix, target, turn in (
            (heads + pair, key, True),
            (heads + pairs + pair, value, False),
        ):

            def write(sequence, result, target=target, columns=columns):
                for inner in range(per_device):
                    target[sequence * per_device + inner, :, columns] = result[
                        inner * rows : (inner + 1) * rows
                    ]

            projected(matrix, write, turn, 1.0)

    keys = CtxGather(at, ctx, key, lambda c: key_all.at[:, c], 1, scratch[9:14])
    values = CtxGather(at, ctx, value, lambda c: value_all.at[:, c], 1, scratch[14:19])
    keys.start()
    values.start()
    for index in range(heads):

        def write(sequence, result, index=index):
            query[sequence * tokens : (sequence + 1) * tokens, index * head : (index + 1) * head] = result

        projected(index, write, True, head ** (-0.5))
    keys.forward()
    values.forward()
    keys.rest()
    values.rest()
    for chunk in range(chunks):
        line.drain(chunk)
    keys.finish()
    values.finish()


def project(own, mine, cosine, sine, sequences, heads, pairs, ctx, fsdp):
    tokens, width = own.shape
    local_rows = mine.shape[0]
    head = 2 * cosine.shape[1]
    rows = tokens // sequences
    chunks = 4
    dma = pltpu.SemaphoreType.DMA
    block = (fsdp * sequences, rows, pairs * head)
    spread = (fsdp * sequences, ctx, rows, pairs * head)
    return pl.pallas_call(
        functools.partial(project_kernel, ctx, fsdp, tokens // chunks, heads),
        in_specs=[VMEM_SPEC] * 4,
        out_specs=[VMEM_SPEC] * 3 + [ANY_SPEC] * 2,
        out_shape=[
            jax.ShapeDtypeStruct((fsdp, tokens, width), LOW),
            jax.ShapeDtypeStruct((ctx * local_rows, mine.shape[1]), LOW),
            jax.ShapeDtypeStruct((fsdp * tokens, heads * head), LOW),
            jax.ShapeDtypeStruct(spread, LOW),
            jax.ShapeDtypeStruct(spread, LOW),
        ],
        scratch_shapes=[
            pltpu.VMEM(block, LOW),
            pltpu.VMEM(block, LOW),
            dma((2, fsdp, chunks)),
            dma((fsdp, chunks)),
        ]
        + ctx_gather_sems(ctx) * 3,
        compiler_params=pltpu.CompilerParams(vmem_limit_bytes=VMEM_LIMIT, collective_id=1),
        name="project",
    )(own, mine, cosine, sine)


class LineExchange:
    def __init__(self, at, size, span, part, low_all, mid, scratch):
        self.at, self.size, self.span, self.part, self.mid = at, size, span, part, mid
        self.hold, self.landed, self.total, self.send, self.receive = scratch[:5]
        self.chunks = part.shape[1] // span
        self.low_all = low_all
        if low_all is not None:
            self.line = LineGather(at, size, span, low_all, *scratch[5:7])
        self.steps = self.chunks + (size - 1) * (1 if low_all is None else 2)

    def hop(self, source, target, chunk, side):
        to = (self.at + (1 if side == 0 else self.size - 1)) % self.size
        rows = pl.ds(pl.multiple_of(chunk * self.span, self.span), self.span)
        return remote(
            source.at[target, rows],
            self.landed.at[side, target, rows],
            self.send.at[target, chunk],
            self.receive.at[side, target, chunk],
            "fsdp",
            to,
        )

    def pass_on(self, target, chunk, side):
        rows = pl.ds(pl.multiple_of(chunk * self.span, self.span), self.span)
        origin = self.at == 0 if side == 0 else self.at == self.size - 1

        @pl.when(origin)
        def _():
            self.hop(self.part, target, chunk, side).start()

        @pl.when(jnp.logical_not(origin))
        def _():
            self.hop(self.part, target, chunk, side).wait_recv()
            added = self.part[target, rows, :].astype(FULL)
            added = added + self.landed[side, target, rows, :].astype(FULL)
            self.hold[target, rows, :] = added.astype(LOW)
            self.hop(self.hold, target, chunk, side).start()

    def step(self, index):
        at, size, chunks = self.at, self.size, self.chunks
        for gap in range(size - 1, 0, -1):
            chunk = index - at

            @pl.when((at + gap < size) & (chunk >= 0) & (chunk < chunks))
            def _(target=at + gap, chunk=chunk):
                self.pass_on(target, chunk, 0)

            chunk = index - (size - 1 - at)

            @pl.when((at >= gap) & (chunk >= 0) & (chunk < chunks))
            def _(target=at - gap, chunk=chunk):
                self.pass_on(target, chunk, 1)

        chunk = index - (size - 1)

        @pl.when((chunk >= 0) & (chunk < chunks))
        def _():
            rows = pl.ds(pl.multiple_of(chunk * self.span, self.span), self.span)
            self.total[...] = self.part[at, rows, :].astype(FULL)
            for side, ok in ((0, at > 0), (1, at < size - 1)):

                @pl.when(ok)
                def _(side=side):
                    self.hop(self.part, at, chunk, side).wait_recv()
                    self.total[...] += self.landed[side, at, rows, :].astype(FULL)

            low = self.mid(chunk, rows, self.total[...])
            if self.low_all is not None:
                self.low_all[at, rows, :] = low
                self.line.start(chunk)

        if self.low_all is not None:
            for gap in range(1, size):
                chunk = index - (size - 1) - gap

                @pl.when((chunk >= 0) & (chunk < chunks))
                def _(gap=gap, chunk=chunk):
                    self.line.forward(chunk, gap)

    def run(self, first, last):
        def one(index, carried):
            self.step(index)
            return carried

        lax.fori_loop(first, last, one, 0)

    def drain(self):
        at, size = self.at, self.size

        def one(chunk, carried):
            for gap in range(1, size):

                @pl.when(at + gap < size)
                def _(target=at + gap):
                    self.hop(self.part, target, chunk, 0).wait_send()

                @pl.when(at >= gap)
                def _(target=at - gap):
                    self.hop(self.part, target, chunk, 1).wait_send()

            if self.low_all is not None:
                self.line.drain(chunk)
            return carried

        lax.fori_loop(0, self.chunks, one, 0)


def line_span(tokens):
    return 16


def line_scratch(fsdp, tokens, width, gather):
    span = line_span(tokens)
    chunks = tokens // span
    dma = pltpu.SemaphoreType.DMA
    return [
        pltpu.VMEM((fsdp, tokens, width), LOW),
        pltpu.VMEM((2, fsdp, tokens, width), LOW),
        pltpu.VMEM((span, width), FULL),
        dma((fsdp, chunks)),
        dma((2, fsdp, chunks)),
    ] + ([dma((2, fsdp, chunks)), dma((fsdp, chunks))] if gather else [])


def exchange_kernel(mid, size, inputs, part, *refs):
    at = lax.axis_index("fsdp")
    ins, gains, low_all, refs = refs[:inputs], refs[inputs], refs[inputs + 1], refs[inputs + 2 :]
    outs, scratch = refs[:-7], refs[-7:]
    line_greet(at, size)
    line = LineExchange(
        at,
        size,
        line_span(part.shape[1]),
        part,
        low_all,
        lambda chunk, rows, total: mid(chunk, rows, total, ins, gains, outs),
        scratch,
    )
    line.run(0, line.steps)
    line.drain()


def exchange(part, ins, gains, mid, out_shape, fsdp, collective_id, name):
    _, tokens, width = part.shape
    return pl.pallas_call(
        functools.partial(exchange_kernel, mid, fsdp, len(ins)),
        in_specs=[VMEM_SPEC] * (len(ins) + 2),
        out_specs=[VMEM_SPEC] * (len(out_shape) + 1),
        out_shape=[jax.ShapeDtypeStruct(part.shape, LOW)] + out_shape,
        scratch_shapes=line_scratch(fsdp, tokens, width, True),
        compiler_params=pltpu.CompilerParams(
            vmem_limit_bytes=VMEM_LIMIT, collective_id=collective_id
        ),
        name=name,
    )(part, *ins, gains)


def spread(step, steps, work, body):
    def one(index, carried):
        body(index)
        return carried

    lax.fori_loop((step * work) // steps, ((step + 1) * work) // steps, one, 0)


class Copies:
    def __init__(self, copies):
        self.copies = [pltpu.make_async_copy(*copy) for copy in copies]

    def start(self):
        for copy in self.copies:
            copy.start()

    def wait(self):
        for copy in self.copies:
            copy.wait()


class Forward:
    def __init__(self, mid, weights, results, part, scratch):
        self.source, self.weights, self.results, self.part = mid, weights, results, part
        self.mid, self.hidden, self.pair, self.down = scratch[:4]
        self.pair_sem, self.down_sem, self.mid_sem, self.result_sem = scratch[4:8]
        self.outs = scratch[8:]
        self.sequences, self.tokens, _ = mid.shape
        self.half = self.tokens // 2
        self.span, self.reach = self.pair.shape[3], self.down.shape[1]
        self.tiles = weights.shape[2] // self.span
        self.ends = weights.shape[1] // self.reach
        self.count = self.tiles + self.ends

    def fetch_rows(self, half, s):
        return pltpu.make_async_copy(
            self.source.at[s, self.rows(half)],
            self.mid.at[half, pl.ds(s * self.half, self.half)],
            self.mid_sem.at[half, s],
        )

    def begin(self):
        for half in range(2):
            for s in range(self.sequences):
                self.fetch_rows(half, s).start()
        self.fetch(0)

    def give(self, index):
        return pltpu.make_async_copy(
            self.outs[index], self.results[index], self.result_sem.at[index]
        )

    def fetch_pair(self, half, tile):
        slot = (half * self.tiles + tile) % 2
        columns = pl.ds(pl.multiple_of(tile * self.span, self.span), self.span)
        return pltpu.make_async_copy(
            self.weights.at[pl.ds(0, 2), :, columns], self.pair.at[slot], self.pair_sem.at[slot]
        )

    def fetch_down(self, half, tile):
        slot = (half * self.ends + tile) % 2
        rows = pl.ds(pl.multiple_of(tile * self.reach, self.reach), self.reach)
        return pltpu.make_async_copy(
            self.weights.at[2, rows], self.down.at[slot], self.down_sem.at[slot]
        )

    def fetch(self, index):
        half, tile = index // self.count, index % self.count

        @pl.when(tile < self.tiles)
        def _():
            self.fetch_pair(half, tile).start()

        @pl.when(tile >= self.tiles)
        def _():
            self.fetch_down(half, tile - self.tiles).start()

    def rows(self, half):
        return pl.ds(pl.multiple_of(half * self.half, 16), self.half)

    def run(self, index):
        half, tile = index // self.count, index % self.count

        @pl.when(index + 1 < 2 * self.count)
        def _():
            self.fetch(index + 1)

        @pl.when(tile == 0)
        def _():
            for s in range(self.sequences):
                self.fetch_rows(half, s).wait()

        @pl.when(tile < self.tiles)
        def _():
            self.fetch_pair(half, tile).wait()
            slot = (half * self.tiles + tile) % 2
            mid = self.mid[half]
            gate = dot(mid, self.pair[slot, 0], 1, 0)
            up = dot(mid, self.pair[slot, 1], 1, 0)
            columns = pl.ds(pl.multiple_of(tile * self.span, self.span), self.span)
            results = [value.astype(LOW) for value in activate(gate, up)]
            self.hidden[half, :, columns] = results[0]
            for out, value in zip(self.outs, results):
                for sequence in range(self.sequences):
                    out[sequence, self.rows(half), columns] = value[
                        sequence * self.half : (sequence + 1) * self.half
                    ]

        @pl.when(tile >= self.tiles)
        def _():
            end = tile - self.tiles
            self.fetch_down(half, end).wait()
            slot = (half * self.ends + end) % 2
            value = dot(self.hidden[half], self.down[slot], 1, 1).astype(LOW)
            columns = pl.ds(pl.multiple_of(end * self.reach, self.reach), self.reach)
            for sequence in range(self.sequences):
                self.part[sequence, self.rows(half), columns] = value[
                    sequence * self.half : (sequence + 1) * self.half
                ]


def activate(gate, up):
    square = gate * gate
    squashed = jnp.tanh(GELU_SCALE * gate * (1.0 + GELU_CUBE * square))
    half = 0.5 + 0.5 * squashed
    act = gate * half
    slope = half + act * (1.0 - squashed) * (GELU_SCALE + 3.0 * GELU_SCALE * GELU_CUBE * square)
    return act * up, up * slope, act


def late_kernel(
    size, gains, mid, mixed_in, cotangent_in, weights,
    late, out, gain, hidden, gate_factor, up_factor, *scratch
):
    at = lax.axis_index("fsdp")
    line_greet(at, size)
    part, line_parts, (mixed, cotangent, side_sem) = scratch[0], scratch[1:8], scratch[8:11]
    line = LineExchange(
        at,
        size,
        line_span(part.shape[1]),
        part,
        late,
        lambda chunk, rows, total: late_mid(
            chunk, rows, total, (mixed, cotangent), gains, (out, gain)
        ),
        line_parts,
    )
    forward = Forward(mid, weights, (hidden, gate_factor, up_factor), part, scratch[11:])
    forward.begin()
    sides = [
        pltpu.make_async_copy(source, target, side_sem.at[index])
        for index, (source, target) in enumerate(((mixed_in, mixed), (cotangent_in, cotangent)))
    ]
    for copy in sides:
        copy.start()

    def one(index, carried):
        forward.run(index)
        return carried

    lax.fori_loop(0, forward.count, one, 0)
    for copy in sides:
        copy.wait()
    ahead = line.chunks // 2

    def both(index, carried):
        line.step(index)
        spread(index, ahead, forward.count, lambda tile: forward.run(forward.count + tile))
        return carried

    lax.fori_loop(0, ahead, both, 0)
    for index in range(3):
        forward.give(index).start()
    line.run(ahead, line.steps)
    line.drain()
    for index in range(3):
        forward.give(index).wait()


def late_exchange(mid, weights, mixed, cotangent, gains, collective_id):
    fsdp, tokens, width = mid.shape
    units = weights.shape[2]
    span, reach = tile_of(units), tile_of(width)
    rows = fsdp * tokens // 2
    dma = pltpu.SemaphoreType.DMA
    low = jax.ShapeDtypeStruct((fsdp, tokens, units), LOW)
    return pl.pallas_call(
        functools.partial(late_kernel, fsdp),
        in_specs=[VMEM_SPEC] + [ANY_SPEC] * 4,
        out_specs=[VMEM_SPEC] * 3 + [ANY_SPEC] * 3,
        out_shape=[
            jax.ShapeDtypeStruct(mid.shape, LOW),
            jax.ShapeDtypeStruct((tokens, width), LOW),
            jax.ShapeDtypeStruct((1, width), FULL),
            low,
            low,
            low,
        ],
        scratch_shapes=[pltpu.VMEM(mid.shape, LOW)]
        + line_scratch(fsdp, tokens, width, True)
        + [
            pltpu.VMEM((tokens, width), FULL),
            pltpu.VMEM((tokens, width), LOW),
            dma((2,)),
            pltpu.VMEM((2, rows, width), LOW),
            pltpu.VMEM((2, rows, units), LOW),
            pltpu.VMEM((2, 2, width, span), LOW),
            pltpu.VMEM((2, reach, units), LOW),
            dma((2,)),
            dma((2,)),
            dma((2, fsdp)),
            dma((3,)),
        ]
        + [pltpu.VMEM((fsdp, tokens, units), LOW)] * 3,
        compiler_params=pltpu.CompilerParams(
            vmem_limit_bytes=VMEM_LIMIT, collective_id=collective_id
        ),
        name="late_exchange",
    )(gains, mid, mixed, cotangent, weights)


class Backward:
    def __init__(self, late, mid, weights, factors, part, grads, scratch):
        self.weights, self.part, self.grads = weights, part, grads
        self.late, self.mid, self.factors = late, mid, factors
        self.rows_in, self.turned, self.pairs, self.wide, self.tall, self.stage = scratch[:6]
        self.wide_sem, self.tall_sem, self.stage_sem, self.row_sem, self.factor_sem = scratch[6:11]
        self.block, self.block_sem = scratch[11:13]
        self.own_factors = scratch[13:]
        self.sequences, self.tokens, self.width = late.shape
        self.half = self.tokens // 2
        self.span, self.reach = self.wide.shape[2], self.tall.shape[2]
        self.units = weights.shape[2]
        self.tiles = self.units // self.span
        self.ends = self.width // self.reach
        self.count = self.tiles + self.ends
        self.sums = 2 * self.units // self.stage.shape[2]
        self.pieces = 2 * self.ends
        self.work = self.sums * (self.width // 768)

    def rows(self, half):
        return pl.ds(pl.multiple_of(half * self.half, 16), self.half)

    def fetch_rows(self, half, s):
        return pltpu.make_async_copy(
            self.late.at[s, self.rows(half)],
            self.rows_in.at[half, pl.ds(s * self.half, self.half)],
            self.row_sem.at[half, s],
        )

    def begin(self):
        for half in range(2):
            for s in range(self.sequences):
                self.fetch_rows(half, s).start()
        self.fetch(0)
        self.fetch_block(0).start()

    def fetch_block(self, piece):
        half, block = piece // self.ends, piece % self.ends
        span = pl.ds(pl.multiple_of(block * self.reach, self.reach), self.reach)
        return Copies(
            (
                self.mid.at[s, self.rows(half), span],
                self.block.at[piece % 2, pl.ds(s * self.half, self.half)],
                self.block_sem.at[piece % 2, s],
            )
            for s in range(self.sequences)
        )

    def turn(self, piece):
        @pl.when(piece + 1 < self.pieces)
        def _():
            self.fetch_block(piece + 1).start()

        self.fetch_block(piece).wait()
        rows = self.sequences * self.half
        half, block = piece // self.ends, piece % self.ends
        span = pl.ds(pl.multiple_of(block * self.reach, self.reach), self.reach)
        columns = pl.ds(pl.multiple_of(half * rows, 128), rows)
        self.turned[span, columns] = self.block[piece % 2].T

    def fetch_wide(self, half, tile):
        slot = (half * self.tiles + tile) % 2
        columns = pl.ds(pl.multiple_of(tile * self.span, self.span), self.span)
        rows = self.rows(half)
        return Copies(
            [(self.weights.at[2, :, columns], self.wide.at[slot], self.wide_sem.at[slot])]
            + [
                (
                    self.factors[side].at[:, rows, columns],
                    self.own_factors[side].at[:, rows, columns],
                    self.factor_sem.at[slot, side],
                )
                for side in range(2)
            ]
        )

    def fetch_tall(self, half, tile):
        slot = (half * self.ends + tile) % 2
        rows = pl.ds(pl.multiple_of(tile * self.reach, self.reach), self.reach)
        return pltpu.make_async_copy(
            self.weights.at[pl.ds(0, 2), rows], self.tall.at[slot], self.tall_sem.at[slot]
        )

    def fetch(self, index):
        half, tile = index // self.count, index % self.count

        @pl.when(tile < self.tiles)
        def _():
            self.fetch_wide(half, tile).start()

        @pl.when(tile >= self.tiles)
        def _():
            self.fetch_tall(half, tile - self.tiles).start()

    def run(self, index):
        half, tile = index // self.count, index % self.count
        rows = self.rows(half)

        @pl.when(index + 1 < 2 * self.count)
        def _():
            self.fetch(index + 1)

        @pl.when(tile == 0)
        def _():
            for s in range(self.sequences):
                self.fetch_rows(half, s).wait()

        @pl.when(tile < self.tiles)
        def _():
            self.fetch_wide(half, tile).wait()
            slot = (half * self.tiles + tile) % 2
            hidden_grad = dot(self.rows_in[half], self.wide[slot], 1, 0)
            columns = pl.ds(pl.multiple_of(tile * self.span, self.span), self.span)
            for side, factor in enumerate(self.own_factors):
                target = pl.ds(
                    pl.multiple_of(side * self.units + tile * self.span, self.span), self.span
                )
                for s in range(self.sequences):
                    own = slice(s * self.half, (s + 1) * self.half)
                    value = hidden_grad[own] * factor[s, rows, columns].astype(FULL)
                    self.pairs[half, own, target] = value.astype(LOW)

        @pl.when(tile >= self.tiles)
        def _():
            end = tile - self.tiles
            self.fetch_tall(half, end).wait()
            slot = (half * self.ends + end) % 2
            value = dot(self.pairs[half, :, : self.units], self.tall[slot, 0], 1, 1)
            value = value + dot(self.pairs[half, :, self.units :], self.tall[slot, 1], 1, 1)
            value = value.astype(LOW)
            columns = pl.ds(pl.multiple_of(end * self.reach, self.reach), self.reach)
            for s in range(self.sequences):
                self.part[s, rows, columns] = value[s * self.half : (s + 1) * self.half]

    def put(self, index):
        span = self.stage.shape[2]
        columns = pl.ds(pl.multiple_of(index * span, span), span)
        return pltpu.make_async_copy(
            self.stage.at[index % 2], self.grads.at[:, columns], self.stage_sem.at[index % 2]
        )

    def sum(self, unit):
        thirds = self.width // 768
        index, third = unit // thirds, unit % thirds

        @pl.when((third == 0) & (index >= 2))
        def _():
            self.put(index - 2).wait()

        span = self.stage.shape[2]
        columns = pl.ds(pl.multiple_of(index * span, span), span)
        rows = self.sequences * self.half
        own = pl.ds(pl.multiple_of(third * 768, 768), 768)
        value = dot(self.turned[own, :rows], self.pairs[0, :, columns], 1, 0)
        value = value + dot(self.turned[own, rows:], self.pairs[1, :, columns], 1, 0)
        self.stage[index % 2, own, :] = value.astype(LOW)

        @pl.when(third == thirds - 1)
        def _():
            self.put(index).start()


def mid_kernel(
    size, gains, late, mixed_in, branch_in, cotangent_in, gate_factor, up_factor, mid, weights,
    low, mixed_grad, gain, grads, *scratch
):
    at = lax.axis_index("fsdp")
    line_greet(at, size)
    part, line_parts, sides = scratch[0], scratch[1:8], scratch[8:11]
    side_sem = scratch[11]
    line = LineExchange(
        at,
        size,
        line_span(part.shape[1]),
        part,
        low,
        lambda chunk, rows, total: mid_mid(
            chunk, rows, total, sides, gains, (mixed_grad, gain)
        ),
        line_parts,
    )
    backward = Backward(late, mid, weights, (gate_factor, up_factor), part, grads, scratch[12:])
    backward.begin()
    copies = [
        pltpu.make_async_copy(source, target, side_sem.at[index])
        for index, (source, target) in enumerate(zip((mixed_in, branch_in, cotangent_in), sides))
    ]
    for copy in copies:
        copy.start()

    def one(index, carried):
        backward.run(index)
        spread(index, backward.count, backward.pieces, backward.turn)
        return carried

    lax.fori_loop(0, backward.count, one, 0)
    for copy in copies:
        copy.wait()
    ahead = line.chunks // 2

    def both(index, carried):
        line.step(index)
        spread(index, ahead, backward.count, lambda tile: backward.run(backward.count + tile))
        return carried

    lax.fori_loop(0, ahead, both, 0)
    busy = 6

    def more(index, carried):
        line.step(ahead + index)
        spread(index, busy, backward.work, backward.sum)
        return carried

    lax.fori_loop(0, busy, more, 0)
    line.run(ahead + busy, line.steps)
    line.drain()
    backward.put(backward.sums - 2).wait()
    backward.put(backward.sums - 1).wait()


def mid_exchange(
    late, mid, mixed, branch, cotangent, gains, gate_factor, up_factor, weights, collective_id
):
    fsdp, tokens, width = mid.shape
    units = weights.shape[2]
    span, reach, stage = tile_of(units), 384, 384 if fsdp <= 4 else 256
    rows = fsdp * tokens // 2
    dma = pltpu.SemaphoreType.DMA
    return pl.pallas_call(
        functools.partial(mid_kernel, fsdp),
        in_specs=[VMEM_SPEC] + [ANY_SPEC] * 8,
        out_specs=[VMEM_SPEC] * 3 + [ANY_SPEC],
        out_shape=[
            jax.ShapeDtypeStruct(mid.shape, LOW),
            jax.ShapeDtypeStruct((tokens, width), FULL),
            jax.ShapeDtypeStruct((2, width), FULL),
            jax.ShapeDtypeStruct((width, 2 * units), LOW),
        ],
        scratch_shapes=[pltpu.VMEM(mid.shape, LOW)]
        + line_scratch(fsdp, tokens, width, True)
        + [
            pltpu.VMEM((tokens, width), FULL),
            pltpu.VMEM((tokens, width), FULL),
            pltpu.VMEM((tokens, width), LOW),
            dma((3,)),
            pltpu.VMEM((2, rows, width), LOW),
            pltpu.VMEM((width, 2 * rows), LOW),
            pltpu.VMEM((2, rows, 2 * units), LOW),
            pltpu.VMEM((2, width, span), LOW),
            pltpu.VMEM((2, 2, reach, units), LOW),
            pltpu.VMEM((2, width, stage), LOW),
            dma((2,)),
            dma((2,)),
            dma((2,)),
            dma((2, fsdp)),
            dma((2, 2)),
            pltpu.VMEM((2, rows, reach), LOW),
            dma((2, fsdp)),
        ]
        + [pltpu.VMEM((fsdp, tokens, units), LOW)] * 2,
        compiler_params=pltpu.CompilerParams(
            vmem_limit_bytes=VMEM_LIMIT, collective_id=collective_id
        ),
        name="mid_exchange",
    )(gains, late, mixed, branch, cotangent, gate_factor, up_factor, mid, weights)


def row_sum(values):
    return jnp.sum(values, 0, keepdims=True)


def add_gain(ref, chunk, index, values):
    @pl.when(chunk == 0)
    def _():
        ref[index : index + 1, :] = row_sum(values)

    @pl.when(chunk > 0)
    def _():
        ref[index : index + 1, :] += row_sum(values)


def branch_mid(chunk, rows, branch, ins, gains, outs):
    (x,), (branch_out, mixed_out) = ins, outs
    branch_out[rows, :] = branch
    post_hat = branch * rms_scale(branch)
    mixed = x[rows, :].astype(FULL) + post_hat * (1.0 + gains[1:2, :])
    mixed_out[rows, :] = mixed
    return (mixed * rms_scale(mixed) * (1.0 + gains[2:3, :])).astype(LOW)


def late_mid(chunk, rows, ffn_branch, ins, gains, outs):
    (mixed, cotangent), (out, gain) = ins, outs
    inv_late = rms_scale(ffn_branch)
    late_hat = ffn_branch * inv_late
    scale = 1.0 + gains[3:4, :]
    out[rows, :] = (mixed[rows, :] + late_hat * scale).astype(LOW)
    upstream = cotangent[rows, :].astype(FULL)
    add_gain(gain, chunk, 0, upstream * late_hat)
    scaled = upstream * scale
    grad = inv_late * (scaled - late_hat * jnp.mean(scaled * late_hat, -1, keepdims=True))
    return grad.astype(LOW)


def mid_mid(chunk, rows, mid_grad, ins, gains, outs):
    (mixed, branch, cotangent), (mixed_grad_out, gain) = ins, outs
    mixed = mixed[rows, :]
    inv_mid = rms_scale(mixed)
    mid_hat = mixed * inv_mid
    add_gain(gain, chunk, 1, mid_grad * mid_hat)
    scaled = mid_grad * (1.0 + gains[2:3, :])
    mixed_grad = cotangent[rows, :].astype(FULL) + inv_mid * (
        scaled - mid_hat * jnp.mean(scaled * mid_hat, -1, keepdims=True)
    )
    mixed_grad_out[rows, :] = mixed_grad
    branch = branch[rows, :]
    inv_post = rms_scale(branch)
    post_hat = branch * inv_post
    add_gain(gain, chunk, 0, mixed_grad * post_hat)
    hat = mixed_grad * (1.0 + gains[1:2, :])
    grad = inv_post * (hat - post_hat * jnp.mean(hat * post_hat, -1, keepdims=True))
    return grad.astype(LOW)


def pre_mid(chunk, rows, normed_grad, ins, gains, outs):
    (x, mixed_grad), (out, gain) = ins, outs
    x = x[rows, :].astype(FULL)
    inv_pre = rms_scale(x)
    normed = x * inv_pre
    add_gain(gain, chunk, 0, normed_grad * normed)
    scaled = normed_grad * (1.0 + gains[0:1, :])
    out[rows, :] = mixed_grad[rows, :] + inv_pre * (
        scaled - normed * jnp.mean(scaled * normed, -1, keepdims=True)
    )


def pair_sums_kernel(ctx, key, value, key_sum, value_sum, *scratch):
    at = lax.axis_index("ctx")
    greet(ctx_peers(at, ctx))
    keys = ctx_scatter(at, ctx, lambda c: key.at[:, c], scratch)
    values = ctx_scatter(at, ctx, lambda c: value.at[:, c], scratch[SCATTER:])
    keys.start()
    values.start()
    keys.diagonal()
    values.diagonal()
    keys.neighbours()
    values.neighbours()
    keys.passing()
    values.passing()
    for scatter, out in ((keys, key_sum), (values, value_sum)):

        def store(block, rows, total, out=out):
            out[block, rows, :] = total

        scatter.finish(store)
    keys.drain()
    values.drain()


def scatter_pairs(key, value):
    sequences, ctx, rows, width = key.shape
    return pl.pallas_call(
        functools.partial(pair_sums_kernel, ctx),
        in_specs=[VMEM_SPEC] * 2,
        out_specs=[VMEM_SPEC] * 2,
        out_shape=[jax.ShapeDtypeStruct((sequences, rows, width), FULL)] * 2,
        scratch_shapes=ctx_scatter_scratch(ctx, sequences, rows, width, LOW) * 2,
        compiler_params=pltpu.CompilerParams(vmem_limit_bytes=VMEM_LIMIT, collective_id=2),
        name="scatter_pairs",
    )(key, value)


def tail_kernel(
    ctx, fsdp, in_part, out_part, pre_part, x, mixed_grad, gains, in_old, out_old, *refs
):
    at, line_at = lax.axis_index("ctx"), lax.axis_index("fsdp")
    in_new, out_new, update, head_sum, input_grad, gain = refs[:6]
    scratch = refs[6:]
    places = head_places(fsdp)
    mine = len(places[0])
    scratch, others = scratch[: 2 * SCATTER], scratch[2 * SCATTER :]
    mine_sum, arrived, move_send, move_receive, out_sum = others[:5]
    gram, packed = others[10:12]
    head = arrived.shape[-1]
    greet(ctx_peers(at, ctx) + [("fsdp", (line_at + k) % fsdp) for k in range(1, fsdp)])
    ins = ctx_scatter(at, ctx, rows_of_ctx(in_part), scratch)
    outs = ctx_scatter(at, ctx, rows_of_ctx(out_part), scratch[SCATTER:])
    line = LineExchange(
        line_at,
        fsdp,
        line_span(pre_part.shape[1]),
        pre_part,
        None,
        lambda chunk, rows, total: pre_mid(
            chunk, rows, total, (x, mixed_grad), gains, (input_grad, gain)
        ),
        others[5:10],
    )
    ins.start()
    outs.start()
    ins.diagonal()
    ins.neighbours()
    line.run(0, 3)
    ins.passing()
    outs.diagonal()
    outs.neighbours()
    line.run(3, 6)
    outs.passing()
    line.run(6, 8)

    def store_in(block, rows, total):
        mine_sum[rows, :] = total.astype(LOW)

    def store_out(block, rows, total):
        out_sum[rows, :] = total

    ins.finish(store_in)

    def copies_of(owner, index):
        return [
            (user, slot)
            for user in range(fsdp)
            for slot in range(mine)
            if places[user][slot] == (owner, index)
        ]

    def move(user, slot):
        owner, index = places[user][slot]
        copy = copies_of(owner, index).index((user, slot))
        return remote(
            mine_sum.at[:, pl.ds(slot * head, head)],
            arrived.at[index, copy],
            move_send.at[slot],
            move_receive.at[index, copy],
            "fsdp",
            owner,
        )

    for user in range(fsdp):
        for slot in range(mine):

            @pl.when(line_at == user)
            def _(user=user, slot=slot):
                owner, index = places[user][slot]
                if owner == user:
                    copy = copies_of(owner, index).index((user, slot))
                    arrived[index, copy] = mine_sum[:, slot * head : (slot + 1) * head]
                else:
                    move(user, slot).start()

    line.run(8, line.steps)
    outs.finish(store_out)

    def step_of(index, grad, old_ref, new_ref, at):
        new = MOMENTUM_DECAY * old_ref[:, at, :] + grad
        new_ref[:, at, :] = new
        low = (grad + MOMENTUM_DECAY * new).astype(LOW)
        update[index] = low
        gram[index] = dot(low, low, 0, 0)

    stored = in_old.shape[1]
    for index in range(out_old.shape[1]):
        grad = out_sum[:, index * head : (index + 1) * head]
        step_of(stored + index, grad, out_old, out_new, index)
    for index in range(stored + out_old.shape[1], gram.shape[0]):
        gram[index] = jnp.zeros((head, head), FULL)
    for owner in range(fsdp):

        @pl.when(line_at == owner)
        def _(owner=owner):
            for index in range(stored):
                for user, slot in copies_of(owner, index):
                    if user != owner:
                        move(user, slot).wait_recv()

    for index in range(stored):
        grad = arrived[index, 0].astype(FULL)
        for copy in range(1, arrived.shape[1]):
            more = arrived[index, copy].astype(FULL)
            paired = line_at * stored + index >= QUERY_HEADS
            grad = grad + jnp.where(paired, more, 0.0)
        step_of(index, grad, in_old, in_new, index)
    large = gram.shape[0] // ctx
    edge = large * 2 * FBLK

    def pack_for(index, carried):
        packed[index, edge:, :] = jnp.zeros((packed.shape[1] - edge, FBLK), FULL)

        def write(first, rows):
            packed[index, first : first + rows.shape[0], :] = rows

        pack_all((0, None), (large, lambda i: gram[index * large + i]), write)
        return carried

    lax.fori_loop(0, ctx, pack_for, 0)
    heads = ctx_scatter(at, ctx, rows_of_ctx(packed), others[12:])
    heads.start()
    heads.diagonal()
    heads.neighbours()
    heads.passing()

    def store_head(block, rows, total):
        head_sum[rows, :] = total

    heads.finish(store_head)
    heads.drain()
    for user in range(fsdp):
        for slot in range(mine):
            if places[user][slot][0] != user:

                @pl.when(line_at == user)
                def _(user=user, slot=slot):
                    move(user, slot).wait_send()

    ins.drain()
    outs.drain()
    line.drain()


def tail(in_part, out_part, pre_part, x, mixed_grad, gains, in_old, out_old):
    _, stored, head = in_old.shape
    matrices = stored + out_old.shape[1]
    large = -(-matrices // in_part.shape[0])
    ctx, rows, in_width = in_part.shape
    out_width = out_part.shape[2]
    fsdp, tokens, width = pre_part.shape
    mine = len(head_places(fsdp)[0])
    copies = max(1, fsdp // KEY_VALUE_HEADS)
    dma = pltpu.SemaphoreType.DMA
    return pl.pallas_call(
        functools.partial(tail_kernel, ctx, fsdp),
        in_specs=[VMEM_SPEC] * 8,
        out_specs=[VMEM_SPEC] * 6,
        out_shape=[
            jax.ShapeDtypeStruct(in_old.shape, FULL),
            jax.ShapeDtypeStruct(out_old.shape, FULL),
            jax.ShapeDtypeStruct((matrices, rows, head), LOW),
            jax.ShapeDtypeStruct((packed_rows(0, large), FBLK), FULL),
            jax.ShapeDtypeStruct((tokens, width), FULL),
            jax.ShapeDtypeStruct((1, width), FULL),
        ],
        scratch_shapes=ctx_scatter_scratch(ctx, 1, rows, in_width, LOW)
        + ctx_scatter_scratch(ctx, 1, rows, out_width, LOW)
        + [
            pltpu.VMEM((rows, in_width), LOW),
            pltpu.VMEM((stored, copies, rows, head), LOW),
            dma((mine,)),
            dma((stored, copies)),
            pltpu.VMEM((rows, out_width), FULL),
        ]
        + line_scratch(fsdp, tokens, width, False)
        + [
            pltpu.VMEM((ctx * large, head, head), FULL),
            pltpu.VMEM((ctx, packed_rows(0, large), FBLK), FULL),
        ]
        + ctx_scatter_scratch(ctx, 1, packed_rows(0, large), FBLK, FULL),
        compiler_params=pltpu.CompilerParams(vmem_limit_bytes=VMEM_LIMIT, collective_id=3),
        name="tail",
    )(in_part, out_part, pre_part, x, mixed_grad, gains, in_old, out_old)


def packed_rows(small, large):
    squares = -(-small // 2)
    return squares * FBLK + large * 2 * FBLK + 16 * (-(-(squares + large) // 16))


def grid_of(size):
    rows = lax.broadcasted_iota(jnp.int32, (size, size), 0)
    return rows, lax.broadcasted_iota(jnp.int32, (size, size), 1)


def pack_two(first, second):
    rows, columns = grid_of(FBLK)
    if second is None:
        return first, jnp.zeros((1, FBLK), FULL)
    diagonal = jnp.sum(jnp.where(rows == columns, second, 0.0), 0, keepdims=True)
    return jnp.where(rows <= columns, first, second), diagonal


def unpack_two(square, diagonal, both):
    rows, columns = grid_of(FBLK)
    if not both:
        return square, None
    turned = square.T
    first = jnp.where(rows <= columns, square, turned)
    second = jnp.where(rows > columns, square, jnp.where(rows < columns, turned, diagonal))
    return first, second


def pack_all(blocks, heads, write):
    small, large = blocks[0], heads[0]
    squares = -(-small // 2)
    edge = squares * FBLK + large * 2 * FBLK
    for index in range(squares):
        second = blocks[1](2 * index + 1) if 2 * index + 1 < small else None
        square, diagonal = pack_two(blocks[1](2 * index), second)
        write(index * FBLK, square)
        write(edge + index, diagonal)
    for index in range(large):
        head = heads[1](index)
        square, diagonal = pack_two(head[:FBLK, :FBLK], head[FBLK:, FBLK:])
        base = squares * FBLK + index * 2 * FBLK
        write(base, square)
        write(base + FBLK, head[:FBLK, FBLK:])
        write(edge + squares + index, diagonal)


def unpack_all(small, large, read):
    squares = -(-small // 2)
    edge = squares * FBLK + large * 2 * FBLK
    blocks, heads = [], []
    for index in range(squares):
        both = 2 * index + 1 < small
        first, second = unpack_two(read(index * FBLK, FBLK), read(edge + index, 1), both)
        blocks += [first, second] if both else [first]
    for index in range(large):
        base = squares * FBLK + index * 2 * FBLK
        first, second = unpack_two(read(base, FBLK), read(edge + squares + index, 1), True)
        corner = read(base + FBLK, FBLK)
        heads.append(
            jnp.concatenate(
                [
                    jnp.concatenate([first, corner], 1),
                    jnp.concatenate([corner.T, second], 1),
                ],
                0,
            )
        )
    return blocks, heads


def newton_kernel(
    ctx, fsdp, large, head_rate, ffn_rate, heads, blocks, gains, head_update_in, in_old_in, out_old_in,
    ffn_update, ffn_old, in_new, out_new, ffn_new, gains_all, *scratch
):
    at, line_at = lax.axis_index("ctx"), lax.axis_index("fsdp")
    small = blocks.shape[1]
    packed, gram, poly, poly_all, gains_line, gains_sum, gain_send, gain_receive = scratch[:8]
    update, weights, update_sem, weight_sem, out_sem = scratch[8:13]
    head_update, in_old, out_old, side_sem = scratch[13:17]
    scratch = scratch[17:]
    sides = [
        pltpu.make_async_copy(source, target, side_sem.at[index])
        for index, (source, target) in enumerate(
            ((head_update_in, head_update), (in_old_in, in_old), (out_old_in, out_old))
        )
    ]
    matrices, _, width = weights.shape
    per_matrix = width // FBLK
    count = matrices * per_matrix
    greet(ctx_peers(at, ctx) + [("fsdp", (line_at + k) % fsdp) for k in range(1, fsdp)])

    def gain_copy(k):
        return remote(
            gains,
            gains_line.at[k],
            gain_send.at[k],
            gain_receive.at[k],
            "fsdp",
            (line_at + k) % fsdp,
        )

    def fetches(matrix):
        return [
            pltpu.make_async_copy(
                ffn_update.at[matrix], update.at[matrix], update_sem.at[matrix]
            ),
            pltpu.make_async_copy(ffn_old.at[matrix], weights.at[matrix], weight_sem.at[matrix]),
        ]

    for k in range(1, fsdp):
        gain_copy(k).start()
    edge = -(-small // 2) * FBLK

    def pack_for(index, carried):
        packed[index, edge:, :] = jnp.zeros((packed.shape[1] - edge, FBLK), FULL)

        def write(first, rows):
            packed[index, first : first + rows.shape[0], :] = rows

        pack_all((small, lambda i: blocks[index, i]), (0, None), write)
        return carried

    lax.fori_loop(0, ctx, pack_for, 0)
    scatter = ctx_scatter(at, ctx, rows_of_ctx(packed), scratch)
    scatter.start()
    for matrix in range(matrices):
        for copy in fetches(matrix):
            copy.start()
    for copy in sides:
        copy.start()
    scatter.diagonal()
    scatter.neighbours()
    _, head_grams = unpack_all(0, large, lambda first, count: heads[first : first + count, :])
    head_polys = polys_of(head_grams)
    scatter.passing()
    total = gains[...]
    for k in range(1, fsdp):
        gain_copy(k).wait_recv()
        total = total + gains_line[k]
    gains_sum[...] = total
    scratch = scratch[SCATTER:]
    gather_gains = CtxGather(at, ctx, gains_sum, lambda c: gains_all.at[c], 0, scratch[:5])
    gather = CtxGather(at, ctx, poly, lambda c: poly_all.at[c], 0, scratch[5:10])

    def store(block, rows, total):
        gram[rows, :] = total

    scatter.finish(store)
    gather_gains.start()
    block_grams, _ = unpack_all(small, 0, lambda first, count: gram[first : first + count, :])
    block_polys = polys_of(block_grams)
    last = edge + large * 2 * FBLK
    poly[last:, :] = jnp.zeros((poly.shape[0] - last, FBLK), FULL)

    def write(first, rows):
        poly[first : first + rows.shape[0], :] = rows

    pack_all((small, lambda i: block_polys[i]), (large, lambda i: head_polys[i]), write)
    gather.start()
    for matrix in range(matrices):
        for copy in fetches(matrix):
            copy.wait()

    def place(block):
        matrix = block // per_matrix
        columns = pl.ds(pl.multiple_of((block % per_matrix) * FBLK, FBLK), FBLK)
        return matrix, columns

    def put(block):
        matrix, columns = place(block)
        return pltpu.make_async_copy(
            weights.at[matrix, :, columns], ffn_new.at[matrix, :, columns], out_sem.at[block]
        )

    def apply(source, first):
        found, _ = unpack_all(small, 0, lambda row, count: source(row, count))
        for index, found_poly in enumerate(found):
            block = first * small + index

            @pl.when(block < count)
            def _(block=block, found_poly=found_poly):
                matrix, columns = place(block)
                step = moved(update[matrix, :, columns], found_poly)
                weights[matrix, :, columns] = weights[matrix, :, columns] * SHRINK - ffn_rate * step
                put(block).start()

    shift = large * 2 * FBLK

    def reader(view):
        edge_small = -(-small // 2) * FBLK

        def read(row, count):
            row = row + shift if row >= edge_small else row
            return view[row : row + count, :]

        return read

    apply(reader(poly), at)
    gather_gains.forward()
    gather.forward()
    gather_gains.rest()
    gather.rest()
    square = gather.square
    for j in range(square.column):
        for turn in (False, True):
            if j > 0 or turn:
                device = square.device(j, turn)
                apply(reader(poly_all.at[device]), device)
    for k in range(1, fsdp):
        gain_copy(k).wait_send()
    gather_gains.finish()
    gather.finish()
    for j in range(square.column):
        for turn in (False, True):
            device = square.device(j, turn, 1 - square.core)
            apply(reader(poly_all.at[device]), device)
    stored = in_old.shape[1]
    for copy in sides:
        copy.wait()
    for device in range(ctx):
        first = device * large
        if first < head_update.shape[0]:
            _, found = unpack_all(
                small, large, lambda row, count: poly_all[device, row : row + count, :]
            )
            for index in range(first, min(first + large, head_update.shape[0])):
                step = head_rate * moved(head_update[index], found[index - first])
                if index < stored:
                    in_new[:, index, :] = in_old[:, index, :] * SHRINK - step
                else:
                    out_new[:, index - stored, :] = out_old[:, index - stored, :] * SHRINK - step
    scatter.drain()

    def finish(block, carried):
        put(block).wait()
        return carried

    lax.fori_loop(0, count, finish, 0)


def newton(
    heads, blocks, gains, head_update, in_old, out_old, ffn_update, ffn_old, head_rate, ffn_rate, fsdp
):
    ctx, small = blocks.shape[:2]
    large = -(-head_update.shape[0] // ctx)
    rows, block_rows = packed_rows(small, large), packed_rows(small, 0)
    dma = pltpu.SemaphoreType.DMA
    matrices = ffn_old.shape[0]
    return pl.pallas_call(
        functools.partial(newton_kernel, ctx, fsdp, large, head_rate, ffn_rate),
        in_specs=[VMEM_SPEC] * 3 + [ANY_SPEC] * 5,
        out_specs=[VMEM_SPEC] * 2 + [ANY_SPEC, VMEM_SPEC],
        out_shape=[
            jax.ShapeDtypeStruct(in_old.shape, FULL),
            jax.ShapeDtypeStruct(out_old.shape, FULL),
            jax.ShapeDtypeStruct(ffn_old.shape, FULL),
            jax.ShapeDtypeStruct((ctx,) + gains.shape, FULL),
        ],
        scratch_shapes=[
            pltpu.VMEM((ctx, block_rows, FBLK), FULL),
            pltpu.VMEM((block_rows, FBLK), FULL),
            pltpu.VMEM((rows, FBLK), FULL),
            pltpu.VMEM((ctx, rows, FBLK), FULL),
            pltpu.VMEM((fsdp,) + gains.shape, FULL),
            pltpu.VMEM(gains.shape, FULL),
            dma((fsdp,)),
            dma((fsdp,)),
            pltpu.VMEM(ffn_update.shape, LOW),
            pltpu.VMEM(ffn_old.shape, FULL),
            dma((matrices,)),
            dma((matrices,)),
            dma((ctx * small,)),
            pltpu.VMEM(head_update.shape, LOW),
            pltpu.VMEM(in_old.shape, FULL),
            pltpu.VMEM(out_old.shape, FULL),
            dma((3,)),
        ]
        + ctx_scatter_scratch(ctx, 1, block_rows, FBLK, FULL)
        + ctx_gather_sems(ctx) * 2,
        compiler_params=pltpu.CompilerParams(vmem_limit_bytes=VMEM_LIMIT, collective_id=4),
        name="newton",
    )(heads, blocks, gains, head_update, in_old, out_old, ffn_update, ffn_old)


def local(
    inputs,
    cotangent,
    weights_in,
    weights_out,
    ffn_weights,
    norm_gains,
    momentum_in,
    momentum_out,
    ffn_momentum,
    gain_first,
    gain_second,
    stretch_order,
):
    sequences, rows, width = inputs.shape
    stretch_rows = rows // 2
    local_rows, in_local, head = weights_in.shape
    out_local = weights_out.shape[1]
    ffn_local = ffn_weights.shape[2]
    ctx, fsdp = lax.axis_size("ctx"), lax.axis_size("fsdp")
    ctx_at = lax.axis_index("ctx")
    tokens = sequences * rows
    all_sequences = sequences * fsdp
    heads = QUERY_HEADS // fsdp
    pairs = max(1, KEY_VALUE_HEADS // fsdp)
    shared = heads // pairs
    mine = heads + 2 * pairs

    ffn_mine = jnp.transpose(ffn_weights, (1, 0, 2))

    flat = inputs.reshape(tokens, width)
    mine_in, w_out, ffn_cut, own_normed = prepare(
        weights_in, weights_out, ffn_mine, flat, norm_gains, ctx, fsdp
    )
    ffn_low = lax.all_gather(ffn_cut, "ctx", axis=1, tiled=True)
    own_places = positions_of(
        ctx_at * rows + jnp.arange(rows, dtype=jnp.int32), stretch_order, stretch_rows
    )
    all_places = positions_of(
        jnp.arange(ctx * rows, dtype=jnp.int32), stretch_order, stretch_rows
    )
    cosine, sine = rope_tables(own_places, head)
    normed_low, w_in, query, key_all, value_all = project(
        own_normed,
        mine_in,
        jnp.tile(cosine, (sequences, 1)),
        jnp.tile(sine, (sequences, 1)),
        sequences,
        heads,
        pairs,
        ctx,
        fsdp,
    )
    normed_low = normed_low.reshape(fsdp * tokens, width)
    w_out = w_out.reshape(width, out_local * head)
    cosine, sine = jnp.tile(cosine, (all_sequences, 1)), jnp.tile(sine, (all_sequences, 1))
    scale = head ** (-0.5)

    def column(values, index):
        return values[:, index * head : (index + 1) * head]

    def by_sequence(columns):
        return jnp.concatenate([c.reshape(all_sequences, rows, head) for c in columns], 1)

    def flat_heads(values, count):
        return [
            values[:, g * rows : (g + 1) * rows].reshape(all_sequences * rows, head)
            for g in range(count)
        ]

    def heads_of(pair):
        return range(pair * shared, (pair + 1) * shared)

    query = [by_sequence([column(query, h) for h in heads_of(pair)]) for pair in range(pairs)]
    key_all = key_all.reshape(all_sequences, ctx * rows, pairs * head)
    value_all = value_all.reshape(all_sequences, ctx * rows, pairs * head)
    key_of = [key_all[:, :, p * head : (p + 1) * head] for p in range(pairs)]
    value_of = [value_all[:, :, p * head : (p + 1) * head] for p in range(pairs)]
    visible = jnp.tile(all_places[None, :] <= own_places[:, None], (shared, 1))[None]
    exponent, slope, exponent_low, row_total, attended = [], [], [], [], []
    for p in range(pairs):
        scores = batched(query[p], key_of[p], 2, 2)
        squashed = jnp.tanh(scores / SOFT_CAP)
        exponent.append(jnp.where(visible, jnp.exp(SOFT_CAP * squashed - EXP_SHIFT), 0.0))
        slope.append(exponent[p] * (1.0 - squashed * squashed))
        row_total.append(jnp.sum(exponent[p], -1, keepdims=True))
        exponent_low.append(exponent[p].astype(LOW))
        attended.append(batched(exponent_low[p], value_of[p], 2, 1) / row_total[p])
    attended_low = jnp.concatenate(
        sum([flat_heads(attended[p].astype(LOW), shared) for p in range(pairs)], []), 1
    )

    def parts(values):
        return values.astype(LOW).reshape(fsdp, tokens, width)

    full_rows = jax.ShapeDtypeStruct((tokens, width), FULL)
    low_rows = jax.ShapeDtypeStruct((tokens, width), LOW)

    def gain_rows(count):
        return jax.ShapeDtypeStruct((count, width), FULL)

    upstream = cotangent.reshape(tokens, width)
    mid_low, branch, mixed = exchange(
        parts(dot(attended_low, w_out, 1, 1)),
        [flat],
        norm_gains,
        branch_mid,
        [full_rows, full_rows],
        fsdp,
        5,
        "branch_exchange",
    )

    late_low, outputs, gain_late, hidden_low, gate_factor, up_factor = late_exchange(
        mid_low, ffn_low, mixed, upstream, norm_gains, 6
    )
    down_grads = lax.psum_scatter(
        dot(
            late_low.reshape(fsdp * tokens, width),
            hidden_low.reshape(fsdp * tokens, ffn_local),
            0,
            0,
        ).astype(LOW),
        "ctx",
        scatter_dimension=0,
        tiled=True,
    )
    branch_low, mixed_grad, gain_middle, pair_part = mid_exchange(
        late_low, mid_low, mixed, branch, upstream, norm_gains, gate_factor, up_factor, ffn_low, 7
    )
    pair_grads = lax.psum_scatter(pair_part, "ctx", scatter_dimension=0, tiled=True)

    branch_low = branch_low.reshape(fsdp * tokens, width)
    attended_grad = dot(branch_low, w_out, 1, 0)
    query_grad, key_part, value_part = [], [], []
    for p in range(pairs):
        grad = by_sequence([column(attended_grad, h) for h in heads_of(p)])
        numerator_low = (grad / row_total[p]).astype(LOW)
        row_term = jnp.sum(grad * attended[p], -1, keepdims=True) / row_total[p]
        pulled = batched(numerator_low, value_of[p], 2, 2)
        score_low = (slope[p] * (pulled - row_term)).astype(LOW)
        query_grad += flat_heads(batched(score_low, key_of[p], 2, 1), shared)
        key_part.append(batched(score_low, query[p], 1, 1).astype(LOW))
        value_part.append(batched(exponent_low[p], numerator_low, 1, 1).astype(LOW))
    spread = (all_sequences, ctx, rows, pairs * head)
    key_grad, value_grad = scatter_pairs(
        jnp.concatenate(key_part, 2).reshape(spread), jnp.concatenate(value_part, 2).reshape(spread)
    )
    key_grad = key_grad.reshape(all_sequences * rows, pairs * head)
    value_grad = value_grad.reshape(all_sequences * rows, pairs * head)
    projected_grad = jnp.concatenate(
        [rotate(grad * scale, cosine, -sine) for grad in query_grad]
        + [rotate(column(key_grad, p), cosine, -sine) for p in range(pairs)]
        + [value_grad],
        1,
    ).astype(LOW)
    momentum = jnp.transpose(ffn_momentum, (1, 0, 2))
    small = -(-3 * (ffn_local // FBLK) // ctx)
    earlier = ffn_gram(down_grads, momentum, 2, ctx * small, [])
    momentum_new_in, momentum_new_out, head_update, head_sum, input_grad, gain_pre = tail(
        dot(normed_low, projected_grad, 0, 0).astype(LOW).reshape(ctx, local_rows, mine * head),
        dot(branch_low, attended_low, 0, 0).astype(LOW).reshape(ctx, local_rows, out_local * head),
        parts(dot(projected_grad, w_in, 1, 1)),
        flat,
        mixed_grad,
        norm_gains,
        momentum_in,
        momentum_out,
    )
    input_grad = input_grad.reshape(inputs.shape)
    outputs = outputs.reshape(inputs.shape)
    gain_parts = jnp.concatenate([gain_pre, gain_middle, gain_late], 0)

    new_ffn, ffn_update, block_gram = ffn_gram(pair_grads, momentum, 0, ctx * small, earlier)
    new_weights_in, new_weights_out, new_ffn_weights, gain_every = newton(
        head_sum,
        block_gram.reshape(ctx, small, FBLK, FBLK),
        gain_parts,
        head_update,
        weights_in,
        weights_out,
        ffn_update,
        ffn_mine,
        LEARN_RATE * (width / head) ** 0.5,
        LEARN_RATE * (width / FBLK) ** 0.5,
        fsdp,
    )
    gain_grad = jnp.sum(gain_every, 0)
    new_gain_first = BETA_ONE * gain_first + (1.0 - BETA_ONE) * gain_grad
    new_gain_second = BETA_TWO * gain_second + (1.0 - BETA_TWO) * gain_grad * gain_grad
    corrected_one = new_gain_first / (1.0 - BETA_ONE**STEP)
    corrected_two = new_gain_second / (1.0 - BETA_TWO**STEP)
    new_norm_gains = norm_gains - GAIN_RATE * corrected_one / (jnp.sqrt(corrected_two) + ADAM_EPS)
    return (
        outputs,
        input_grad,
        new_weights_in,
        new_weights_out,
        jnp.transpose(new_ffn_weights, (1, 0, 2)),
        momentum_new_in,
        momentum_new_out,
        jnp.transpose(new_ffn, (1, 0, 2)),
        new_norm_gains,
        new_gain_first,
        new_gain_second,
    )


def solution(mesh):
    return jax.shard_map(
        local,
        mesh=mesh,
        in_specs=(
            P("fsdp", "ctx", None),
            P("fsdp", "ctx", None),
            P("ctx", "fsdp", None),
            P("ctx", "fsdp", None),
            P("ctx", None, "fsdp"),
            P(),
            P("ctx", "fsdp", None),
            P("ctx", "fsdp", None),
            P("ctx", None, "fsdp"),
            P(),
            P(),
            P(),
        ),
        out_specs=(
            P("fsdp", "ctx", None),
            P("fsdp", "ctx", None),
            P("ctx", "fsdp", None),
            P("ctx", "fsdp", None),
            P("ctx", None, "fsdp"),
            P("ctx", "fsdp", None),
            P("ctx", "fsdp", None),
            P("ctx", None, "fsdp"),
            P(),
            P(),
            P(),
        ),
        check_vma=False,
    )
```
